256 devices in a mesh: tok: 8 (over y, core), lat: 32 (over z, x).
Axes of the slice: x: 4, y: 4, z: 8, core: 2. Of those that a mesh axis runs over, the one named last changes fastest.
Arguments:
- tokens: bfloat16 [32768, 8192], P(('tok', 'lat')), may hold values from -6 to 6
- dec_bias: float32 [8192], replicated, may hold values from -3 to 3
- enc_weight: bfloat16 [4096, 8192], P('lat'), may hold values from -0.0625 to 0.0625
- enc_bias: float32 [4096], P('lat'), may hold values from -3 to 3
- dec_weight: bfloat16 [4096, 8192], P('lat'), may hold values from -0.75 to 0.75
- block_ids: int32 [32768, 1], P(('tok', 'lat')), may hold values from 0 to 63, as said below
- block_home: int32 [64], replicated, may hold values from 0 to 63, as said below
Outputs:
- enc_grad: float32 [4096, 8192], P('lat', 'tok')
- dec_grad: float32 [4096, 8192], P('lat', 'tok')
The draws below stay inside these ranges and needn't reach their ends.
Inputs may be any that keep to these rules, and one draw needn't show every extreme that they name: `block_ids`: each row names 1 different blocks. The 128 names in the rows of one device (aligned groups of 128 rows) name each block at most 6 times; in every token group the blocks of one lat device are each named exactly 6 times by the rows of every device of the group. A permutation: block b has place block_home[b], held by lat device block_home[b] // 2.
All inputs are finite; a program needn't handle non-finite values.
Results may differ from the reference program's by a relative error of at most 0.0024.
Values may be sent and summed in bfloat16 or wider, within the bound.
No kernel may reach another device: no remote copies, remote signals or barrier semaphores. Data moves between devices by JAX's collectives and lax.ppermute only.
A program may use at most 128 MiB of HBM per device.

```python
import jax
import jax.numpy as jnp
from jax import lax

D = 8192
BLK = 64
BLK_DEV = 2
K = 1
TOK_DEV = 128
LAT_BLOCKS = 64
CAP = 6
TOKENS = 32768
LATENTS = 4096
N_TOK = 8


def routing(key):
    source_count = TOKENS // TOK_DEV
    lat_count = LAT_BLOCKS // BLK_DEV
    tok_count = source_count // lat_count
    pair_total = TOK_DEV * K
    hot_total = BLK_DEV * CAP
    cold_slots = LAT_BLOCKS - BLK_DEV
    cold_total = pair_total - hot_total
    base_key = jax.random.fold_in(key, 7)
    home_key, hot_key, source_key = jax.random.split(base_key, 3)
    block_home = jax.random.permutation(home_key, LAT_BLOCKS).astype(jnp.int32)
    owner = jnp.argsort(block_home).astype(jnp.int32)
    hot_devices = jax.random.randint(hot_key, (tok_count,), 0, lat_count).astype(jnp.int32)

    def one_source(source):
        own_key = jax.random.fold_in(source_key, source)
        pick_key, label_key, row_key = jax.random.split(own_key, 3)
        hot_device = hot_devices[source // lat_count]
        hot_places = hot_device * BLK_DEV + jnp.arange(BLK_DEV, dtype=jnp.int32)
        hot_entries = jnp.repeat(hot_places, CAP)
        cold_index = jnp.arange(cold_slots, dtype=jnp.int32)
        cold_places = cold_index + BLK_DEV * (cold_index >= hot_device * BLK_DEV).astype(jnp.int32)
        candidates = jnp.repeat(cold_places, CAP)
        chosen = jax.random.permutation(pick_key, candidates.shape[0])[:cold_total]
        entries = jnp.concatenate([hot_entries, candidates[chosen]])
        relabel = jax.random.permutation(label_key, LAT_BLOCKS).astype(jnp.int32)
        entry_index = jnp.arange(pair_total, dtype=jnp.int32)
        scores = relabel[entries] * pair_total + entry_index
        sorted_places = entries[jnp.argsort(scores)]
        row_order = jax.random.permutation(row_key, TOK_DEV).astype(jnp.int32)
        target_row = row_order[entry_index % TOK_DEV]
        target_col = entry_index // TOK_DEV
        named = jnp.zeros((TOK_DEV, K), jnp.int32).at[target_row, target_col].set(owner[sorted_places])
        return named
    block_ids = jax.vmap(one_source)(jnp.arange(source_count, dtype=jnp.int32))
    return (block_home, block_ids.reshape(TOKENS, K))


def draw_block_ids(key, part):
    return routing(key)[1]


def draw_block_home(key, part):
    return routing(key)[0]


def block_scale(key, dims, pieces, low, top_value):
    level = 1.0
    for position, parts in pieces:
        steps = jax.random.uniform(jax.random.fold_in(jax.random.fold_in(key, 6), position), (parts,), jnp.float32, low / len(pieces), top_value / len(pieces))
        level = level * jnp.repeat(jnp.exp(steps), dims[position] // parts).reshape((-1,) + (1,) * (len(dims) - 1 - position))
    return level


def scatter_about(key, dims, deviation, bound, shards=(), kind=jnp.bfloat16):
    loudness = block_scale(key, dims, shards, -0.22, 0.18) if shards else 1.0
    result = jax.random.normal(key, dims, jnp.float32) * deviation * loudness
    return jnp.minimum(jnp.maximum(result, -bound), bound).astype(kind)


def setup_inputs(seed: int = 0) -> dict:
    seeds = jax.random.split(jax.random.key(seed), 8)
    tokens = scatter_about(seeds[0], (TOKENS, D), 1.0, 6.0, ((0, 256),))
    dec_bias = scatter_about(seeds[1], (D,), 0.5, 3.0, (), jnp.float32)
    enc_weight = scatter_about(seeds[2], (LATENTS, D), D ** -0.5, 0.0625, ((0, 32),))
    enc_bias = scatter_about(seeds[3], (LATENTS,), 0.5, 3.0, ((0, 32),), jnp.float32)
    dec_weight = scatter_about(seeds[4], (LATENTS, D), (K * BLK) ** -0.5, 0.75, ((0, 32),))
    block_ids = draw_block_ids(jax.random.fold_in(seeds[7], 71), 0)
    block_home = draw_block_home(jax.random.fold_in(seeds[7], 71), 0)
    return {"tokens": tokens, "dec_bias": dec_bias, "enc_weight": enc_weight, "enc_bias": enc_bias, "dec_weight": dec_weight, "block_ids": block_ids, "block_home": block_home}


def reference(tokens, dec_bias, enc_weight, enc_bias, dec_weight, block_ids, block_home):
    source_count = TOKENS // TOK_DEV
    lat_count = source_count // N_TOK
    pair_total = TOK_DEV * K
    places = block_home[block_ids].astype(jnp.int32)
    ids_dev = block_ids.reshape(source_count, pair_total)
    order = jnp.arange(pair_total, dtype=jnp.int32)
    earlier = order[None, :] < order[:, None]
    same = ids_dev[:, :, None] == ids_dev[:, None, :]
    ranks = jnp.sum(jnp.logical_and(same, earlier[None]), axis=2).astype(jnp.int32)
    sources = jnp.arange(source_count, dtype=jnp.int32)[:, None]
    positions = (sources * LAT_BLOCKS + places.reshape(source_count, pair_total)) * CAP + ranks
    token_of_pair = (jnp.arange(TOKENS * K, dtype=jnp.int32) // K).astype(jnp.int32)
    table = jnp.full((source_count * LAT_BLOCKS * CAP,), -1, jnp.int32)
    table = table.at[positions.reshape(-1)].set(token_of_pair)
    table = table.reshape(source_count, LAT_BLOCKS, CAP).transpose(1, 0, 2).reshape(LAT_BLOCKS, source_count * CAP)
    centered = (tokens.astype(jnp.float32) - dec_bias).astype(jnp.bfloat16)

    def block_inputs(block_place):
        row_idx = table[block_place]
        valid = row_idx >= 0
        safe_idx = jnp.maximum(row_idx, 0)
        picked = centered[safe_idx]
        picked = jnp.where(valid[:, None], picked, jnp.zeros_like(picked))
        start = (block_place * BLK).astype(jnp.int32)
        w_in = lax.dynamic_slice_in_dim(enc_weight, start, BLK, 0)
        b_in = lax.dynamic_slice_in_dim(enc_bias, start, BLK, 0)
        w_out = lax.dynamic_slice_in_dim(dec_weight, start, BLK, 0)
        preact = jnp.dot(picked, w_in.T, preferred_element_type=jnp.float32) + b_in
        return row_idx, valid, safe_idx, picked, preact, w_out

    def forward(recon, block_place):
        row_idx, valid, safe_idx, picked, preact, w_out = block_inputs(block_place)
        latent = (preact * jax.nn.sigmoid(preact)).astype(jnp.bfloat16)
        decoded = jnp.dot(latent, w_out, preferred_element_type=jnp.float32).astype(jnp.bfloat16)
        target = jnp.where(valid, row_idx, TOKENS)
        recon = recon.at[target].add(decoded.astype(jnp.float32), mode="drop")
        return recon, None

    block_list = jnp.arange(LAT_BLOCKS, dtype=jnp.int32)
    recon, unused = lax.scan(forward, jnp.zeros((TOKENS, D), jnp.float32), block_list)
    recon = recon + dec_bias
    error = ((recon - tokens.astype(jnp.float32)) / 32.0).astype(jnp.bfloat16)

    def backward(block_place):
        row_idx, valid, safe_idx, picked, preact, w_out = block_inputs(block_place)
        squash = jax.nn.sigmoid(preact)
        latent = (preact * squash).astype(jnp.bfloat16)
        err_rows = error[safe_idx]
        err_rows = jnp.where(valid[:, None], err_rows, jnp.zeros_like(err_rows))
        dlatent = jnp.dot(err_rows, w_out.T, preferred_element_type=jnp.float32)
        dpreact = (dlatent * squash * (1.0 + preact * (1.0 - squash))).astype(jnp.bfloat16)
        group_pairs = lat_count * CAP
        enc_part = jnp.einsum("tnl,tnd->tld", dpreact.reshape(N_TOK, group_pairs, BLK).astype(jnp.float32), picked.reshape(N_TOK, group_pairs, D).astype(jnp.float32))
        dec_part = jnp.einsum("tnl,tnd->tld", latent.reshape(N_TOK, group_pairs, BLK).astype(jnp.float32), err_rows.reshape(N_TOK, group_pairs, D).astype(jnp.float32))
        return jnp.sum(enc_part, axis=0), jnp.sum(dec_part, axis=0)

    enc_grad, dec_grad = lax.map(backward, block_list)
    return enc_grad.reshape(LATENTS, D), dec_grad.reshape(LATENTS, D)
```

```python
import jax
import jax.numpy as jnp
from jax import lax
from jax.sharding import PartitionSpec as P


def fill_slots(rows_in, filled, source_row):
    taken = jnp.take(rows_in, source_row, axis=0)
    return jnp.where(filled[:, None], taken, jnp.zeros_like(taken))


def on_device(tokens, dec_bias, enc_weight, enc_bias, dec_weight, block_ids, block_home):
    rows_here = tokens.shape[0]
    width = tokens.shape[1]
    lat_count = lax.axis_size("lat")
    block_total = block_home.shape[0]
    per_device = block_total // lat_count
    block_width = enc_weight.shape[0] // per_device
    picks = block_ids.shape[1]
    capacity = 3 * rows_here * picks // block_total
    slot_total = block_total * capacity
    pair_total = rows_here * picks
    flat_ids = block_ids.reshape(-1)
    matches = flat_ids[:, None] == jnp.arange(block_total, dtype=jnp.int32)[None, :]
    places = jnp.sum(jnp.where(matches, block_home[None, :], 0), axis=1)
    order = jnp.arange(pair_total, dtype=jnp.int32)
    earlier = order[None, :] < order[:, None]
    same = flat_ids[:, None] == flat_ids[None, :]
    ranks = jnp.sum(jnp.logical_and(same, earlier), axis=1)
    positions = places * capacity + ranks
    slot_hits = positions[None, :] == jnp.arange(slot_total, dtype=jnp.int32)[:, None]
    filled = jnp.any(slot_hits, axis=1)
    source_row = jnp.sum(jnp.where(slot_hits, (order // picks)[None, :], 0), axis=1)
    slot_shape = (lat_count, per_device * capacity, width)
    outgoing = fill_slots(tokens, filled, source_row).reshape(slot_shape)
    received = lax.all_to_all(outgoing, "lat", split_axis=0, concat_axis=0, tiled=True)
    named = lax.all_to_all(
        filled.astype(jnp.float32).reshape(lat_count, per_device * capacity),
        "lat",
        split_axis=0,
        concat_axis=0,
        tiled=True,
    )
    used = named.reshape(lat_count, per_device, capacity, 1) > 0.5
    rows_in = received.reshape(lat_count, per_device, capacity, width)
    arrived = jnp.where(
        used, (rows_in.astype(jnp.float32) - dec_bias).astype(jnp.bfloat16), jnp.bfloat16(0)
    )
    enc_blocks = enc_weight.reshape(per_device, block_width, width)
    dec_blocks = dec_weight.reshape(per_device, block_width, width)
    bias_blocks = enc_bias.reshape(per_device, block_width)
    preact = (
        jnp.einsum("sbcd,bld->sbcl", arrived, enc_blocks, preferred_element_type=jnp.float32)
        + bias_blocks[None, :, None, :]
    )
    squash = jax.nn.sigmoid(preact)
    latent = (preact * squash).astype(jnp.bfloat16)
    decoded = jnp.einsum(
        "sbcl,bld->sbcd", latent, dec_blocks, preferred_element_type=jnp.float32
    ).astype(jnp.bfloat16)
    recon = dec_bias + decoded.astype(jnp.float32)
    error_in = jnp.where(
        used, ((recon - rows_in.astype(jnp.float32)) / 32.0).astype(jnp.bfloat16), jnp.bfloat16(0)
    )
    dlatent = jnp.einsum("sbcd,bld->sbcl", error_in, dec_blocks, preferred_element_type=jnp.float32)
    dpreact = (dlatent * squash * (1.0 + preact * (1.0 - squash))).astype(jnp.bfloat16)
    half = per_device * block_width
    enc_part = jnp.einsum(
        "sbcl,sbcd->bld", dpreact, arrived, preferred_element_type=jnp.float32
    ).reshape(half, width)
    dec_part = jnp.einsum(
        "sbcl,sbcd->bld", latent, error_in, preferred_element_type=jnp.float32
    ).reshape(half, width)
    enc_grad, dec_grad = (
        lax.psum_scatter(enc_part, "tok", scatter_dimension=1, tiled=True),
        lax.psum_scatter(dec_part, "tok", scatter_dimension=1, tiled=True),
    )
    return (enc_grad, dec_grad)


def solution(mesh):
    in_specs = (
        P(("tok", "lat"), None),
        P(),
        P("lat", None),
        P("lat"),
        P("lat", None),
        P(("tok", "lat"), None),
        P(),
    )
    out_specs = (P("lat", "tok"), P("lat", "tok"))
    return jax.shard_map(
        on_device, mesh=mesh, in_specs=in_specs, out_specs=out_specs, check_vma=False
    )
```

```python
import functools

import jax
import jax.numpy as jnp
from jax import lax
from jax.experimental import pallas as pl
from jax.experimental.pallas import tpu as pltpu
from jax.sharding import PartitionSpec as P

BF = jnp.bfloat16
F32 = jnp.float32
I32 = jnp.int32

HALVES = 2
SLOTS = 4
DIRECT = 2 * SLOTS
LENT = 7
EXTRA = 128
STRIDE = 16
BIG = pltpu.CompilerParams(vmem_limit_bytes=52 * 2**20)


def mm(a, b):
    return jnp.dot(a, b, preferred_element_type=F32)


def mm_t(a, b):
    return lax.dot_general(a, b, (((1,), (1,)), ((), ())), preferred_element_type=F32)


def iota(shape, axis):
    return lax.broadcasted_iota(I32, shape, axis)


def slot_codes(lat_count, first):
    row = iota((lat_count * HALVES * SLOTS, 1), 0)
    inner = row % (HALVES * SLOTS)
    return (row // (HALVES * SLOTS)) * STRIDE + first + inner % SLOTS, inner // SLOTS


def pick(codes, half, row_codes):
    hit = (row_codes >> 1) == codes
    block = jnp.sum(jnp.where(hit, 1 + (row_codes & 1), 0), axis=1, keepdims=True)
    low = jnp.where(jnp.logical_and(hit, half == 0), 1.0, 0.0).astype(BF)
    high = jnp.where(jnp.logical_and(hit, half == 1), 1.0, 0.0).astype(BF)
    return low, high, block


def before(n):
    return (iota((n, n), 0) < iota((n, n), 1)).astype(F32).astype(BF)


def ranks_of(dest, lat_count):
    g, n = dest.shape
    members = (dest[:, None, :] == iota((g, lat_count, n), 1)).astype(F32)
    counts = mm(members.reshape(g * lat_count, n).astype(BF), before(n)).reshape(g, lat_count, n)
    return members, jnp.sum(members * counts, axis=1)


def first_kernel(lat_count, ids, home, tokens, chunk, lent):
    rows, width = tokens.shape
    part = width // HALVES
    total = home.shape[0]
    hit = iota((total, rows), 0) == ids[...]
    places = jnp.sum(jnp.where(hit, home[...], 0), axis=0, keepdims=True)
    dest, block = places >> 1, places & 1
    unused, rank = ranks_of(dest, lat_count)
    rank = rank.astype(I32)
    codes, half = slot_codes(lat_count, 0)
    low, high, meta = pick(codes, half, (dest * STRIDE + rank) * 2 + block)
    both = jnp.concatenate([low, high], axis=1)
    step = 1024
    for i in range(part // step):
        a = tokens[:, i * step : (i + 1) * step]
        b = tokens[:, part + i * step : part + (i + 1) * step]
        chunk[:, i * step : (i + 1) * step] = mm(both, jnp.concatenate([a, b], axis=0)).astype(BF)
    chunk[:, part:] = jnp.broadcast_to(meta.astype(F32), (meta.shape[0], EXTRA)).astype(BF)
    over = (rank >= DIRECT).astype(F32)
    order = mm(jnp.broadcast_to(over, (8, rows)).astype(BF), before(rows))[:1]
    list_row = iota((LENT + 1, rows), 0)
    take = jnp.logical_and(order.astype(I32) == list_row, over > 0.5)
    take = jnp.logical_and(take, list_row < LENT)
    take = jnp.where(take, 1.0, 0.0).astype(BF)
    for i in range(width // step):
        got = mm(take, tokens[:, i * step : (i + 1) * step])
        if i == 0:
            head = jnp.where(list_row == LENT, places.astype(F32), got[:, :rows])
            got = jnp.concatenate([head, got[:, rows:]], axis=1)
        lent[:, i * step : (i + 1) * step] = got.astype(BF)


def second_kernel(lat_count, group, tokens, loans, chunk, left):
    rows, width = tokens.shape
    part = width // HALVES
    groups = loans.shape[0] // (LENT + 1)
    me = group[0]
    heads = loans[:, :rows].astype(F32).reshape(groups, LENT + 1, rows)
    places = heads[:, LENT, :].astype(I32)
    dest, block = places >> 1, places & 1
    members, rank_f = ranks_of(dest, lat_count)
    rank = rank_f.astype(I32)
    over = rank >= DIRECT
    order = mm(over.astype(F32).astype(BF), before(rows)).astype(I32)
    listed = jnp.logical_and(over, order < LENT)
    count = jnp.sum(members, axis=2, keepdims=True)
    asked = jnp.sum(members * listed.astype(F32)[:, None, :], axis=2, keepdims=True)
    used = jnp.maximum(count, float(SLOTS))
    free = jnp.maximum(DIRECT - used, 0.0)
    my_group = iota((groups, 1, 1), 0)
    asked_before = []
    running = jnp.zeros((1, lat_count, 1), F32)
    free_total = jnp.zeros((1, lat_count, 1), F32)
    free_before = jnp.zeros((1, lat_count, 1), F32)
    for t in range(groups):
        asked_before.append(running)
        running = running + asked[t : t + 1]
        free_before = free_before + jnp.where(me > t, free[t : t + 1], 0.0)
        free_total = free_total + free[t : t + 1]
    mine = (my_group == me).astype(F32)
    my_free = jnp.sum(free * mine, axis=0, keepdims=True)
    my_used = jnp.sum(used * mine, axis=0, keepdims=True)

    def look(values):
        return jnp.sum(members * values, axis=1).astype(I32)

    place_in_pool = look(jnp.concatenate(asked_before, axis=0)) + rank - DIRECT
    placed = jnp.logical_and(listed, place_in_pool < look(free_total))
    at = place_in_pool - look(free_before)
    here = jnp.logical_and(placed, jnp.logical_and(at >= 0, at < look(my_free)))
    slot = look(my_used) + at
    lent_code = jnp.where(here, (dest * STRIDE + slot) * 2 + block, -1)
    list_row = iota((LENT + 1, rows), 0)
    columns = []
    for t in range(groups):
        chosen = jnp.logical_and(order[t : t + 1] == list_row, listed[t : t + 1])
        value = jnp.sum(jnp.where(chosen, lent_code[t : t + 1] + 1, 0), axis=1, keepdims=True) - 1
        columns.append(value)
    column = jnp.concatenate(columns, axis=0)
    size = groups * (LENT + 1)
    lent_row = jnp.sum(
        jnp.where(iota((size, size), 0) == iota((size, size), 1), column, 0), axis=0, keepdims=True
    )
    mine2 = (iota((groups, 1), 0) == me).astype(I32)
    own_code = jnp.sum(((dest * STRIDE + rank) * 2 + block) * mine2, axis=0, keepdims=True)
    missing = jnp.logical_and(over, jnp.logical_not(placed)).astype(I32)
    own_missing = jnp.sum(missing * mine2, axis=0, keepdims=True)
    left[...] = jnp.broadcast_to(jnp.where(own_missing > 0, own_code, -1), left.shape)
    flag = jnp.max(jnp.max(missing.astype(F32), axis=1, keepdims=True), axis=0, keepdims=True)
    codes, half = slot_codes(lat_count, SLOTS)
    low, high, meta = pick(codes, half, own_code)
    low2, high2, meta2 = pick(codes, half, lent_row)
    both = jnp.concatenate([low, high], axis=1)
    both2 = jnp.concatenate([low2, high2], axis=1)
    step = 1024
    for i in range(part // step):
        lo, hi = slice(i * step, (i + 1) * step), slice(part + i * step, part + (i + 1) * step)
        own = jnp.concatenate([tokens[:, lo], tokens[:, hi]], axis=0)
        other = jnp.concatenate([loans[:, lo], loans[:, hi]], axis=0)
        chunk[:, lo] = (mm(both, own) + mm(both2, other)).astype(BF)
    code = (meta + meta2).astype(F32) + 4.0 * flag
    chunk[:, part:] = jnp.broadcast_to(code, (code.shape[0], EXTRA)).astype(BF)


def gradient_body(chunk, enc, dec, bias, dec_bias, cent, err, acc, store):
    rows, padded = chunk.shape
    part = padded - EXTRA
    latents = enc.shape[0]
    step = 1024
    steps = part // step
    group = HALVES * SLOTS
    half = iota((rows, 1), 0) % group // SLOTS
    high_row = iota((group, 1), 0) // SLOTS == 1

    def pair(i):
        lo, hi = slice(i * step, (i + 1) * step), slice(part + i * step, part + (i + 1) * step)
        return lo, hi

    def offset(i):
        lo, hi = pair(i)
        return jnp.where(high_row, dec_bias[:, hi], dec_bias[:, lo])[None]

    def joined(total):
        own = jnp.where(half == 0, total[:, :latents], total[:, latents:])
        down = pltpu.roll(own, SLOTS, 0)
        up = pltpu.roll(own, rows - SLOTS, 0)
        return own + jnp.where(half == 0, up, down)

    def spread(values):
        zero = jnp.zeros_like(values)
        return jnp.concatenate(
            [jnp.where(half == 0, values, zero), jnp.where(half == 1, values, zero)], axis=1
        )

    for i in range(steps):
        lo, hi = pair(i)
        x = chunk[:, lo].astype(F32).reshape(rows // group, group, step)
        c = (x - offset(i)).reshape(rows, step).astype(BF)
        cent[:, lo] = c
        w = jnp.concatenate([enc[:, lo], enc[:, hi]], axis=0)
        if i == 0:
            acc[...] = mm_t(c, w)
        else:
            acc[...] += mm_t(c, w)
    code = chunk[:, part:].astype(F32)
    code = jnp.where(code >= 4.0, code - 4.0, code)
    second = iota((1, latents), 1) >= latents // 2
    valid = code == jnp.where(second, 2.0, 1.0)
    pre = joined(acc[...]) + bias[...]
    gate = 1.0 / (1.0 + jnp.exp(-pre))
    latent = spread(jnp.where(valid, pre * gate, 0.0))
    latent_b = latent.astype(BF)
    for i in range(steps):
        lo, hi = pair(i)
        w = jnp.concatenate([dec[:, lo], dec[:, hi]], axis=0)
        d = mm(latent_b, w).astype(BF).astype(F32).reshape(rows // group, group, step)
        x = chunk[:, lo].astype(F32).reshape(rows // group, group, step)
        e = ((offset(i) + d - x) * (1.0 / 32.0)).reshape(rows, step).astype(BF)
        err[:, lo] = e
        if i == 0:
            acc[...] = mm_t(e, w)
        else:
            acc[...] += mm_t(e, w)
    dlatent = joined(acc[...])
    dpre = spread(jnp.where(valid, dlatent * gate * (1.0 + pre * (1.0 - gate)), 0.0))
    dpre_t = dpre.T.astype(BF)
    latent_t = latent.T.astype(BF)
    for i in range(steps):
        lo, hi = pair(i)
        store(i, 0, mm(dpre_t, cent[:, lo]))
        store(i, 1, mm(latent_t, err[:, lo]))


def part_kernel(chunk, enc, dec, bias, dec_bias, parts, cent, err, acc):
    latents = enc.shape[0]
    steps = parts.shape[0] // HALVES

    def store(i, grad, value):
        rows = slice(grad * latents, (grad + 1) * latents)
        parts[i, rows] = value[:latents]
        parts[steps + i, rows] = value[latents:]

    gradient_body(chunk, enc, dec, bias, dec_bias, cent, err, acc, store)


def last_kernel(
    core, chunk, enc, dec, bias, dec_bias, parts, mine, other, flags, cent, err, acc
):
    latents = enc.shape[0]
    steps = parts.shape[0] // HALVES

    def store(i, grad, value):
        rows = slice(grad * latents, (grad + 1) * latents)
        for h in range(HALVES):
            k = h * steps + i
            total = value[h * latents : (h + 1) * latents] + parts[k, rows]

            @pl.when(core[0] == k % 2)
            def _():
                mine[k // 2, rows] = total

            @pl.when(core[0] != k % 2)
            def _():
                other[k // 2, rows] = total.astype(BF)

    top = jnp.max(chunk[:, chunk.shape[1] - EXTRA :].astype(F32), axis=0, keepdims=True)
    flags[...] = jnp.broadcast_to(top, flags.shape)
    gradient_body(chunk, enc, dec, bias, dec_bias, cent, err, acc, store)


def vmem():
    return pl.BlockSpec(memory_space=pltpu.VMEM)


def smem():
    return pl.BlockSpec(memory_space=pltpu.SMEM)


def on_device(tokens, dec_bias, enc_weight, enc_bias, dec_weight, block_ids, block_home):
    rows, width = tokens.shape
    lat_count = lax.axis_size("lat")
    groups = lax.axis_size("tok")
    part = width // HALVES
    slot_rows = lat_count * HALVES * SLOTS
    latents = enc_weight.shape[0]
    out_width = width // groups
    me = lax.axis_index("tok").astype(I32)
    chunk_shape = jax.ShapeDtypeStruct((slot_rows, part + EXTRA), BF)
    matmul_cost = pl.CostEstimate(
        flops=5 * 2 * slot_rows * 2 * latents * part, bytes_accessed=16 * 2**20, transcendentals=0
    )
    move_cost = pl.CostEstimate(
        flops=2 * slot_rows * 2 * rows * part, bytes_accessed=5 * 2**20, transcendentals=0
    )

    chunk1, lent = pl.pallas_call(
        functools.partial(first_kernel, lat_count),
        out_shape=[chunk_shape, jax.ShapeDtypeStruct((LENT + 1, width), BF)],
        in_specs=[vmem()] * 3,
        out_specs=[vmem()] * 2,
        compiler_params=BIG,
        cost_estimate=move_cost,
        name="first_slots",
    )(block_ids.reshape(1, rows), block_home.reshape(-1, 1), tokens)

    def exchange(chunk):
        shaped = chunk.reshape(lat_count, HALVES * SLOTS, part + EXTRA)
        got = lax.all_to_all(shaped, "lat", split_axis=0, concat_axis=0, tiled=True)
        return got.reshape(slot_rows, part + EXTRA)

    loans = lax.all_gather(lent, "tok", tiled=True)
    got1 = exchange(chunk1)
    chunk2, left = pl.pallas_call(
        functools.partial(second_kernel, lat_count),
        out_shape=[chunk_shape, jax.ShapeDtypeStruct((8, rows), I32)],
        in_specs=[smem(), vmem(), vmem()],
        out_specs=[vmem()] * 2,
        compiler_params=BIG,
        cost_estimate=move_cost,
        name="second_slots",
    )(me.reshape(1), tokens, loans)
    got2 = exchange(chunk2)

    bias_row = enc_bias.reshape(1, latents)
    offset_row = dec_bias.reshape(1, width)
    work = [
        pltpu.VMEM((slot_rows, part), BF),
        pltpu.VMEM((slot_rows, part), BF),
        pltpu.VMEM((slot_rows, HALVES * latents), F32),
    ]
    part_call = pl.pallas_call(
        part_kernel,
        out_shape=jax.ShapeDtypeStruct((groups, 2 * latents, out_width), F32),
        in_specs=[vmem()] * 5,
        out_specs=vmem(),
        scratch_shapes=work,
        compiler_params=BIG,
        cost_estimate=matmul_cost,
        name="chunk_gradients",
    )
    parts = part_call(got1, enc_weight, dec_weight, bias_row, offset_row)
    core = me % 2
    half_groups = groups // 2
    mine, other, flags = pl.pallas_call(
        last_kernel,
        out_shape=[
            jax.ShapeDtypeStruct((half_groups, 2 * latents, out_width), F32),
            jax.ShapeDtypeStruct((half_groups, 2 * latents, out_width), BF),
            jax.ShapeDtypeStruct((8, EXTRA), F32),
        ],
        in_specs=[smem()] + [vmem()] * 6,
        out_specs=[vmem()] * 3,
        scratch_shapes=work,
        compiler_params=BIG,
        cost_estimate=matmul_cost,
        name="last_gradients",
    )(core.reshape(1), got2, enc_weight, dec_weight, bias_row, offset_row, parts)

    def finish(mine, other):
        swapped = lax.ppermute(other, "tok", [(i, i ^ 1) for i in range(groups)])
        summed = (mine + swapped.astype(F32)).astype(BF)
        same_core = [[2 * i + c for i in range(half_groups)] for c in range(2)]
        terms = lax.all_to_all(
            summed, "tok", split_axis=0, concat_axis=0, tiled=True, axis_index_groups=same_core
        )
        total = jnp.sum(terms.astype(F32), axis=0)
        return total[:latents], total[latents:]

    def with_rest(mine, other):
        codes, half = slot_codes(lat_count, DIRECT)
        low, high, meta = pick(codes, half, left[:1])
        data = mm(low, tokens[:, :part]) + mm(high, tokens[:, part:])
        extra = jnp.broadcast_to(meta.astype(F32), (slot_rows, EXTRA))
        chunk3 = jnp.concatenate([data, extra], axis=1).astype(BF)
        rest = part_call(exchange(chunk3), enc_weight, dec_weight, bias_row, offset_row)
        rest = rest.reshape(half_groups, 2, 2 * latents, out_width)
        mine = mine + lax.dynamic_index_in_dim(rest, core, 1, keepdims=False)
        more = lax.dynamic_index_in_dim(rest, 1 - core, 1, keepdims=False)
        return finish(mine, (other.astype(F32) + more).astype(BF))

    return lax.cond(flags[0, 0] >= 4.0, with_rest, finish, mine, other)


def solution(mesh):
    in_specs = (
        P(("tok", "lat"), None),
        P(),
        P("lat", None),
        P("lat"),
        P("lat", None),
        P(("tok", "lat"), None),
        P(),
    )
    out_specs = (P("lat", "tok"), P("lat", "tok"))
    return jax.shard_map(
        on_device, mesh=mesh, in_specs=in_specs, out_specs=out_specs, check_vma=False
    )
```

```python
import functools

import jax
import jax.numpy as jnp
from jax import lax
from jax.experimental import pallas as pl
from jax.experimental.pallas import tpu as pltpu
from jax.sharding import PartitionSpec as P

BF = jnp.bfloat16
F32 = jnp.float32
I32 = jnp.int32

HALVES = 2
SLOTS = 4
DIRECT = 2 * SLOTS
LENT = 6
PIECES = 8
EXTRA = 128
STRIDE = 16


def room(mib):
    return pltpu.CompilerParams(vmem_limit_bytes=mib * 2**20)


def mm(a, b):
    return jnp.dot(a, b, preferred_element_type=F32)


def mm_t(a, b):
    return lax.dot_general(a, b, (((1,), (1,)), ((), ())), preferred_element_type=F32)


def iota(shape, axis):
    return lax.broadcasted_iota(I32, shape, axis)


def slot_codes(lat_count, first):
    row = iota((lat_count * HALVES * SLOTS, 1), 0)
    inner = row % (HALVES * SLOTS)
    return (row // (HALVES * SLOTS)) * STRIDE + first + inner % SLOTS, inner // SLOTS


def pick(codes, half, row_codes):
    hit = (row_codes >> 1) == codes
    block = jnp.sum(jnp.where(hit, 1 + (row_codes & 1), 0), axis=1, keepdims=True)
    low = jnp.where(jnp.logical_and(hit, half == 0), 1.0, 0.0).astype(BF)
    high = jnp.where(jnp.logical_and(hit, half == 1), 1.0, 0.0).astype(BF)
    return low, high, block


def before(n):
    return (iota((n, n), 0) < iota((n, n), 1)).astype(F32).astype(BF)


def ranks_of(dest, lat_count):
    g, n = dest.shape
    members = (dest[:, None, :] == iota((g, lat_count, n), 1)).astype(F32)
    counts = mm(members.reshape(g * lat_count, n).astype(BF), before(n)).reshape(g, lat_count, n)
    return members, jnp.sum(members * counts, axis=1)


def first_kernel(lat_count, ids, home, tokens, chunk, lent):
    rows, width = tokens.shape
    part = width // HALVES
    total = home.shape[1]
    hit = (iota((total, rows), 0) == ids[...]).astype(F32).astype(BF)
    table = jnp.broadcast_to(home[...], (8, total)).astype(F32).astype(BF)
    places = mm(table, hit)[:1].astype(I32)
    dest, block = places >> 1, places & 1
    unused, rank = ranks_of(dest, lat_count)
    rank = rank.astype(I32)
    codes, half = slot_codes(lat_count, 0)
    low, high, meta = pick(codes, half, (dest * STRIDE + rank) * 2 + block)
    both = jnp.concatenate([low, high], axis=1)
    step = 1024
    for i in range(part // step):
        a = tokens[:, i * step : (i + 1) * step]
        b = tokens[:, part + i * step : part + (i + 1) * step]
        chunk[:, i * step : (i + 1) * step] = mm(both, jnp.concatenate([a, b], axis=0)).astype(BF)
    chunk[:, part:] = jnp.broadcast_to(meta.astype(F32), (meta.shape[0], EXTRA)).astype(BF)
    over = (rank >= DIRECT).astype(F32)
    order = mm(jnp.broadcast_to(over, (8, rows)).astype(BF), before(rows))[:1]
    lines = (LENT + 1) * PIECES
    line = iota((lines, rows), 0)
    take = jnp.logical_and(order.astype(I32) == line // PIECES, over > 0.5)
    take = jnp.where(jnp.logical_and(take, line < LENT * PIECES), 1.0, 0.0)
    piece = iota((lines, 1), 0) % PIECES
    got = jnp.zeros((lines, width // PIECES), F32)
    for i in range(PIECES):
        chosen = jnp.where(piece == i, take, 0.0).astype(BF)
        got = got + mm(chosen, tokens[:, i * step : (i + 1) * step])
    head = jnp.where(line == LENT * PIECES, places.astype(F32), got[:, :rows])
    lent[...] = jnp.concatenate([head, got[:, rows:]], axis=1).astype(BF)


def second_kernel(lat_count, group, tokens, loans, chunk, left):
    rows, width = tokens.shape
    part = width // HALVES
    lines = (LENT + 1) * PIECES
    groups = loans.shape[0] // lines
    me = group[0]
    heads = loans[:, :rows].astype(F32).reshape(groups, lines, rows)
    places = heads[:, LENT * PIECES, :].astype(I32)
    dest, block = places >> 1, places & 1
    members, rank_f = ranks_of(dest, lat_count)
    rank = rank_f.astype(I32)
    over = rank >= DIRECT
    order = mm(over.astype(F32).astype(BF), before(rows)).astype(I32)
    listed = jnp.logical_and(over, order < LENT)
    count = jnp.sum(members, axis=2, keepdims=True)
    asked = jnp.sum(members * listed.astype(F32)[:, None, :], axis=2, keepdims=True)
    used = jnp.maximum(count, float(SLOTS))
    free = jnp.maximum(DIRECT - used, 0.0)
    my_group = iota((groups, 1, 1), 0)
    asked_before = []
    running = jnp.zeros((1, lat_count, 1), F32)
    free_total = jnp.zeros((1, lat_count, 1), F32)
    free_before = jnp.zeros((1, lat_count, 1), F32)
    for t in range(groups):
        asked_before.append(running)
        running = running + asked[t : t + 1]
        free_before = free_before + jnp.where(me > t, free[t : t + 1], 0.0)
        free_total = free_total + free[t : t + 1]
    mine = (my_group == me).astype(F32)
    my_free = jnp.sum(free * mine, axis=0, keepdims=True)
    my_used = jnp.sum(used * mine, axis=0, keepdims=True)

    def look(values):
        return jnp.sum(members * values, axis=1).astype(I32)

    place_in_pool = look(jnp.concatenate(asked_before, axis=0)) + rank - DIRECT
    placed = jnp.logical_and(listed, place_in_pool < look(free_total))
    at = place_in_pool - look(free_before)
    here = jnp.logical_and(placed, jnp.logical_and(at >= 0, at < look(my_free)))
    slot = look(my_used) + at
    lent_code = jnp.where(here, (dest * STRIDE + slot) * 2 + block, -1)
    list_row = iota((lines, rows), 0) // PIECES
    columns = []
    for t in range(groups):
        chosen = jnp.logical_and(order[t : t + 1] == list_row, listed[t : t + 1])
        value = jnp.sum(jnp.where(chosen, lent_code[t : t + 1] + 1, 0), axis=1, keepdims=True) - 1
        columns.append(value)
    column = jnp.concatenate(columns, axis=0)
    size = groups * lines
    lent_row = jnp.sum(
        jnp.where(iota((size, size), 0) == iota((size, size), 1), column, 0), axis=0, keepdims=True
    )
    mine2 = (iota((groups, 1), 0) == me).astype(I32)
    own_code = jnp.sum(((dest * STRIDE + rank) * 2 + block) * mine2, axis=0, keepdims=True)
    missing = jnp.logical_and(over, jnp.logical_not(placed)).astype(I32)
    own_missing = jnp.sum(missing * mine2, axis=0, keepdims=True)
    left[...] = jnp.broadcast_to(jnp.where(own_missing > 0, own_code, -1), left.shape)
    flag = jnp.max(jnp.max(missing.astype(F32), axis=1, keepdims=True), axis=0, keepdims=True)
    codes, half = slot_codes(lat_count, SLOTS)
    low, high, meta = pick(codes, half, own_code)
    low2, high2, meta2 = pick(codes, half, lent_row)
    meta2 = meta2 // PIECES
    both = jnp.concatenate([low, high], axis=1)
    low2, high2 = low2.astype(F32), high2.astype(F32)
    piece = iota((1, size), 1) % PIECES
    step = 1024
    for i in range(part // step):
        lo, hi = slice(i * step, (i + 1) * step), slice(part + i * step, part + (i + 1) * step)
        own = jnp.concatenate([tokens[:, lo], tokens[:, hi]], axis=0)
        both2 = jnp.where(piece == i, low2, 0.0) + jnp.where(piece == i + part // step, high2, 0.0)
        chunk[:, lo] = (mm(both, own) + mm(both2.astype(BF), loans[...])).astype(BF)
    code = (meta + meta2).astype(F32) + 4.0 * flag
    chunk[:, part:] = jnp.broadcast_to(code, (code.shape[0], EXTRA)).astype(BF)


def gradient_body(chunk, enc, dec, bias, dec_bias, cent, err, acc, store):
    rows, padded = chunk.shape
    part = padded - EXTRA
    latents = enc.shape[0]
    step = 1024
    steps = part // step
    group = HALVES * SLOTS
    half = iota((rows, 1), 0) % group // SLOTS
    high_row = iota((group, 1), 0) // SLOTS == 1

    def pair(i):
        lo, hi = slice(i * step, (i + 1) * step), slice(part + i * step, part + (i + 1) * step)
        return lo, hi

    def offset(i):
        lo, hi = pair(i)
        return jnp.where(high_row, dec_bias[:, hi], dec_bias[:, lo])[None]

    def joined(total):
        own = jnp.where(half == 0, total[:, :latents], total[:, latents:])
        down = pltpu.roll(own, SLOTS, 0)
        up = pltpu.roll(own, rows - SLOTS, 0)
        return own + jnp.where(half == 0, up, down)

    def spread(values):
        zero = jnp.zeros_like(values)
        return jnp.concatenate(
            [jnp.where(half == 0, values, zero), jnp.where(half == 1, values, zero)], axis=1
        )

    for i in range(steps):
        lo, hi = pair(i)
        x = chunk[:, lo].astype(F32).reshape(rows // group, group, step)
        c = (x - offset(i)).reshape(rows, step).astype(BF)
        cent[:, lo] = c
        w = jnp.concatenate([enc[:, lo], enc[:, hi]], axis=0)
        if i == 0:
            acc[...] = mm_t(c, w)
        else:
            acc[...] += mm_t(c, w)
    code = chunk[:, part:].astype(F32)
    code = jnp.where(code >= 4.0, code - 4.0, code)
    second = iota((1, latents), 1) >= latents // 2
    valid = code == jnp.where(second, 2.0, 1.0)
    pre = joined(acc[...]) + bias[...]
    gate = 1.0 / (1.0 + jnp.exp(-pre))
    latent = spread(jnp.where(valid, pre * gate, 0.0))
    latent_b = latent.astype(BF)
    for i in range(steps):
        lo, hi = pair(i)
        w = jnp.concatenate([dec[:, lo], dec[:, hi]], axis=0)
        d = mm(latent_b, w).astype(BF).astype(F32).reshape(rows // group, group, step)
        x = chunk[:, lo].astype(F32).reshape(rows // group, group, step)
        e = ((offset(i) + d - x) * (1.0 / 32.0)).reshape(rows, step).astype(BF)
        err[:, lo] = e
        if i == 0:
            acc[...] = mm_t(e, w)
        else:
            acc[...] += mm_t(e, w)
    dlatent = joined(acc[...])
    dpre = spread(jnp.where(valid, dlatent * gate * (1.0 + pre * (1.0 - gate)), 0.0))
    dpre_t = dpre.T.astype(BF)
    latent_t = latent.T.astype(BF)
    for i in range(steps):
        lo, hi = pair(i)
        store(i, 0, mm(dpre_t, cent[:, lo]))
        store(i, 1, mm(latent_t, err[:, lo]))


def part_kernel(chunk, enc, dec, bias, dec_bias, parts, cent, err, acc):
    latents = enc.shape[0]
    steps = parts.shape[0] // HALVES

    def store(i, grad, value):
        rows = slice(grad * latents, (grad + 1) * latents)
        parts[i, rows] = value[:latents]
        parts[steps + i, rows] = value[latents:]

    gradient_body(chunk, enc, dec, bias, dec_bias, cent, err, acc, store)


def last_kernel(
    core, chunk, enc, dec, bias, dec_bias, parts, mine, other, flags, cent, err, acc
):
    latents = enc.shape[0]
    steps = parts.shape[0] // HALVES

    def store(i, grad, value):
        rows = slice(grad * latents, (grad + 1) * latents)
        for h in range(HALVES):
            k = h * steps + i
            total = value[h * latents : (h + 1) * latents] + parts[k, rows]

            @pl.when(core[0] == k % 2)
            def _():
                mine[k // 2, rows] = total

            @pl.when(core[0] != k % 2)
            def _():
                other[k // 2, rows] = total.astype(BF)

    top = jnp.max(chunk[:, chunk.shape[1] - EXTRA :].astype(F32), axis=0, keepdims=True)
    flags[...] = jnp.broadcast_to(top, flags.shape)
    gradient_body(chunk, enc, dec, bias, dec_bias, cent, err, acc, store)


def vmem():
    return pl.BlockSpec(memory_space=pltpu.VMEM)


def smem():
    return pl.BlockSpec(memory_space=pltpu.SMEM)


def on_device(tokens, dec_bias, enc_weight, enc_bias, dec_weight, block_ids, block_home):
    rows, width = tokens.shape
    lat_count = lax.axis_size("lat")
    groups = lax.axis_size("tok")
    part = width // HALVES
    slot_rows = lat_count * HALVES * SLOTS
    latents = enc_weight.shape[0]
    out_width = width // groups
    me = lax.axis_index("tok").astype(I32)
    chunk_shape = jax.ShapeDtypeStruct((slot_rows, part + EXTRA), BF)
    matmul_cost = pl.CostEstimate(
        flops=5 * 2 * slot_rows * 2 * latents * part, bytes_accessed=16 * 2**20, transcendentals=0
    )
    move_cost = pl.CostEstimate(
        flops=2 * slot_rows * 2 * rows * part, bytes_accessed=5 * 2**20, transcendentals=0
    )

    chunk1, lent = pl.pallas_call(
        functools.partial(first_kernel, lat_count),
        out_shape=[chunk_shape, jax.ShapeDtypeStruct(((LENT + 1) * PIECES, width // PIECES), BF)],
        in_specs=[vmem()] * 3,
        out_specs=[vmem()] * 2,
        compiler_params=room(16),
        cost_estimate=move_cost,
        name="first_slots",
    )(block_ids.reshape(1, rows), block_home.reshape(1, -1), tokens)

    def exchange(chunk):
        shaped = chunk.reshape(lat_count, HALVES * SLOTS, part + EXTRA)
        got = lax.all_to_all(shaped, "lat", split_axis=0, concat_axis=0, tiled=True)
        return got.reshape(slot_rows, part + EXTRA)

    loans = lax.all_gather(lent, "tok", tiled=True)
    got1 = exchange(chunk1)
    chunk2, left = pl.pallas_call(
        functools.partial(second_kernel, lat_count),
        out_shape=[chunk_shape, jax.ShapeDtypeStruct((8, rows), I32)],
        in_specs=[smem(), vmem(), vmem()],
        out_specs=[vmem()] * 2,
        compiler_params=room(24),
        cost_estimate=move_cost,
        name="second_slots",
    )(me.reshape(1), tokens, loans)
    got2 = exchange(chunk2)

    bias_row = enc_bias.reshape(1, latents)
    offset_row = dec_bias.reshape(1, width)
    work = [
        pltpu.VMEM((slot_rows, part), BF),
        pltpu.VMEM((slot_rows, part), BF),
        pltpu.VMEM((slot_rows, HALVES * latents), F32),
    ]
    part_call = pl.pallas_call(
        part_kernel,
        out_shape=jax.ShapeDtypeStruct((groups, 2 * latents, out_width), F32),
        in_specs=[vmem()] * 5,
        out_specs=vmem(),
        scratch_shapes=work,
        compiler_params=room(26),
        cost_estimate=matmul_cost,
        name="chunk_gradients",
    )
    parts = part_call(got1, enc_weight, dec_weight, bias_row, offset_row)
    core = me % 2
    half_groups = groups // 2
    mine, other, flags = pl.pallas_call(
        last_kernel,
        out_shape=[
            jax.ShapeDtypeStruct((half_groups, 2 * latents, out_width), F32),
            jax.ShapeDtypeStruct((half_groups, 2 * latents, out_width), BF),
            jax.ShapeDtypeStruct((8, EXTRA), F32),
        ],
        in_specs=[smem()] + [vmem()] * 6,
        out_specs=[vmem()] * 3,
        scratch_shapes=work,
        compiler_params=room(32),
        cost_estimate=matmul_cost,
        name="last_gradients",
    )(core.reshape(1), got2, enc_weight, dec_weight, bias_row, offset_row, parts)

    def finish(mine, other):
        swapped = lax.ppermute(other, "tok", [(i, i ^ 1) for i in range(groups)])
        summed = (mine + swapped.astype(F32)).astype(BF)
        same_core = [[2 * i + c for i in range(half_groups)] for c in range(2)]
        terms = lax.all_to_all(
            summed, "tok", split_axis=0, concat_axis=0, tiled=True, axis_index_groups=same_core
        )
        total = jnp.sum(terms.astype(F32), axis=0)
        return total[:latents], total[latents:]

    def rest(carry):
        mine, other, unused = carry
        codes, half = slot_codes(lat_count, DIRECT)
        low, high, meta = pick(codes, half, left[:1])
        data = mm(low, tokens[:, :part]) + mm(high, tokens[:, part:])
        extra = jnp.broadcast_to(meta.astype(F32), (slot_rows, EXTRA))
        chunk3 = jnp.concatenate([data, extra], axis=1).astype(BF)
        more = part_call(exchange(chunk3), enc_weight, dec_weight, bias_row, offset_row)
        more = more.reshape(half_groups, 2, 2 * latents, out_width)
        mine = mine + lax.dynamic_index_in_dim(more, core, 1, keepdims=False)
        more = lax.dynamic_index_in_dim(more, 1 - core, 1, keepdims=False)
        return mine, (other.astype(F32) + more).astype(BF), jnp.zeros((), F32)

    mine, other, unused = lax.while_loop(
        lambda carry: carry[2] >= 4.0, rest, (mine, other, flags[0, 0])
    )
    return finish(mine, other)


def solution(mesh):
    in_specs = (
        P(("tok", "lat"), None),
        P(),
        P("lat", None),
        P("lat"),
        P("lat", None),
        P(("tok", "lat"), None),
        P(),
    )
    out_specs = (P("lat", "tok"), P("lat", "tok"))
    return jax.shard_map(
        on_device, mesh=mesh, in_specs=in_specs, out_specs=out_specs, check_vma=False
    )
```

```python
import functools

import jax
import jax.numpy as jnp
from jax import lax
from jax.experimental import pallas as pl
from jax.experimental.pallas import tpu as pltpu
from jax.sharding import PartitionSpec as P

BF = jnp.bfloat16
F32 = jnp.float32
I32 = jnp.int32

HALVES = 2
SLOTS = 4
DIRECT = 2 * SLOTS
LENT = 7
PIECES = 8
EXTRA = 128
STRIDE = 16


def room(mib):
    return pltpu.CompilerParams(vmem_limit_bytes=mib * 2**20)


def mm(a, b):
    return jnp.dot(a, b, preferred_element_type=F32)


def mm_t(a, b):
    return lax.dot_general(a, b, (((1,), (1,)), ((), ())), preferred_element_type=F32)


def iota(shape, axis):
    return lax.broadcasted_iota(I32, shape, axis)


def slot_codes(lat_count, first):
    row = iota((lat_count * HALVES * SLOTS, 1), 0)
    inner = row % (HALVES * SLOTS)
    return (row // (HALVES * SLOTS)) * STRIDE + first + inner % SLOTS, inner // SLOTS


def pick(codes, half, row_codes):
    hit = (row_codes >> 1) == codes
    block = jnp.sum(jnp.where(hit, 1 + (row_codes & 1), 0), axis=1, keepdims=True)
    low = jnp.where(jnp.logical_and(hit, half == 0), 1.0, 0.0).astype(BF)
    high = jnp.where(jnp.logical_and(hit, half == 1), 1.0, 0.0).astype(BF)
    return low, high, block


def before(n):
    return (iota((n, n), 0) < iota((n, n), 1)).astype(F32).astype(BF)


def ranks_of(dest, lat_count):
    g, n = dest.shape
    members = (dest[:, None, :] == iota((g, lat_count, n), 1)).astype(F32)
    counts = mm(members.reshape(g * lat_count, n).astype(BF), before(n)).reshape(g, lat_count, n)
    return members, jnp.sum(members * counts, axis=1)


def first_kernel(lat_count, ids, home, tokens, chunk, lent, heads):
    rows, width = tokens.shape
    part = width // HALVES
    total = home.shape[1]
    hit = (iota((total, rows), 0) == ids[...]).astype(F32).astype(BF)
    table = jnp.broadcast_to(home[...], (8, total)).astype(F32).astype(BF)
    places = mm(table, hit)[:1].astype(I32)
    dest, block = places >> 1, places & 1
    unused, rank = ranks_of(dest, lat_count)
    rank = rank.astype(I32)
    codes, half = slot_codes(lat_count, 0)
    low, high, meta = pick(codes, half, (dest * STRIDE + rank) * 2 + block)
    both = jnp.concatenate([low, high], axis=1)
    step = 1024
    for i in range(part // step):
        a = tokens[:, i * step : (i + 1) * step]
        b = tokens[:, part + i * step : part + (i + 1) * step]
        chunk[:, i * step : (i + 1) * step] = mm(both, jnp.concatenate([a, b], axis=0)).astype(BF)
    chunk[:, part:] = jnp.broadcast_to(meta.astype(F32), (meta.shape[0], EXTRA)).astype(BF)
    over = (rank >= DIRECT).astype(F32)
    order = mm(jnp.broadcast_to(over, (8, rows)).astype(BF), before(rows))[:1]
    lines = LENT * PIECES
    line = iota((lines, rows), 0)
    take = jnp.logical_and(order.astype(I32) == line // PIECES, over > 0.5)
    take = jnp.where(take, 1.0, 0.0)
    piece = iota((lines, 1), 0) % PIECES
    got = jnp.zeros((lines, width // PIECES), F32)
    for i in range(PIECES):
        chosen = jnp.where(piece == i, take, 0.0).astype(BF)
        got = got + mm(chosen, tokens[:, i * step : (i + 1) * step])
    lent[...] = got.astype(BF)
    heads[...] = jnp.broadcast_to(places, heads.shape)


def second_kernel(lat_count, group, tokens, loans, heads, chunk, left):
    rows, width = tokens.shape
    part = width // HALVES
    lines = LENT * PIECES
    groups = loans.shape[0] // lines
    me = group[0]
    places = heads[...].reshape(groups, heads.shape[0] // groups, rows)[:, 0, :]
    dest, block = places >> 1, places & 1
    members, rank_f = ranks_of(dest, lat_count)
    rank = rank_f.astype(I32)
    over = rank >= DIRECT
    order = mm(over.astype(F32).astype(BF), before(rows)).astype(I32)
    listed = jnp.logical_and(over, order < LENT)
    count = jnp.sum(members, axis=2, keepdims=True)
    asked = jnp.sum(members * listed.astype(F32)[:, None, :], axis=2, keepdims=True)
    used = jnp.maximum(count, float(SLOTS))
    free = jnp.maximum(DIRECT - used, 0.0)
    my_group = iota((groups, 1, 1), 0)
    asked_before = []
    running = jnp.zeros((1, lat_count, 1), F32)
    free_total = jnp.zeros((1, lat_count, 1), F32)
    free_before = jnp.zeros((1, lat_count, 1), F32)
    for t in range(groups):
        asked_before.append(running)
        running = running + asked[t : t + 1]
        free_before = free_before + jnp.where(me > t, free[t : t + 1], 0.0)
        free_total = free_total + free[t : t + 1]
    mine = (my_group == me).astype(F32)
    my_free = jnp.sum(free * mine, axis=0, keepdims=True)
    my_used = jnp.sum(used * mine, axis=0, keepdims=True)

    def look(values):
        return jnp.sum(members * values, axis=1).astype(I32)

    place_in_pool = look(jnp.concatenate(asked_before, axis=0)) + rank - DIRECT
    placed = jnp.logical_and(listed, place_in_pool < look(free_total))
    at = place_in_pool - look(free_before)
    here = jnp.logical_and(placed, jnp.logical_and(at >= 0, at < look(my_free)))
    slot = look(my_used) + at
    lent_code = jnp.where(here, (dest * STRIDE + slot) * 2 + block, -1)
    list_row = iota((lines, rows), 0) // PIECES
    columns = []
    for t in range(groups):
        chosen = jnp.logical_and(order[t : t + 1] == list_row, listed[t : t + 1])
        value = jnp.sum(jnp.where(chosen, lent_code[t : t + 1] + 1, 0), axis=1, keepdims=True) - 1
        columns.append(value)
    column = jnp.concatenate(columns, axis=0)
    size = groups * lines
    lent_row = jnp.sum(
        jnp.where(iota((size, size), 0) == iota((size, size), 1), column, 0), axis=0, keepdims=True
    )
    mine2 = (iota((groups, 1), 0) == me).astype(I32)
    own_code = jnp.sum(((dest * STRIDE + rank) * 2 + block) * mine2, axis=0, keepdims=True)
    missing = jnp.logical_and(over, jnp.logical_not(placed)).astype(I32)
    own_missing = jnp.sum(missing * mine2, axis=0, keepdims=True)
    left[...] = jnp.broadcast_to(jnp.where(own_missing > 0, own_code, -1), left.shape)
    flag = jnp.max(jnp.max(missing.astype(F32), axis=1, keepdims=True), axis=0, keepdims=True)
    codes, half = slot_codes(lat_count, SLOTS)
    low, high, meta = pick(codes, half, own_code)
    low2, high2, meta2 = pick(codes, half, lent_row)
    meta2 = meta2 // PIECES
    both = jnp.concatenate([low, high], axis=1)
    low2, high2 = low2.astype(F32), high2.astype(F32)
    piece = iota((1, size), 1) % PIECES
    step = 1024
    for i in range(part // step):
        lo, hi = slice(i * step, (i + 1) * step), slice(part + i * step, part + (i + 1) * step)
        own = jnp.concatenate([tokens[:, lo], tokens[:, hi]], axis=0)
        both2 = jnp.where(piece == i, low2, 0.0) + jnp.where(piece == i + part // step, high2, 0.0)
        chunk[:, lo] = (mm(both, own) + mm(both2.astype(BF), loans[...])).astype(BF)
    code = (meta + meta2).astype(F32) + 4.0 * flag
    chunk[:, part:] = jnp.broadcast_to(code, (code.shape[0], EXTRA)).astype(BF)


def gradient_body(chunk, enc, dec, bias, dec_bias, cent, err, acc, store, ready):
    rows, padded = chunk.shape
    part = padded - EXTRA
    latents = enc.shape[0]
    step = 1024
    steps = part // step
    group = HALVES * SLOTS
    half = iota((rows, 1), 0) % group // SLOTS
    high_row = iota((group, 1), 0) // SLOTS == 1

    def pair(i):
        lo, hi = slice(i * step, (i + 1) * step), slice(part + i * step, part + (i + 1) * step)
        return lo, hi

    def offset(i):
        lo, hi = pair(i)
        return jnp.where(high_row, dec_bias[:, hi], dec_bias[:, lo])[None]

    def joined(total):
        own = jnp.where(half == 0, total[:, :latents], total[:, latents:])
        down = pltpu.roll(own, SLOTS, 0)
        up = pltpu.roll(own, rows - SLOTS, 0)
        return own + jnp.where(half == 0, up, down)

    def spread(values):
        zero = jnp.zeros_like(values)
        return jnp.concatenate(
            [jnp.where(half == 0, values, zero), jnp.where(half == 1, values, zero)], axis=1
        )

    for i in range(steps):
        lo, hi = pair(i)
        ready("first", i)
        x = chunk[:, lo].astype(F32).reshape(rows // group, group, step)
        c = (x - offset(i)).reshape(rows, step).astype(BF)
        cent[:, lo] = c
        w = jnp.concatenate([enc[:, lo], enc[:, hi]], axis=0)
        if i == 0:
            acc[...] = mm_t(c, w)
        else:
            acc[...] += mm_t(c, w)
    ready("code", 0)
    code = chunk[:, part:].astype(F32)
    code = jnp.where(code >= 4.0, code - 4.0, code)
    second = iota((1, latents), 1) >= latents // 2
    valid = code == jnp.where(second, 2.0, 1.0)
    pre = joined(acc[...]) + bias[...]
    gate = 1.0 / (1.0 + jnp.exp(-pre))
    latent = spread(jnp.where(valid, pre * gate, 0.0))
    latent_b = latent.astype(BF)
    ready("second", 0)
    for i in range(steps):
        lo, hi = pair(i)
        w = jnp.concatenate([dec[:, lo], dec[:, hi]], axis=0)
        d = mm(latent_b, w).astype(BF).astype(F32).reshape(rows // group, group, step)
        x = chunk[:, lo].astype(F32).reshape(rows // group, group, step)
        e = ((offset(i) + d - x) * (1.0 / 32.0)).reshape(rows, step).astype(BF)
        err[:, lo] = e
        if i == 0:
            acc[...] = mm_t(e, w)
        else:
            acc[...] += mm_t(e, w)
    dlatent = joined(acc[...])
    dpre = spread(jnp.where(valid, dlatent * gate * (1.0 + pre * (1.0 - gate)), 0.0))
    dpre_t = dpre.T.astype(BF)
    latent_t = latent.T.astype(BF)
    ready("third", 0)
    for i in range(steps):
        lo, hi = pair(i)
        store(i, 0, mm(dpre_t, cent[:, lo]))
        store(i, 1, mm(latent_t, err[:, lo]))


def part_kernel(chunk, enc, dec, bias, dec_bias, parts, cent, err, acc):
    latents = enc.shape[0]
    steps = parts.shape[0] // HALVES

    def store(i, grad, value):
        rows = slice(grad * latents, (grad + 1) * latents)
        parts[i, rows] = value[:latents]
        parts[steps + i, rows] = value[latents:]

    gradient_body(
        chunk, enc, dec, bias, dec_bias, cent, err, acc, store, lambda stage, i: None
    )


def last_kernel(
    core,
    chunk_in,
    enc_in,
    dec_in,
    bias,
    dec_bias,
    parts_in,
    mine_out,
    other_out,
    flags,
    chunk,
    enc,
    dec,
    parts,
    mine,
    other,
    cent,
    err,
    acc,
    sems_in,
    sems_out,
):
    latents = enc.shape[0]
    steps = parts.shape[0] // HALVES
    part = chunk.shape[1] - EXTRA
    step = part // steps
    moves = {}

    def move(key, source, target):
        moves[key] = pltpu.make_async_copy(source, target, sems_in.at[len(moves)])
        moves[key].start()

    for i in range(steps):
        lo = pl.ds(i * step, step)
        move(("chunk", i), chunk_in.at[:, lo], chunk.at[:, lo])
        for h in range(HALVES):
            cols = pl.ds(h * part + i * step, step)
            move(("enc", i, h), enc_in.at[:, cols], enc.at[:, cols])
    tail = pl.ds(part, EXTRA)
    move("code", chunk_in.at[:, tail], chunk.at[:, tail])
    move("dec", dec_in, dec)
    move("parts", parts_in, parts)

    def ready(stage, i):
        if stage == "first":
            moves[("chunk", i)].wait()
            for h in range(HALVES):
                moves[("enc", i, h)].wait()
        elif stage == "code":
            moves["code"].wait()
        elif stage == "second":
            moves["dec"].wait()
        else:
            moves["parts"].wait()

    def out_copy(which, place):
        source, target = ((mine, mine_out), (other, other_out))[which]
        sem = sems_out.at[which * steps + place]
        return pltpu.make_async_copy(source.at[place], target.at[place], sem)

    def store(i, grad, value):
        rows = slice(grad * latents, (grad + 1) * latents)
        for h in range(HALVES):
            k = h * steps + i
            total = value[h * latents : (h + 1) * latents] + parts[k, rows]

            @pl.when(core[0] == k % 2)
            def _():
                mine[k // 2, rows] = total
                if grad == 1:
                    out_copy(0, k // 2).start()

            @pl.when(core[0] != k % 2)
            def _():
                other[k // 2, rows] = total.astype(BF)
                if grad == 1:
                    out_copy(1, k // 2).start()

    gradient_body(chunk, enc, dec, bias, dec_bias, cent, err, acc, store, ready)
    top = jnp.max(chunk[:, part:].astype(F32), axis=0, keepdims=True)
    flags[...] = jnp.broadcast_to(top, flags.shape)
    for which in range(2):
        for place in range(steps):
            out_copy(which, place).wait()


def vmem():
    return pl.BlockSpec(memory_space=pltpu.VMEM)


def anywhere():
    return pl.BlockSpec(memory_space=pl.ANY)


def smem():
    return pl.BlockSpec(memory_space=pltpu.SMEM)


def on_device(tokens, dec_bias, enc_weight, enc_bias, dec_weight, block_ids, block_home):
    rows, width = tokens.shape
    lat_count = lax.axis_size("lat")
    groups = lax.axis_size("tok")
    part = width // HALVES
    slot_rows = lat_count * HALVES * SLOTS
    latents = enc_weight.shape[0]
    out_width = width // groups
    me = lax.axis_index("tok").astype(I32)
    chunk_shape = jax.ShapeDtypeStruct((slot_rows, part + EXTRA), BF)
    matmul_cost = pl.CostEstimate(
        flops=5 * 2 * slot_rows * 2 * latents * part, bytes_accessed=16 * 2**20, transcendentals=0
    )
    move_cost = pl.CostEstimate(
        flops=2 * slot_rows * 2 * rows * part, bytes_accessed=5 * 2**20, transcendentals=0
    )

    chunk1, lent, heads = pl.pallas_call(
        functools.partial(first_kernel, lat_count),
        out_shape=[
            chunk_shape,
            jax.ShapeDtypeStruct((LENT * PIECES, width // PIECES), BF),
            jax.ShapeDtypeStruct((8, rows), I32),
        ],
        in_specs=[vmem()] * 3,
        out_specs=[vmem()] * 3,
        compiler_params=room(16),
        cost_estimate=move_cost,
        name="first_slots",
    )(block_ids.reshape(1, rows), block_home.reshape(1, -1), tokens)

    def exchange(chunk):
        shaped = chunk.reshape(lat_count, HALVES * SLOTS, part + EXTRA)
        got = lax.all_to_all(shaped, "lat", split_axis=0, concat_axis=0, tiled=True)
        return got.reshape(slot_rows, part + EXTRA)

    heads = lax.all_gather(heads, "tok", tiled=True)
    lent, heads = lax.optimization_barrier((lent, heads))
    loans = lax.all_gather(lent, "tok", tiled=True)
    got1 = exchange(chunk1)
    chunk2, left = pl.pallas_call(
        functools.partial(second_kernel, lat_count),
        out_shape=[chunk_shape, jax.ShapeDtypeStruct((8, rows), I32)],
        in_specs=[smem(), vmem(), vmem(), vmem()],
        out_specs=[vmem()] * 2,
        compiler_params=room(24),
        cost_estimate=move_cost,
        name="second_slots",
    )(me.reshape(1), tokens, loans, heads)
    got2 = exchange(chunk2)

    bias_row = enc_bias.reshape(1, latents)
    offset_row = dec_bias.reshape(1, width)
    work = [
        pltpu.VMEM((slot_rows, part), BF),
        pltpu.VMEM((slot_rows, part), BF),
        pltpu.VMEM((slot_rows, HALVES * latents), F32),
    ]
    part_call = pl.pallas_call(
        part_kernel,
        out_shape=jax.ShapeDtypeStruct((groups, 2 * latents, out_width), F32),
        in_specs=[vmem()] * 5,
        out_specs=vmem(),
        scratch_shapes=work,
        compiler_params=room(56),
        cost_estimate=matmul_cost,
        name="chunk_gradients",
    )
    parts = part_call(got1, enc_weight, dec_weight, bias_row, offset_row)
    core = me % 2
    half_groups = groups // 2
    mine, other, flags = pl.pallas_call(
        last_kernel,
        out_shape=[
            jax.ShapeDtypeStruct((half_groups, 2 * latents, out_width), F32),
            jax.ShapeDtypeStruct((half_groups, 2 * latents, out_width), BF),
            jax.ShapeDtypeStruct((8, EXTRA), F32),
        ],
        in_specs=[smem()] + [anywhere()] * 3 + [vmem()] * 2 + [anywhere()],
        out_specs=[anywhere()] * 2 + [vmem()],
        scratch_shapes=[
            pltpu.VMEM((slot_rows, part + EXTRA), BF),
            pltpu.VMEM((latents, width), BF),
            pltpu.VMEM((latents, width), BF),
            pltpu.VMEM((groups, 2 * latents, out_width), F32),
            pltpu.VMEM((half_groups, 2 * latents, out_width), F32),
            pltpu.VMEM((half_groups, 2 * latents, out_width), BF),
            *work,
            pltpu.SemaphoreType.DMA((3 * half_groups + 3,)),
            pltpu.SemaphoreType.DMA((2 * half_groups,)),
        ],
        compiler_params=room(56),
        cost_estimate=matmul_cost,
        name="last_gradients",
    )(core.reshape(1), got2, enc_weight, dec_weight, bias_row, offset_row, parts)

    def finish(mine, other):
        swapped = lax.ppermute(other, "tok", [(i, i ^ 1) for i in range(groups)])
        summed = (mine + swapped.astype(F32)).astype(BF)
        same_core = [[2 * i + c for i in range(half_groups)] for c in range(2)]
        terms = lax.all_to_all(
            summed, "tok", split_axis=0, concat_axis=0, tiled=True, axis_index_groups=same_core
        )
        total = jnp.sum(terms.astype(F32), axis=0)
        return total[:latents], total[latents:]

    def rest(carry):
        mine, other, unused = carry
        codes, half = slot_codes(lat_count, DIRECT)
        low, high, meta = pick(codes, half, left[:1])
        data = mm(low, tokens[:, :part]) + mm(high, tokens[:, part:])
        extra = jnp.broadcast_to(meta.astype(F32), (slot_rows, EXTRA))
        chunk3 = jnp.concatenate([data, extra], axis=1).astype(BF)
        more = part_call(exchange(chunk3), enc_weight, dec_weight, bias_row, offset_row)
        more = more.reshape(half_groups, 2, 2 * latents, out_width)
        mine = mine + lax.dynamic_index_in_dim(more, core, 1, keepdims=False)
        more = lax.dynamic_index_in_dim(more, 1 - core, 1, keepdims=False)
        return mine, (other.astype(F32) + more).astype(BF), jnp.zeros((), F32)

    mine, other, unused = lax.while_loop(
        lambda carry: carry[2] >= 4.0, rest, (mine, other, flags[0, 0])
    )
    return finish(mine, other)


def solution(mesh):
    in_specs = (
        P(("tok", "lat"), None),
        P(),
        P("lat", None),
        P("lat"),
        P("lat", None),
        P(("tok", "lat"), None),
        P(),
    )
    out_specs = (P("lat", "tok"), P("lat", "tok"))
    return jax.shard_map(
        on_device, mesh=mesh, in_specs=in_specs, out_specs=out_specs, check_vma=False
    )
```

```python
import functools

import jax
import jax.numpy as jnp
from jax import lax
from jax.experimental import pallas as pl
from jax.experimental.pallas import tpu as pltpu
from jax.sharding import PartitionSpec as P

BF = jnp.bfloat16
F32 = jnp.float32
I32 = jnp.int32

CUTS = 4
SLOTS = 2
DIRECT = 2 * SLOTS
GROUP = CUTS * SLOTS
STRIDE = 8
EXTRA = 128
STEP = 1024
PIECES = 8
LENT = (6, 7)
MISSING = 4.0


def room(mib):
    return pltpu.CompilerParams(vmem_limit_bytes=mib * 2**20)


def mm(a, b):
    return jnp.dot(a, b, preferred_element_type=F32)


def mm_t(a, b):
    return lax.dot_general(a, b, (((1,), (1,)), ((), ())), preferred_element_type=F32)


def iota(shape, axis):
    return lax.broadcasted_iota(I32, shape, axis)


def flat(mask):
    return jnp.where(mask, 1.0, 0.0)


def slot_codes(targets, first):
    row = iota((targets * GROUP, 1), 0)
    inner = row % GROUP
    return (row // GROUP) * STRIDE + first + inner % SLOTS, inner // SLOTS


def before(n):
    return (iota((n, n), 0) < iota((n, n), 1)).astype(F32).astype(BF)


def ranks_of(target, targets):
    g, n = target.shape
    members = flat(target[:, None, :] == iota((g, targets, n), 1))
    counts = mm(members.reshape(g * targets, n).astype(BF), before(n)).reshape(g, targets, n)
    return members, jnp.sum(members * counts, axis=1)


def target_of(places, targets):
    return (places & 1) * (targets // 2) + (places >> 1)


def cut_columns(ref, i):
    part = ref.shape[1] // CUTS
    return [ref[:, h * part + i * STEP : h * part + (i + 1) * STEP] for h in range(CUTS)]


def first_kernel(targets, ids, home, tokens, chunk, lent_a, lent_b):
    rows, width = tokens.shape
    part = width // CUTS
    total = home.shape[1]
    named = flat(iota((total, rows), 0) == ids[...]).astype(BF)
    table = jnp.broadcast_to(home[...], (8, total)).astype(F32).astype(BF)
    places = mm(table, named)[:1].astype(I32)
    target = target_of(places, targets)
    unused, rank = ranks_of(target, targets)
    rank = rank.astype(I32)
    codes, cut = slot_codes(targets, 0)
    hit = flat(codes == target * STRIDE + rank)
    wide = jnp.concatenate([jnp.where(cut == h, hit, 0.0) for h in range(CUTS)], axis=1)
    wide = wide.astype(BF)
    for i in range(part // STEP):
        got = mm(wide, jnp.concatenate(cut_columns(tokens, i), axis=0))
        chunk[:, i * STEP : (i + 1) * STEP] = got.astype(BF)
    meta = jnp.sum(hit, axis=1, keepdims=True)
    chunk[:, part:] = jnp.broadcast_to(meta, (meta.shape[0], EXTRA)).astype(BF)
    over = flat(rank >= DIRECT)
    order = mm(jnp.broadcast_to(over, (8, rows)).astype(BF), before(rows))[:1].astype(I32)
    first = 0
    for count, lent in zip(LENT, (lent_a, lent_b)):
        lines = lent.shape[0]
        line = iota((lines, rows), 0)
        take = jnp.logical_and(order == first + line // PIECES, over > 0.5)
        take = flat(jnp.logical_and(take, line < count * PIECES))
        piece = iota((lines, 1), 0) % PIECES
        got = jnp.zeros((lines, STEP), F32)
        for i in range(PIECES):
            chosen = jnp.where(piece == i, take, 0.0).astype(BF)
            got = got + mm(chosen, tokens[:, i * STEP : (i + 1) * STEP])
        if first == 0:
            head = jnp.where(line == count * PIECES, places.astype(F32), got[:, :rows])
            got = jnp.concatenate([head, got[:, rows:]], axis=1)
        lent[...] = got.astype(BF)
        first += count


def second_kernel(targets, group, tokens, loans_a, loans_b, chunk, left):
    rows, width = tokens.shape
    part = width // CUTS
    lines = (LENT[0] + 1) * PIECES
    groups = loans_a.shape[0] // lines
    me = group[0]
    heads = loans_a[:, :rows].astype(F32).reshape(groups, lines, rows)
    places = heads[:, LENT[0] * PIECES, :].astype(I32)
    target = target_of(places, targets)
    members, rank_f = ranks_of(target, targets)
    rank = rank_f.astype(I32)
    over = rank >= DIRECT
    order = mm(flat(over).astype(BF), before(rows)).astype(I32)
    listed = jnp.logical_and(over, order < sum(LENT))
    count = jnp.sum(members, axis=2, keepdims=True)
    asked = jnp.sum(members * flat(listed)[:, None, :], axis=2, keepdims=True)
    used = jnp.maximum(count, float(SLOTS))
    free = jnp.maximum(DIRECT - used, 0.0)
    asked_before = []
    running = jnp.zeros((1, targets, 1), F32)
    free_total = jnp.zeros((1, targets, 1), F32)
    free_before = jnp.zeros((1, targets, 1), F32)
    for t in range(groups):
        asked_before.append(running)
        running = running + asked[t : t + 1]
        free_before = free_before + jnp.where(me > t, free[t : t + 1], 0.0)
        free_total = free_total + free[t : t + 1]
    mine = flat(iota((groups, 1, 1), 0) == me)
    my_free = jnp.sum(free * mine, axis=0, keepdims=True)
    my_used = jnp.sum(used * mine, axis=0, keepdims=True)

    def look(values):
        return jnp.sum(members * values, axis=1).astype(I32)

    in_pool = look(jnp.concatenate(asked_before, axis=0)) + rank - DIRECT
    placed = jnp.logical_and(listed, in_pool < look(free_total))
    at = in_pool - look(free_before)
    here = jnp.logical_and(placed, jnp.logical_and(at >= 0, at < look(my_free)))
    lent_code = jnp.where(here, target * STRIDE + look(my_used) + at, -1)
    size = groups * lines
    square = iota((size, size), 0) == iota((size, size), 1)
    line_of = iota((lines, rows), 0) // PIECES

    def codes_of_lines(first, count):
        columns = []
        for t in range(groups):
            chosen = jnp.logical_and(order[t : t + 1] == first + line_of, listed[t : t + 1])
            chosen = jnp.logical_and(chosen, line_of < count)
            value = jnp.where(chosen, lent_code[t : t + 1] + 1, 0)
            columns.append(jnp.sum(value, axis=1, keepdims=True) - 1)
        column = jnp.concatenate(columns, axis=0)
        return jnp.sum(jnp.where(square, column, 0), axis=0, keepdims=True)

    mine2 = (iota((groups, 1), 0) == me).astype(I32)
    own_code = jnp.sum((target * STRIDE + rank) * mine2, axis=0, keepdims=True)
    missing = jnp.logical_and(over, jnp.logical_not(placed)).astype(I32)
    own_missing = jnp.sum(missing * mine2, axis=0, keepdims=True)
    left[...] = jnp.broadcast_to(jnp.where(own_missing > 0, own_code, -1), left.shape)
    flag = jnp.max(jnp.max(missing.astype(F32), axis=1, keepdims=True), axis=0, keepdims=True)
    codes, cut = slot_codes(targets, SLOTS)
    hit = flat(codes == own_code)
    wide = jnp.concatenate([jnp.where(cut == h, hit, 0.0) for h in range(CUTS)], axis=1)
    wide = wide.astype(BF)
    hit_a = flat(codes == codes_of_lines(0, LENT[0]))
    hit_b = flat(codes == codes_of_lines(LENT[0], LENT[1]))
    per_cut = part // STEP
    piece = iota((1, size), 1) % PIECES
    for i in range(per_cut):
        at_cut = cut * per_cut + i == piece
        got = mm(wide, jnp.concatenate(cut_columns(tokens, i), axis=0))
        got = got + mm(jnp.where(at_cut, hit_a, 0.0).astype(BF), loans_a[...])
        got = got + mm(jnp.where(at_cut, hit_b, 0.0).astype(BF), loans_b[...])
        chunk[:, i * STEP : (i + 1) * STEP] = got.astype(BF)
    lent_meta = jnp.sum(hit_a, axis=1, keepdims=True) + jnp.sum(hit_b, axis=1, keepdims=True)
    code = jnp.sum(hit, axis=1, keepdims=True) + lent_meta * (1.0 / PIECES) + MISSING * flag
    chunk[:, part:] = jnp.broadcast_to(code, (code.shape[0], EXTRA)).astype(BF)


def gradient_body(chunk, enc, dec, bias, dec_bias, cent, err, acc, store, ready):
    rows, padded = chunk.shape
    part = padded - EXTRA
    latents = enc.shape[0]
    steps = part // STEP
    inner = iota((rows, 1), 0) % GROUP
    cut = inner // SLOTS
    cut8 = iota((GROUP, 1), 0) // SLOTS

    def here(i):
        return slice(i * STEP, (i + 1) * STEP)

    def offset(i):
        value = jnp.zeros((GROUP, STEP), F32)
        for h, columns in enumerate(cut_columns(dec_bias, i)):
            value = jnp.where(cut8 == h, columns, value)
        return value[None]

    def joined(total):
        own = total[:, :latents]
        for h in range(1, CUTS):
            own = jnp.where(cut == h, total[:, h * latents : (h + 1) * latents], own)
        shift = GROUP // 2
        while shift >= SLOTS:
            down = pltpu.roll(own, rows - shift, 0)
            wrapped = pltpu.roll(own, GROUP - shift, 0)
            own = own + jnp.where(inner < GROUP - shift, down, wrapped)
            shift //= 2
        return own

    def spread(values):
        return jnp.concatenate([jnp.where(cut == h, values, 0.0) for h in range(CUTS)], axis=1)

    for i in range(steps):
        ready("first", i)
        x = chunk[:, here(i)].astype(F32).reshape(rows // GROUP, GROUP, STEP)
        c = (x - offset(i)).reshape(rows, STEP).astype(BF)
        cent[:, here(i)] = c
        w = jnp.concatenate(cut_columns(enc, i), axis=0)
        if i == 0:
            acc[...] = mm_t(c, w)
        else:
            acc[...] += mm_t(c, w)
    ready("code", 0)
    code = chunk[:, part : part + latents].astype(F32)
    valid = jnp.where(code >= MISSING, code - MISSING, code) > 0.5
    pre = joined(acc[...]) + bias[...]
    gate = 1.0 / (1.0 + jnp.exp(-pre))
    latent = spread(jnp.where(valid, pre * gate, 0.0))
    latent_b = latent.astype(BF)
    ready("second", 0)
    for i in range(steps):
        w = jnp.concatenate(cut_columns(dec, i), axis=0)
        d = mm(latent_b, w).astype(BF).astype(F32).reshape(rows // GROUP, GROUP, STEP)
        x = chunk[:, here(i)].astype(F32).reshape(rows // GROUP, GROUP, STEP)
        e = ((offset(i) + d - x) * (1.0 / 32.0)).reshape(rows, STEP).astype(BF)
        err[:, here(i)] = e
        if i == 0:
            acc[...] = mm_t(e, w)
        else:
            acc[...] += mm_t(e, w)
    dlatent = joined(acc[...])
    dpre = spread(jnp.where(valid, dlatent * gate * (1.0 + pre * (1.0 - gate)), 0.0))
    dpre_t = dpre.T.astype(BF)
    latent_t = latent.T.astype(BF)
    ready("third", 0)
    for i in range(steps):
        store(i, 0, mm(dpre_t, cent[:, here(i)]))
        store(i, 1, mm(latent_t, err[:, here(i)]))


class Loader:
    def __init__(self, sems, first_row, chunk_in, enc_in, dec_in, chunk, enc, dec):
        self.sems = sems
        self.moves = {}
        part = chunk.shape[1] - EXTRA
        latents = enc.shape[0]
        rows = pl.ds(pl.multiple_of(first_row, latents), latents)
        for i in range(part // STEP):
            here = pl.ds(i * STEP, STEP)
            self.move(("chunk", i), chunk_in.at[:, here], chunk.at[:, here])
            for h in range(CUTS):
                columns = pl.ds(h * part + i * STEP, STEP)
                self.move(("enc", i, h), enc_in.at[rows, columns], enc.at[:, columns])
        tail = pl.ds(part, EXTRA)
        self.move("code", chunk_in.at[:, tail], chunk.at[:, tail])
        self.move("second", dec_in.at[rows], dec)

    def move(self, key, source, target):
        self.moves[key] = pltpu.make_async_copy(source, target, self.sems.at[len(self.moves)])
        self.moves[key].start()

    def __call__(self, stage, i):
        if stage == "first":
            self.moves[("chunk", i)].wait()
            for h in range(CUTS):
                self.moves[("enc", i, h)].wait()
        elif stage in self.moves:
            self.moves[stage].wait()


def part_kernel(
    at, chunk_in, enc_in, dec_in, bias, dec_bias, parts, chunk, enc, dec, cent, err, acc, sems
):
    latents = enc.shape[0]
    ready = Loader(sems, at[1], chunk_in, enc_in, dec_in, chunk, enc, dec)

    def store(i, grad, value):
        rows = slice(grad * latents, (grad + 1) * latents)
        for h in range(CUTS):
            parts[i, h, rows] = value[h * latents : (h + 1) * latents]

    gradient_body(chunk, enc, dec, bias, dec_bias, cent, err, acc, store, ready)


def last_kernel(
    at,
    chunk_in,
    enc_in,
    dec_in,
    bias,
    dec_bias,
    parts_in,
    mine_out,
    other_out,
    flags,
    chunk,
    enc,
    dec,
    cent,
    err,
    acc,
    sems,
    parts,
    mine,
    other,
    sems_out,
):
    latents = enc.shape[0]
    core = at[0]
    ready = Loader(sems, at[1], chunk_in, enc_in, dec_in, chunk, enc, dec)
    ready.move("third", parts_in, parts)

    def out_copy(which, grad):
        source, result = ((mine, mine_out), (other, other_out))[which]
        rows = pl.ds(grad * latents, latents)
        sem = sems_out.at[2 * which + grad]
        return pltpu.make_async_copy(source.at[:, rows], result.at[:, rows], sem)

    def store(i, grad, value):
        rows = slice(grad * latents, (grad + 1) * latents)
        totals = [
            value[h * latents : (h + 1) * latents] + parts[i, h, rows] for h in range(CUTS)
        ]

        @pl.when(core == i)
        def _():
            for h in range(CUTS):
                mine[h, rows] = totals[h]
            out_copy(0, grad).start()

        @pl.when(core != i)
        def _():
            for h in range(CUTS):
                other[h, rows] = totals[h].astype(BF)
            out_copy(1, grad).start()

    gradient_body(chunk, enc, dec, bias, dec_bias, cent, err, acc, store, ready)
    top = jnp.max(chunk[:, chunk.shape[1] - EXTRA :].astype(F32), axis=0, keepdims=True)
    flags[0] = jnp.max(top)
    for which in range(2):
        for grad in range(2):
            out_copy(which, grad).wait()


def vmem():
    return pl.BlockSpec(memory_space=pltpu.VMEM)


def anywhere():
    return pl.BlockSpec(memory_space=pl.ANY)


def smem():
    return pl.BlockSpec(memory_space=pltpu.SMEM)


def on_device(tokens, dec_bias, enc_weight, enc_bias, dec_weight, block_ids, block_home):
    rows, width = tokens.shape
    lat_count = lax.axis_size("lat")
    groups = lax.axis_size("tok")
    chips = groups // 2
    targets = 2 * lat_count
    part = width // CUTS
    slot_rows = targets * GROUP
    latents = enc_weight.shape[0] // 2
    per_cut = part // STEP
    me = lax.axis_index("tok").astype(I32)
    core = me % 2
    first_row = (me // 2 % 2) * latents
    scalars = jnp.stack([core, first_row])
    exchange_groups = [
        [(4 * p + 2 * b + c) * lat_count + at for b in range(2) for at in range(lat_count)]
        for p in range(groups // 4)
        for c in range(2)
    ]
    chunk_shape = jax.ShapeDtypeStruct((slot_rows, part + EXTRA), BF)
    lent_shape = jax.ShapeDtypeStruct((max(LENT) * PIECES, STEP), BF)
    matmul_cost = pl.CostEstimate(
        flops=5 * 2 * slot_rows * CUTS * latents * part,
        bytes_accessed=12 * 2**20,
        transcendentals=0,
    )
    move_cost = pl.CostEstimate(
        flops=2 * slot_rows * CUTS * rows * part, bytes_accessed=5 * 2**20, transcendentals=0
    )

    chunk1, lent_a, lent_b = pl.pallas_call(
        functools.partial(first_kernel, targets),
        out_shape=[chunk_shape, lent_shape, lent_shape],
        in_specs=[vmem()] * 3,
        out_specs=[vmem()] * 3,
        compiler_params=room(20),
        cost_estimate=move_cost,
        name="first_slots",
    )(block_ids.reshape(1, rows), block_home.reshape(1, -1), tokens)

    def exchange(chunk):
        shaped = chunk.reshape(targets, GROUP, part + EXTRA)
        got = lax.all_to_all(
            shaped,
            ("tok", "lat"),
            split_axis=0,
            concat_axis=0,
            tiled=True,
            axis_index_groups=exchange_groups,
        )
        return got.reshape(slot_rows, part + EXTRA)

    loans_a = lax.all_gather(lent_a, "tok", tiled=True)
    loans_a, lent_b = lax.optimization_barrier((loans_a, lent_b))
    loans_b = lax.all_gather(lent_b, "tok", tiled=True)
    got1 = exchange(chunk1)
    chunk2, left = pl.pallas_call(
        functools.partial(second_kernel, targets),
        out_shape=[chunk_shape, jax.ShapeDtypeStruct((8, rows), I32)],
        in_specs=[smem()] + [vmem()] * 3,
        out_specs=[vmem()] * 2,
        compiler_params=room(24),
        cost_estimate=move_cost,
        name="second_slots",
    )(me.reshape(1), tokens, loans_a, loans_b)
    got2 = exchange(chunk2)

    bias_row = lax.dynamic_slice_in_dim(enc_bias, first_row, latents).reshape(1, latents)
    offset_row = dec_bias.reshape(1, width)
    work = [
        pltpu.VMEM((slot_rows, part + EXTRA), BF),
        pltpu.VMEM((latents, width), BF),
        pltpu.VMEM((latents, width), BF),
        pltpu.VMEM((slot_rows, part), BF),
        pltpu.VMEM((slot_rows, part), BF),
        pltpu.VMEM((slot_rows, CUTS * latents), F32),
        pltpu.SemaphoreType.DMA((per_cut * (CUTS + 1) + 3,)),
    ]
    parts_shape = (per_cut, CUTS, 2 * latents, STEP)
    half_shape = (CUTS, 2 * latents, STEP)
    part_call = pl.pallas_call(
        part_kernel,
        out_shape=jax.ShapeDtypeStruct(parts_shape, F32),
        in_specs=[smem()] + [anywhere()] * 3 + [vmem()] * 2,
        out_specs=vmem(),
        scratch_shapes=work,
        compiler_params=room(56),
        cost_estimate=matmul_cost,
        name="chunk_gradients",
    )
    parts = part_call(scalars, got1, enc_weight, dec_weight, bias_row, offset_row)
    mine, other, flags = pl.pallas_call(
        last_kernel,
        out_shape=[
            jax.ShapeDtypeStruct(half_shape, F32),
            jax.ShapeDtypeStruct(half_shape, BF),
            jax.ShapeDtypeStruct((1,), F32),
        ],
        in_specs=[smem()] + [anywhere()] * 3 + [vmem()] * 2 + [anywhere()],
        out_specs=[anywhere()] * 2 + [smem()],
        scratch_shapes=[
            *work,
            pltpu.VMEM(parts_shape, F32),
            pltpu.VMEM(half_shape, F32),
            pltpu.VMEM(half_shape, BF),
            pltpu.SemaphoreType.DMA((4,)),
        ],
        compiler_params=room(56),
        cost_estimate=matmul_cost,
        name="last_gradients",
    )(scalars, got2, enc_weight, dec_weight, bias_row, offset_row, parts)

    def rest(carry):
        mine, other, unused = carry
        codes, cut = slot_codes(targets, DIRECT)
        hit = flat(codes == left[:1])
        data = jnp.zeros((slot_rows, part), F32)
        for h in range(CUTS):
            chosen = jnp.where(cut == h, hit, 0.0).astype(BF)
            data = data + mm(chosen, tokens[:, h * part : (h + 1) * part])
        extra = jnp.broadcast_to(jnp.sum(hit, axis=1, keepdims=True), (slot_rows, EXTRA))
        chunk3 = jnp.concatenate([data, extra], axis=1).astype(BF)
        more = part_call(scalars, exchange(chunk3), enc_weight, dec_weight, bias_row, offset_row)
        mine = mine + lax.dynamic_index_in_dim(more, core, 0, keepdims=False)
        more = lax.dynamic_index_in_dim(more, 1 - core, 0, keepdims=False)
        return mine, (other.astype(F32) + more).astype(BF), jnp.zeros((), F32)

    mine, other, unused = lax.while_loop(
        lambda carry: carry[2] >= MISSING, rest, (mine, other, flags.reshape(()))
    )
    swapped = lax.ppermute(other, "tok", [(i, i ^ 1) for i in range(groups)])
    summed = (mine + swapped.astype(F32)).astype(BF)
    terms = lax.all_to_all(
        summed,
        "tok",
        split_axis=0,
        concat_axis=0,
        tiled=True,
        axis_index_groups=[[2 * i + c for i in range(chips)] for c in range(2)],
    )
    total = jnp.sum(terms.astype(F32).reshape(chips // 2, 2, 2, latents, STEP), axis=0)
    return total[:, 0].reshape(2 * latents, STEP), total[:, 1].reshape(2 * latents, STEP)


def solution(mesh):
    in_specs = (
        P(("tok", "lat"), None),
        P(),
        P("lat", None),
        P("lat"),
        P("lat", None),
        P(("tok", "lat"), None),
        P(),
    )
    out_specs = (P("lat", "tok"), P("lat", "tok"))
    return jax.shard_map(
        on_device, mesh=mesh, in_specs=in_specs, out_specs=out_specs, check_vma=False
    )
```

```python
import functools

import jax
import jax.numpy as jnp
from jax import lax
from jax.experimental import pallas as pl
from jax.experimental.pallas import tpu as pltpu
from jax.sharding import PartitionSpec as P

BF = jnp.bfloat16
F32 = jnp.float32
I32 = jnp.int32

CUTS = 4
SLOTS = 2
DIRECT = 2 * SLOTS
GROUP = CUTS * SLOTS
STRIDE = 8
EMPTY = 2.0**100
STEP = 1024
PIECES = 8
LENT = (6, 7)


def room(mib):
    return pltpu.CompilerParams(vmem_limit_bytes=mib * 2**20)


def mm(a, b):
    return jnp.dot(a, b, preferred_element_type=F32)


def mm_t(a, b):
    return lax.dot_general(a, b, (((1,), (1,)), ((), ())), preferred_element_type=F32)


def iota(shape, axis):
    return lax.broadcasted_iota(I32, shape, axis)


def flat(mask):
    return jnp.where(mask, 1.0, 0.0)


def slot_codes(targets, first):
    row = iota((targets * GROUP, 1), 0)
    inner = row % GROUP
    return (row // GROUP) * STRIDE + first + inner % SLOTS, inner // SLOTS


def before(n):
    return (iota((n, n), 0) < iota((n, n), 1)).astype(F32).astype(BF)


def ranks_of(target, targets):
    g, n = target.shape
    members = flat(target[:, None, :] == iota((g, targets, n), 1))
    counts = mm(members.reshape(g * targets, n).astype(BF), before(n)).reshape(g, targets, n)
    return members, jnp.sum(members * counts, axis=1)


def target_of(places, targets):
    return (places & 1) * (targets // 2) + (places >> 1)


def cut_columns(ref, i):
    part = ref.shape[1] // CUTS
    return [ref[:, h * part + i * STEP : h * part + (i + 1) * STEP] for h in range(CUTS)]


def first_kernel(targets, ids, home, tokens, chunk, lent_a, lent_b):
    rows, width = tokens.shape
    part = width // CUTS
    total = home.shape[1]
    named = flat(iota((total, rows), 0) == ids[...]).astype(BF)
    table = jnp.broadcast_to(home[...], (8, total)).astype(F32).astype(BF)
    places = mm(table, named)[:1].astype(I32)
    target = target_of(places, targets)
    unused, rank = ranks_of(target, targets)
    rank = rank.astype(I32)
    codes, cut = slot_codes(targets, 0)
    hit = flat(codes == target * STRIDE + rank)
    wide = jnp.concatenate([jnp.where(cut == h, hit, 0.0) for h in range(CUTS)], axis=1)
    wide = wide.astype(BF)
    filled = jnp.sum(hit, axis=1, keepdims=True) > 0.5
    for i in range(part // STEP):
        got = mm(wide, jnp.concatenate(cut_columns(tokens, i), axis=0))
        chunk[:, i * STEP : (i + 1) * STEP] = jnp.where(filled, got, EMPTY).astype(BF)
    over = flat(rank >= DIRECT)
    order = mm(jnp.broadcast_to(over, (8, rows)).astype(BF), before(rows))[:1].astype(I32)
    first = 0
    for count, lent in zip(LENT, (lent_a, lent_b)):
        lines = lent.shape[0]
        line = iota((lines, rows), 0)
        take = jnp.logical_and(order == first + line // PIECES, over > 0.5)
        take = flat(jnp.logical_and(take, line < count * PIECES))
        piece = iota((lines, 1), 0) % PIECES
        got = jnp.zeros((lines, STEP), F32)
        for i in range(PIECES):
            chosen = jnp.where(piece == i, take, 0.0).astype(BF)
            got = got + mm(chosen, tokens[:, i * STEP : (i + 1) * STEP])
        if first == 0:
            head = jnp.where(line == count * PIECES, places.astype(F32), got[:, :rows])
            got = jnp.concatenate([head, got[:, rows:]], axis=1)
        lent[...] = got.astype(BF)
        first += count


def second_kernel(targets, group, tokens, loans_a, loans_b, chunk, left, flags):
    rows, width = tokens.shape
    part = width // CUTS
    lines = (LENT[0] + 1) * PIECES
    groups = loans_a.shape[0] // lines
    me = group[0]
    heads = loans_a[:, :rows].astype(F32).reshape(groups, lines, rows)
    places = heads[:, LENT[0] * PIECES, :].astype(I32)
    target = target_of(places, targets)
    members, rank_f = ranks_of(target, targets)
    rank = rank_f.astype(I32)
    over = rank >= DIRECT
    order = mm(flat(over).astype(BF), before(rows)).astype(I32)
    listed = jnp.logical_and(over, order < sum(LENT))
    count = jnp.sum(members, axis=2, keepdims=True)
    asked = jnp.sum(members * flat(listed)[:, None, :], axis=2, keepdims=True)
    used = jnp.maximum(count, float(SLOTS))
    free = jnp.maximum(DIRECT - used, 0.0)
    asked_before = []
    running = jnp.zeros((1, targets, 1), F32)
    free_total = jnp.zeros((1, targets, 1), F32)
    free_before = jnp.zeros((1, targets, 1), F32)
    for t in range(groups):
        asked_before.append(running)
        running = running + asked[t : t + 1]
        free_before = free_before + jnp.where(me > t, free[t : t + 1], 0.0)
        free_total = free_total + free[t : t + 1]
    mine = flat(iota((groups, 1, 1), 0) == me)
    my_free = jnp.sum(free * mine, axis=0, keepdims=True)
    my_used = jnp.sum(used * mine, axis=0, keepdims=True)

    def look(values):
        return jnp.sum(members * values, axis=1).astype(I32)

    in_pool = look(jnp.concatenate(asked_before, axis=0)) + rank - DIRECT
    placed = jnp.logical_and(listed, in_pool < look(free_total))
    at = in_pool - look(free_before)
    here = jnp.logical_and(placed, jnp.logical_and(at >= 0, at < look(my_free)))
    lent_code = jnp.where(here, target * STRIDE + look(my_used) + at, -1)
    size = groups * lines
    square = iota((size, size), 0) == iota((size, size), 1)
    line_of = iota((lines, rows), 0) // PIECES

    def codes_of_lines(first, count):
        columns = []
        for t in range(groups):
            chosen = jnp.logical_and(order[t : t + 1] == first + line_of, listed[t : t + 1])
            chosen = jnp.logical_and(chosen, line_of < count)
            value = jnp.where(chosen, lent_code[t : t + 1] + 1, 0)
            columns.append(jnp.sum(value, axis=1, keepdims=True) - 1)
        column = jnp.concatenate(columns, axis=0)
        return jnp.sum(jnp.where(square, column, 0), axis=0, keepdims=True)

    mine2 = (iota((groups, 1), 0) == me).astype(I32)
    own_code = jnp.sum((target * STRIDE + rank) * mine2, axis=0, keepdims=True)
    missing = jnp.logical_and(over, jnp.logical_not(placed)).astype(I32)
    own_missing = jnp.sum(missing * mine2, axis=0, keepdims=True)
    left[...] = jnp.broadcast_to(jnp.where(own_missing > 0, own_code, -1), left.shape)
    flag = jnp.max(jnp.max(missing.astype(F32), axis=1, keepdims=True), axis=0, keepdims=True)
    codes, cut = slot_codes(targets, SLOTS)
    hit = flat(codes == own_code)
    wide = jnp.concatenate([jnp.where(cut == h, hit, 0.0) for h in range(CUTS)], axis=1)
    wide = wide.astype(BF)
    hit_a = flat(codes == codes_of_lines(0, LENT[0]))
    hit_b = flat(codes == codes_of_lines(LENT[0], LENT[1]))
    filled = jnp.sum(hit, axis=1, keepdims=True) + jnp.sum(hit_a, axis=1, keepdims=True)
    filled = filled + jnp.sum(hit_b, axis=1, keepdims=True) > 0.5
    flags[...] = jnp.broadcast_to(flag, flags.shape)
    per_cut = part // STEP
    piece = iota((1, size), 1) % PIECES
    for i in range(per_cut):
        at_cut = cut * per_cut + i == piece
        got = mm(wide, jnp.concatenate(cut_columns(tokens, i), axis=0))
        got = got + mm(jnp.where(at_cut, hit_a, 0.0).astype(BF), loans_a[...])
        got = got + mm(jnp.where(at_cut, hit_b, 0.0).astype(BF), loans_b[...])
        chunk[:, i * STEP : (i + 1) * STEP] = jnp.where(filled, got, EMPTY).astype(BF)


def gradient_body(chunk, enc, dec, bias, dec_bias, cent, err, acc, store, ready):
    rows, part = chunk.shape
    latents = enc.shape[0]
    steps = part // STEP
    inner = iota((rows, 1), 0) % GROUP
    cut = inner // SLOTS
    cut8 = iota((GROUP, 1), 0) // SLOTS

    def here(i):
        return slice(i * STEP, (i + 1) * STEP)

    def offset(i):
        value = jnp.zeros((GROUP, STEP), F32)
        for h, columns in enumerate(cut_columns(dec_bias, i)):
            value = jnp.where(cut8 == h, columns, value)
        return value[None]

    def joined(total):
        own = total[:, :latents]
        for h in range(1, CUTS):
            own = jnp.where(cut == h, total[:, h * latents : (h + 1) * latents], own)
        shift = GROUP // 2
        while shift >= SLOTS:
            down = pltpu.roll(own, rows - shift, 0)
            wrapped = pltpu.roll(own, GROUP - shift, 0)
            own = own + jnp.where(inner < GROUP - shift, down, wrapped)
            shift //= 2
        return own

    def spread(values):
        return jnp.concatenate([jnp.where(cut == h, values, 0.0) for h in range(CUTS)], axis=1)

    for i in range(steps):
        ready("first", i)
        x = chunk[:, here(i)].astype(F32).reshape(rows // GROUP, GROUP, STEP)
        c = (x - offset(i)).reshape(rows, STEP).astype(BF)
        cent[:, here(i)] = c
        w = jnp.concatenate(cut_columns(enc, i), axis=0)
        if i == 0:
            acc[...] = mm_t(c, w)
        else:
            acc[...] += mm_t(c, w)
    valid = chunk[:, :latents].astype(F32) < EMPTY / 2
    pre = joined(acc[...]) + bias[...]
    gate = 1.0 / (1.0 + jnp.exp(-pre))
    latent = spread(jnp.where(valid, pre * gate, 0.0))
    latent_b = latent.astype(BF)
    ready("second", 0)
    for i in range(steps):
        w = jnp.concatenate(cut_columns(dec, i), axis=0)
        d = mm(latent_b, w).astype(BF).astype(F32).reshape(rows // GROUP, GROUP, STEP)
        x = chunk[:, here(i)].astype(F32).reshape(rows // GROUP, GROUP, STEP)
        e = ((offset(i) + d - x) * (1.0 / 32.0)).reshape(rows, STEP).astype(BF)
        err[:, here(i)] = e
        if i == 0:
            acc[...] = mm_t(e, w)
        else:
            acc[...] += mm_t(e, w)
    dlatent = joined(acc[...])
    dpre = spread(jnp.where(valid, dlatent * gate * (1.0 + pre * (1.0 - gate)), 0.0))
    dpre_t = dpre.T.astype(BF)
    latent_t = latent.T.astype(BF)
    ready("third", 0)
    for i in range(steps):
        store(i, 0, mm(dpre_t, cent[:, here(i)]))
        store(i, 1, mm(latent_t, err[:, here(i)]))


class Loader:
    def __init__(self, sems, first_row, chunk_in, enc_in, dec_in, chunk, enc, dec):
        self.sems = sems
        self.moves = {}
        part = chunk.shape[1]
        latents = enc.shape[0]
        rows = pl.ds(pl.multiple_of(first_row, latents), latents)
        for i in range(part // STEP):
            here = pl.ds(i * STEP, STEP)
            self.move(("chunk", i), chunk_in.at[:, here], chunk.at[:, here])
            for h in range(CUTS):
                columns = pl.ds(h * part + i * STEP, STEP)
                self.move(("enc", i, h), enc_in.at[rows, columns], enc.at[:, columns])
        self.move("second", dec_in.at[rows], dec)

    def move(self, key, source, target):
        self.moves[key] = pltpu.make_async_copy(source, target, self.sems.at[len(self.moves)])
        self.moves[key].start()

    def __call__(self, stage, i):
        if stage == "first":
            self.moves[("chunk", i)].wait()
            for h in range(CUTS):
                self.moves[("enc", i, h)].wait()
        elif stage in self.moves:
            self.moves[stage].wait()


def part_kernel(
    at, chunk_in, enc_in, dec_in, bias, dec_bias, parts, chunk, enc, dec, cent, err, acc, sems
):
    latents = enc.shape[0]
    ready = Loader(sems, at[1], chunk_in, enc_in, dec_in, chunk, enc, dec)

    def store(i, grad, value):
        rows = slice(grad * latents, (grad + 1) * latents)
        for h in range(CUTS):
            parts[i, h, rows] = value[h * latents : (h + 1) * latents]

    gradient_body(chunk, enc, dec, bias, dec_bias, cent, err, acc, store, ready)


def last_kernel(
    at,
    chunk_in,
    enc_in,
    dec_in,
    bias,
    dec_bias,
    parts_in,
    mine_out,
    other_out,
    chunk,
    enc,
    dec,
    cent,
    err,
    acc,
    sems,
    parts,
    mine,
    other,
    sems_out,
):
    latents = enc.shape[0]
    core = at[0]
    ready = Loader(sems, at[1], chunk_in, enc_in, dec_in, chunk, enc, dec)
    ready.move("third", parts_in, parts)

    def out_copy(which, grad):
        source, result = ((mine, mine_out), (other, other_out))[which]
        rows = pl.ds(grad * latents, latents)
        sem = sems_out.at[2 * which + grad]
        return pltpu.make_async_copy(source.at[:, rows], result.at[:, rows], sem)

    def store(i, grad, value):
        rows = slice(grad * latents, (grad + 1) * latents)
        totals = [
            value[h * latents : (h + 1) * latents] + parts[i, h, rows] for h in range(CUTS)
        ]

        @pl.when(core == i)
        def _():
            for h in range(CUTS):
                mine[h, rows] = totals[h]
            out_copy(0, grad).start()

        @pl.when(core != i)
        def _():
            for h in range(CUTS):
                other[h, rows] = totals[h].astype(BF)
            out_copy(1, grad).start()

    gradient_body(chunk, enc, dec, bias, dec_bias, cent, err, acc, store, ready)
    for which in range(2):
        for grad in range(2):
            out_copy(which, grad).wait()


def vmem():
    return pl.BlockSpec(memory_space=pltpu.VMEM)


def anywhere():
    return pl.BlockSpec(memory_space=pl.ANY)


def smem():
    return pl.BlockSpec(memory_space=pltpu.SMEM)


def on_device(tokens, dec_bias, enc_weight, enc_bias, dec_weight, block_ids, block_home):
    rows, width = tokens.shape
    lat_count = lax.axis_size("lat")
    groups = lax.axis_size("tok")
    chips = groups // 2
    targets = 2 * lat_count
    part = width // CUTS
    slot_rows = targets * GROUP
    latents = enc_weight.shape[0] // 2
    per_cut = part // STEP
    me = lax.axis_index("tok").astype(I32)
    core = me % 2
    first_row = (me // 2 % 2) * latents
    scalars = jnp.stack([core, first_row])
    exchange_groups = [
        [(4 * p + 2 * b + c) * lat_count + at for b in range(2) for at in range(lat_count)]
        for p in range(groups // 4)
        for c in range(2)
    ]
    chunk_shape = jax.ShapeDtypeStruct((slot_rows, part), BF)
    lent_shape = jax.ShapeDtypeStruct((max(LENT) * PIECES, STEP), BF)
    matmul_cost = pl.CostEstimate(
        flops=5 * 2 * slot_rows * CUTS * latents * part,
        bytes_accessed=12 * 2**20,
        transcendentals=0,
    )
    move_cost = pl.CostEstimate(
        flops=2 * slot_rows * CUTS * rows * part, bytes_accessed=5 * 2**20, transcendentals=0
    )

    chunk1, lent_a, lent_b = pl.pallas_call(
        functools.partial(first_kernel, targets),
        out_shape=[chunk_shape, lent_shape, lent_shape],
        in_specs=[vmem()] * 3,
        out_specs=[vmem()] * 3,
        compiler_params=room(20),
        cost_estimate=move_cost,
        name="first_slots",
    )(block_ids.reshape(1, rows), block_home.reshape(1, -1), tokens)

    def exchange(chunk):
        shaped = chunk.reshape(targets, GROUP, part)
        got = lax.all_to_all(
            shaped,
            ("tok", "lat"),
            split_axis=0,
            concat_axis=0,
            tiled=True,
            axis_index_groups=exchange_groups,
        )
        return got.reshape(slot_rows, part)

    loans_a = lax.all_gather(lent_a, "tok", tiled=True)
    loans_a, lent_b = lax.optimization_barrier((loans_a, lent_b))
    loans_b = lax.all_gather(lent_b, "tok", tiled=True)
    got1 = exchange(chunk1)
    chunk2, left, flags = pl.pallas_call(
        functools.partial(second_kernel, targets),
        out_shape=[
            chunk_shape,
            jax.ShapeDtypeStruct((8, rows), I32),
            jax.ShapeDtypeStruct((8, rows), F32),
        ],
        in_specs=[smem()] + [vmem()] * 3,
        out_specs=[vmem()] * 3,
        compiler_params=room(24),
        cost_estimate=move_cost,
        name="second_slots",
    )(me.reshape(1), tokens, loans_a, loans_b)
    got2 = exchange(chunk2)
    line = 4
    along_x = [[i * line + j for j in range(line)] for i in range(lat_count // line)]
    along_z = [[i * line + j for i in range(lat_count // line)] for j in range(line)]
    for lines in (along_x, along_z):
        flags = lax.all_gather(flags, "lat", axis_index_groups=lines)
        flags = jnp.max(flags, axis=0)

    bias_row = lax.dynamic_slice_in_dim(enc_bias, first_row, latents).reshape(1, latents)
    offset_row = dec_bias.reshape(1, width)
    work = [
        pltpu.VMEM((slot_rows, part), BF),
        pltpu.VMEM((latents, width), BF),
        pltpu.VMEM((latents, width), BF),
        pltpu.VMEM((slot_rows, part), BF),
        pltpu.VMEM((slot_rows, part), BF),
        pltpu.VMEM((slot_rows, CUTS * latents), F32),
        pltpu.SemaphoreType.DMA((per_cut * (CUTS + 1) + 2,)),
    ]
    parts_shape = (per_cut, CUTS, 2 * latents, STEP)
    half_shape = (CUTS, 2 * latents, STEP)
    part_call = pl.pallas_call(
        part_kernel,
        out_shape=jax.ShapeDtypeStruct(parts_shape, F32),
        in_specs=[smem()] + [anywhere()] * 3 + [vmem()] * 2,
        out_specs=vmem(),
        scratch_shapes=work,
        compiler_params=room(56),
        cost_estimate=matmul_cost,
        name="chunk_gradients",
    )
    parts = part_call(scalars, got1, enc_weight, dec_weight, bias_row, offset_row)
    mine, other = pl.pallas_call(
        last_kernel,
        out_shape=[
            jax.ShapeDtypeStruct(half_shape, F32),
            jax.ShapeDtypeStruct(half_shape, BF),
        ],
        in_specs=[smem()] + [anywhere()] * 3 + [vmem()] * 2 + [anywhere()],
        out_specs=[anywhere()] * 2,
        scratch_shapes=[
            *work,
            pltpu.VMEM(parts_shape, F32),
            pltpu.VMEM(half_shape, F32),
            pltpu.VMEM(half_shape, BF),
            pltpu.SemaphoreType.DMA((4,)),
        ],
        compiler_params=room(56),
        cost_estimate=matmul_cost,
        name="last_gradients",
    )(scalars, got2, enc_weight, dec_weight, bias_row, offset_row, parts)

    def rest(carry):
        mine, other, unused = carry
        codes, cut = slot_codes(targets, DIRECT)
        hit = flat(codes == left[:1])
        data = jnp.zeros((slot_rows, part), F32)
        for h in range(CUTS):
            chosen = jnp.where(cut == h, hit, 0.0).astype(BF)
            data = data + mm(chosen, tokens[:, h * part : (h + 1) * part])
        filled = jnp.sum(hit, axis=1, keepdims=True) > 0.5
        chunk3 = jnp.where(filled, data, EMPTY).astype(BF)
        more = part_call(scalars, exchange(chunk3), enc_weight, dec_weight, bias_row, offset_row)
        mine = mine + lax.dynamic_index_in_dim(more, core, 0, keepdims=False)
        more = lax.dynamic_index_in_dim(more, 1 - core, 0, keepdims=False)
        return mine, (other.astype(F32) + more).astype(BF), jnp.zeros((), F32)

    mine, other, unused = lax.while_loop(
        lambda carry: carry[2] > 0.5, rest, (mine, other, flags[0, 0])
    )
    swapped = lax.ppermute(other, "tok", [(i, i ^ 1) for i in range(groups)])
    summed = (mine + swapped.astype(F32)).astype(BF)
    terms = lax.all_to_all(
        summed,
        "tok",
        split_axis=0,
        concat_axis=0,
        tiled=True,
        axis_index_groups=[[2 * i + c for i in range(chips)] for c in range(2)],
    )
    total = jnp.sum(terms.astype(F32).reshape(chips // 2, 2, 2, latents, STEP), axis=0)
    return total[:, 0].reshape(2 * latents, STEP), total[:, 1].reshape(2 * latents, STEP)


def solution(mesh):
    in_specs = (
        P(("tok", "lat"), None),
        P(),
        P("lat", None),
        P("lat"),
        P("lat", None),
        P(("tok", "lat"), None),
        P(),
    )
    out_specs = (P("lat", "tok"), P("lat", "tok"))
    return jax.shard_map(
        on_device, mesh=mesh, in_specs=in_specs, out_specs=out_specs, check_vma=False
    )
```

```python
import functools

import jax
import jax.numpy as jnp
from jax import lax
from jax.experimental import pallas as pl
from jax.experimental.pallas import tpu as pltpu
from jax.sharding import PartitionSpec as P

BF = jnp.bfloat16
F32 = jnp.float32
I32 = jnp.int32

CUTS = 4
SLOTS = 2
DIRECT = 2 * SLOTS
GROUP = CUTS * SLOTS
STRIDE = 8
EMPTY = 2.0**100
EXTRA = 128
STEP = 1024
PIECES = 8
LENT = (6, 7)


def room(mib):
    return pltpu.CompilerParams(vmem_limit_bytes=mib * 2**20)


def mm(a, b):
    return jnp.dot(a, b, preferred_element_type=F32)


def mm_t(a, b):
    return lax.dot_general(a, b, (((1,), (1,)), ((), ())), preferred_element_type=F32)


def iota(shape, axis):
    return lax.broadcasted_iota(I32, shape, axis)


def flat(mask):
    return jnp.where(mask, 1.0, 0.0)


def slot_codes(targets, first):
    row = iota((targets * GROUP, 1), 0)
    inner = row % GROUP
    return (row // GROUP) * STRIDE + first + inner % SLOTS, inner // SLOTS


def before(n):
    return (iota((n, n), 0) < iota((n, n), 1)).astype(F32).astype(BF)


def ranks_of(target, targets):
    g, n = target.shape
    members = flat(target[:, None, :] == iota((g, targets, n), 1))
    counts = mm(members.reshape(g * targets, n).astype(BF), before(n)).reshape(g, targets, n)
    return members, jnp.sum(members * counts, axis=1)


def target_of(places, targets):
    return (places & 1) * (targets // 2) + (places >> 1)


def cut_columns(ref, i):
    part = ref.shape[1] // CUTS
    return [ref[:, h * part + i * STEP : h * part + (i + 1) * STEP] for h in range(CUTS)]


def places_of(ids, home):
    total = home.shape[1]
    named = flat(iota((total, ids.shape[1]), 0) == ids[...]).astype(BF)
    table = jnp.broadcast_to(home[...], (8, total)).astype(F32).astype(BF)
    return mm(table, named)[:1].astype(I32)


def first_kernel(targets, ids, home, tokens_in, chunk_out, tokens, chunk, sems_in, sems_out):
    rows, width = tokens.shape
    part = width // CUTS
    steps = part // STEP
    loads = []
    for i in range(steps):
        for h in range(CUTS):
            columns = pl.ds(h * part + i * STEP, STEP)
            sem = sems_in.at[len(loads)]
            loads.append(pltpu.make_async_copy(tokens_in.at[:, columns], tokens.at[:, columns], sem))
            loads[-1].start()
    target = target_of(places_of(ids, home), targets)
    unused, rank = ranks_of(target, targets)
    codes, cut = slot_codes(targets, 0)
    hit = flat(codes == target * STRIDE + rank.astype(I32))
    wide = jnp.concatenate([jnp.where(cut == h, hit, 0.0) for h in range(CUTS)], axis=1)
    wide = wide.astype(BF)
    filled = jnp.sum(hit, axis=1, keepdims=True) > 0.5
    stores = []
    for i in range(steps):
        for h in range(CUTS):
            loads[i * CUTS + h].wait()
        got = mm(wide, jnp.concatenate(cut_columns(tokens, i), axis=0))
        chunk[:, i * STEP : (i + 1) * STEP] = jnp.where(filled, got, EMPTY).astype(BF)
        columns = pl.ds(i * STEP, STEP)
        stores.append(
            pltpu.make_async_copy(chunk.at[:, columns], chunk_out.at[:, columns], sems_out.at[i])
        )
        stores[-1].start()
    for store in stores:
        store.wait()


def lend_kernel(targets, ids, home, tokens, lent_a, lent_b):
    rows = tokens.shape[0]
    places = places_of(ids, home)
    unused, rank = ranks_of(target_of(places, targets), targets)
    over = flat(rank.astype(I32) >= DIRECT)
    order = mm(jnp.broadcast_to(over, (8, rows)).astype(BF), before(rows))[:1].astype(I32)
    first = 0
    for count, lent in zip(LENT, (lent_a, lent_b)):
        lines = lent.shape[0]
        line = iota((lines, rows), 0)
        take = jnp.logical_and(order == first + line // PIECES, over > 0.5)
        take = flat(jnp.logical_and(take, line < count * PIECES))
        piece = iota((lines, 1), 0) % PIECES
        got = jnp.zeros((lines, STEP), F32)
        for i in range(PIECES):
            chosen = jnp.where(piece == i, take, 0.0).astype(BF)
            got = got + mm(chosen, tokens[:, i * STEP : (i + 1) * STEP])
        if first == 0:
            head = jnp.where(line == count * PIECES, places.astype(F32), got[:, :rows])
            got = jnp.concatenate([head, got[:, rows:]], axis=1)
        lent[...] = got.astype(BF)
        first += count


def second_kernel(targets, group, tokens, loans_a, loans_b, chunk, left):
    rows, width = tokens.shape
    part = width // CUTS
    lines = (LENT[0] + 1) * PIECES
    groups = loans_a.shape[0] // lines
    me = group[0]
    heads = loans_a[:, :rows].astype(F32).reshape(groups, lines, rows)
    places = heads[:, LENT[0] * PIECES, :].astype(I32)
    target = target_of(places, targets)
    members, rank_f = ranks_of(target, targets)
    rank = rank_f.astype(I32)
    over = rank >= DIRECT
    order = mm(flat(over).astype(BF), before(rows)).astype(I32)
    listed = jnp.logical_and(over, order < sum(LENT))
    count = jnp.sum(members, axis=2, keepdims=True)
    asked = jnp.sum(members * flat(listed)[:, None, :], axis=2, keepdims=True)
    used = jnp.maximum(count, float(SLOTS))
    free = jnp.maximum(DIRECT - used, 0.0)
    asked_before = []
    running = jnp.zeros((1, targets, 1), F32)
    free_total = jnp.zeros((1, targets, 1), F32)
    free_before = jnp.zeros((1, targets, 1), F32)
    for t in range(groups):
        asked_before.append(running)
        running = running + asked[t : t + 1]
        free_before = free_before + jnp.where(me > t, free[t : t + 1], 0.0)
        free_total = free_total + free[t : t + 1]
    mine = flat(iota((groups, 1, 1), 0) == me)
    my_free = jnp.sum(free * mine, axis=0, keepdims=True)
    my_used = jnp.sum(used * mine, axis=0, keepdims=True)

    def look(values):
        return jnp.sum(members * values, axis=1).astype(I32)

    in_pool = look(jnp.concatenate(asked_before, axis=0)) + rank - DIRECT
    placed = jnp.logical_and(listed, in_pool < look(free_total))
    at = in_pool - look(free_before)
    here = jnp.logical_and(placed, jnp.logical_and(at >= 0, at < look(my_free)))
    lent_code = jnp.where(here, target * STRIDE + look(my_used) + at, -1)
    size = groups * lines
    square = iota((size, size), 0) == iota((size, size), 1)
    line_of = iota((lines, rows), 0) // PIECES

    def codes_of_lines(first, count):
        columns = []
        for t in range(groups):
            chosen = jnp.logical_and(order[t : t + 1] == first + line_of, listed[t : t + 1])
            chosen = jnp.logical_and(chosen, line_of < count)
            value = jnp.where(chosen, lent_code[t : t + 1] + 1, 0)
            columns.append(jnp.sum(value, axis=1, keepdims=True) - 1)
        column = jnp.concatenate(columns, axis=0)
        return jnp.sum(jnp.where(square, column, 0), axis=0, keepdims=True)

    mine2 = (iota((groups, 1), 0) == me).astype(I32)
    own_code = jnp.sum((target * STRIDE + rank) * mine2, axis=0, keepdims=True)
    missing = jnp.logical_and(over, jnp.logical_not(placed)).astype(I32)
    own_missing = jnp.sum(missing * mine2, axis=0, keepdims=True)
    left[...] = jnp.broadcast_to(jnp.where(own_missing > 0, own_code, -1), left.shape)
    flag = jnp.max(jnp.max(missing.astype(F32), axis=1, keepdims=True), axis=0, keepdims=True)
    codes, cut = slot_codes(targets, SLOTS)
    hit = flat(codes == own_code)
    wide = jnp.concatenate([jnp.where(cut == h, hit, 0.0) for h in range(CUTS)], axis=1)
    wide = wide.astype(BF)
    hit_a = flat(codes == codes_of_lines(0, LENT[0]))
    hit_b = flat(codes == codes_of_lines(LENT[0], LENT[1]))
    filled = jnp.sum(hit, axis=1, keepdims=True) + jnp.sum(hit_a, axis=1, keepdims=True)
    filled = filled + jnp.sum(hit_b, axis=1, keepdims=True) > 0.5
    chunk[:, part:] = jnp.broadcast_to(flag, (hit.shape[0], EXTRA)).astype(BF)
    per_cut = part // STEP
    piece = iota((1, size), 1) % PIECES
    for i in range(per_cut):
        at_cut = cut * per_cut + i == piece
        got = mm(wide, jnp.concatenate(cut_columns(tokens, i), axis=0))
        got = got + mm(jnp.where(at_cut, hit_a, 0.0).astype(BF), loans_a[...])
        got = got + mm(jnp.where(at_cut, hit_b, 0.0).astype(BF), loans_b[...])
        chunk[:, i * STEP : (i + 1) * STEP] = jnp.where(filled, got, EMPTY).astype(BF)


def gradient_body(chunk, enc, dec, bias, dec_bias, cent, err, acc, store, ready):
    rows, part = chunk.shape
    latents = enc.shape[0]
    steps = part // STEP
    inner = iota((rows, 1), 0) % GROUP
    cut = inner // SLOTS
    cut8 = iota((GROUP, 1), 0) // SLOTS

    def here(i):
        return slice(i * STEP, (i + 1) * STEP)

    def offset(i):
        value = jnp.zeros((GROUP, STEP), F32)
        for h, columns in enumerate(cut_columns(dec_bias, i)):
            value = jnp.where(cut8 == h, columns, value)
        return value[None]

    def joined(total):
        own = total[:, :latents]
        for h in range(1, CUTS):
            own = jnp.where(cut == h, total[:, h * latents : (h + 1) * latents], own)
        shift = GROUP // 2
        while shift >= SLOTS:
            down = pltpu.roll(own, rows - shift, 0)
            wrapped = pltpu.roll(own, GROUP - shift, 0)
            own = own + jnp.where(inner < GROUP - shift, down, wrapped)
            shift //= 2
        return own

    def spread(values):
        return jnp.concatenate([jnp.where(cut == h, values, 0.0) for h in range(CUTS)], axis=1)

    for i in range(steps):
        ready("first", i)
        x = chunk[:, here(i)].astype(F32).reshape(rows // GROUP, GROUP, STEP)
        c = (x - offset(i)).reshape(rows, STEP).astype(BF)
        cent[:, here(i)] = c
        w = jnp.concatenate(cut_columns(enc, i), axis=0)
        if i == 0:
            acc[...] = mm_t(c, w)
        else:
            acc[...] += mm_t(c, w)
    valid = chunk[:, :latents].astype(F32) < EMPTY / 2
    pre = joined(acc[...]) + bias[...]
    gate = 1.0 / (1.0 + jnp.exp(-pre))
    latent = spread(jnp.where(valid, pre * gate, 0.0))
    latent_b = latent.astype(BF)
    ready("second", 0)
    for i in range(steps):
        w = jnp.concatenate(cut_columns(dec, i), axis=0)
        d = mm(latent_b, w).astype(BF).astype(F32).reshape(rows // GROUP, GROUP, STEP)
        x = chunk[:, here(i)].astype(F32).reshape(rows // GROUP, GROUP, STEP)
        e = ((offset(i) + d - x) * (1.0 / 32.0)).reshape(rows, STEP).astype(BF)
        err[:, here(i)] = e
        if i == 0:
            acc[...] = mm_t(e, w)
        else:
            acc[...] += mm_t(e, w)
    dlatent = joined(acc[...])
    dpre = spread(jnp.where(valid, dlatent * gate * (1.0 + pre * (1.0 - gate)), 0.0))
    dpre_t = dpre.T.astype(BF)
    latent_t = latent.T.astype(BF)
    ready("third", 0)
    for i in range(steps):
        store(i, 0, mm(dpre_t, cent[:, here(i)]))
        store(i, 1, mm(latent_t, err[:, here(i)]))


class Loader:
    def __init__(self, sems, first_row, chunk_in, enc_in, dec_in, chunk, enc, dec):
        self.sems = sems
        self.moves = {}
        part = chunk.shape[1]
        latents = enc.shape[0]
        rows = pl.ds(pl.multiple_of(first_row, latents), latents)
        for i in range(part // STEP):
            here = pl.ds(i * STEP, STEP)
            self.move(("chunk", i), chunk_in.at[:, here], chunk.at[:, here])
            for h in range(CUTS):
                columns = pl.ds(h * part + i * STEP, STEP)
                self.move(("enc", i, h), enc_in.at[rows, columns], enc.at[:, columns])
        self.move("second", dec_in.at[rows], dec)

    def move(self, key, source, target):
        self.moves[key] = pltpu.make_async_copy(source, target, self.sems.at[len(self.moves)])
        self.moves[key].start()

    def __call__(self, stage, i):
        if stage == "first":
            self.moves[("chunk", i)].wait()
            for h in range(CUTS):
                self.moves[("enc", i, h)].wait()
        elif stage in self.moves:
            self.moves[stage].wait()


def part_kernel(
    at, chunk_in, enc_in, dec_in, bias, dec_bias, parts, chunk, enc, dec, cent, err, acc, sems
):
    latents = enc.shape[0]
    ready = Loader(sems, at[1], chunk_in, enc_in, dec_in, chunk, enc, dec)

    def store(i, grad, value):
        rows = slice(grad * latents, (grad + 1) * latents)
        for h in range(CUTS):
            parts[i, h, rows] = value[h * latents : (h + 1) * latents]

    gradient_body(chunk, enc, dec, bias, dec_bias, cent, err, acc, store, ready)


def last_kernel(
    at,
    chunk_in,
    enc_in,
    dec_in,
    bias,
    dec_bias,
    parts_in,
    mine_out,
    other_out,
    flags,
    chunk,
    enc,
    dec,
    cent,
    err,
    acc,
    sems,
    parts,
    mine,
    other,
    marks,
    sems_out,
):
    latents = enc.shape[0]
    core = at[0]
    ready = Loader(sems, at[1], chunk_in, enc_in, dec_in, chunk, enc, dec)
    ready.move("third", parts_in, parts)
    ready.move("marks", chunk_in.at[:, pl.ds(chunk.shape[1], EXTRA)], marks)

    def out_copy(which, grad):
        source, result = ((mine, mine_out), (other, other_out))[which]
        rows = pl.ds(grad * latents, latents)
        sem = sems_out.at[2 * which + grad]
        return pltpu.make_async_copy(source.at[:, rows], result.at[:, rows], sem)

    def store(i, grad, value):
        rows = slice(grad * latents, (grad + 1) * latents)
        totals = [
            value[h * latents : (h + 1) * latents] + parts[i, h, rows] for h in range(CUTS)
        ]

        @pl.when(core == i)
        def _():
            for h in range(CUTS):
                mine[h, rows] = totals[h]
            out_copy(0, grad).start()

        @pl.when(core != i)
        def _():
            for h in range(CUTS):
                other[h, rows] = totals[h].astype(BF)
            out_copy(1, grad).start()

    gradient_body(chunk, enc, dec, bias, dec_bias, cent, err, acc, store, ready)
    ready("marks", 0)
    flags[0] = jnp.max(marks[...].astype(F32))
    for which in range(2):
        for grad in range(2):
            out_copy(which, grad).wait()


def vmem():
    return pl.BlockSpec(memory_space=pltpu.VMEM)


def anywhere():
    return pl.BlockSpec(memory_space=pl.ANY)


def smem():
    return pl.BlockSpec(memory_space=pltpu.SMEM)


def on_device(tokens, dec_bias, enc_weight, enc_bias, dec_weight, block_ids, block_home):
    rows, width = tokens.shape
    lat_count = lax.axis_size("lat")
    groups = lax.axis_size("tok")
    chips = groups // 2
    targets = 2 * lat_count
    part = width // CUTS
    slot_rows = targets * GROUP
    latents = enc_weight.shape[0] // 2
    per_cut = part // STEP
    me = lax.axis_index("tok").astype(I32)
    core = me % 2
    first_row = (me // 2 % 2) * latents
    scalars = jnp.stack([core, first_row])
    exchange_groups = [
        [(4 * p + 2 * b + c) * lat_count + at for b in range(2) for at in range(lat_count)]
        for p in range(groups // 4)
        for c in range(2)
    ]
    chunk_shape = jax.ShapeDtypeStruct((slot_rows, part), BF)
    lent_shape = jax.ShapeDtypeStruct((max(LENT) * PIECES, STEP), BF)
    matmul_cost = pl.CostEstimate(
        flops=5 * 2 * slot_rows * CUTS * latents * part,
        bytes_accessed=12 * 2**20,
        transcendentals=0,
    )
    move_cost = pl.CostEstimate(
        flops=2 * slot_rows * CUTS * rows * part, bytes_accessed=5 * 2**20, transcendentals=0
    )

    ids_row = block_ids.reshape(1, rows)
    home_row = block_home.reshape(1, -1)
    chunk1 = pl.pallas_call(
        functools.partial(first_kernel, targets),
        out_shape=chunk_shape,
        in_specs=[vmem()] * 2 + [anywhere()],
        out_specs=anywhere(),
        scratch_shapes=[
            pltpu.VMEM((rows, width), BF),
            pltpu.VMEM((slot_rows, part), BF),
            pltpu.SemaphoreType.DMA((CUTS * per_cut,)),
            pltpu.SemaphoreType.DMA((per_cut,)),
        ],
        compiler_params=room(56),
        cost_estimate=move_cost,
        name="first_slots",
    )(ids_row, home_row, tokens)
    lent_a, lent_b = pl.pallas_call(
        functools.partial(lend_kernel, targets),
        out_shape=[lent_shape, lent_shape],
        in_specs=[vmem()] * 3,
        out_specs=[vmem()] * 2,
        compiler_params=room(20),
        cost_estimate=move_cost,
        name="lent_rows",
    )(ids_row, home_row, tokens)

    def exchange(chunk):
        shaped = chunk.reshape(targets, GROUP, chunk.shape[1])
        got = lax.all_to_all(
            shaped,
            ("tok", "lat"),
            split_axis=0,
            concat_axis=0,
            tiled=True,
            axis_index_groups=exchange_groups,
        )
        return got.reshape(chunk.shape)

    loans_a = lax.all_gather(lent_a, "tok", tiled=True)
    loans_a, lent_b = lax.optimization_barrier((loans_a, lent_b))
    loans_b = lax.all_gather(lent_b, "tok", tiled=True)
    got1 = exchange(chunk1)
    chunk2, left = pl.pallas_call(
        functools.partial(second_kernel, targets),
        out_shape=[
            jax.ShapeDtypeStruct((slot_rows, part + EXTRA), BF),
            jax.ShapeDtypeStruct((8, rows), I32),
        ],
        in_specs=[smem()] + [vmem()] * 3,
        out_specs=[vmem()] * 2,
        compiler_params=room(24),
        cost_estimate=move_cost,
        name="second_slots",
    )(me.reshape(1), tokens, loans_a, loans_b)
    got2 = exchange(chunk2)
    bias_row = lax.dynamic_slice_in_dim(enc_bias, first_row, latents).reshape(1, latents)
    offset_row = dec_bias.reshape(1, width)
    work = [
        pltpu.VMEM((slot_rows, part), BF),
        pltpu.VMEM((latents, width), BF),
        pltpu.VMEM((latents, width), BF),
        pltpu.VMEM((slot_rows, part), BF),
        pltpu.VMEM((slot_rows, part), BF),
        pltpu.VMEM((slot_rows, CUTS * latents), F32),
        pltpu.SemaphoreType.DMA((per_cut * (CUTS + 1) + 3,)),
    ]
    parts_shape = (per_cut, CUTS, 2 * latents, STEP)
    half_shape = (CUTS, 2 * latents, STEP)
    part_call = pl.pallas_call(
        part_kernel,
        out_shape=jax.ShapeDtypeStruct(parts_shape, F32),
        in_specs=[smem()] + [anywhere()] * 3 + [vmem()] * 2,
        out_specs=vmem(),
        scratch_shapes=work,
        compiler_params=room(56),
        cost_estimate=matmul_cost,
        name="chunk_gradients",
    )
    parts = part_call(scalars, got1, enc_weight, dec_weight, bias_row, offset_row)
    mine, other, flags = pl.pallas_call(
        last_kernel,
        out_shape=[
            jax.ShapeDtypeStruct(half_shape, F32),
            jax.ShapeDtypeStruct(half_shape, BF),
            jax.ShapeDtypeStruct((1,), F32),
        ],
        in_specs=[smem()] + [anywhere()] * 3 + [vmem()] * 2 + [anywhere()],
        out_specs=[anywhere()] * 2 + [smem()],
        scratch_shapes=[
            *work,
            pltpu.VMEM(parts_shape, F32),
            pltpu.VMEM(half_shape, F32),
            pltpu.VMEM(half_shape, BF),
            pltpu.VMEM((slot_rows, EXTRA), BF),
            pltpu.SemaphoreType.DMA((4,)),
        ],
        compiler_params=room(56),
        cost_estimate=matmul_cost,
        name="last_gradients",
    )(scalars, got2, enc_weight, dec_weight, bias_row, offset_row, parts)

    def rest(carry):
        mine, other, unused = carry
        codes, cut = slot_codes(targets, DIRECT)
        hit = flat(codes == left[:1])
        data = jnp.zeros((slot_rows, part), F32)
        for h in range(CUTS):
            chosen = jnp.where(cut == h, hit, 0.0).astype(BF)
            data = data + mm(chosen, tokens[:, h * part : (h + 1) * part])
        filled = jnp.sum(hit, axis=1, keepdims=True) > 0.5
        chunk3 = jnp.where(filled, data, EMPTY).astype(BF)
        more = part_call(scalars, exchange(chunk3), enc_weight, dec_weight, bias_row, offset_row)
        mine = mine + lax.dynamic_index_in_dim(more, core, 0, keepdims=False)
        more = lax.dynamic_index_in_dim(more, 1 - core, 0, keepdims=False)
        return mine, (other.astype(F32) + more).astype(BF), jnp.zeros((), F32)

    mine, other, unused = lax.while_loop(
        lambda carry: carry[2] > 0.5, rest, (mine, other, flags.reshape(()))
    )
    swapped = lax.ppermute(other, "tok", [(i, i ^ 1) for i in range(groups)])
    summed = (mine + swapped.astype(F32)).astype(BF)
    terms = lax.all_to_all(
        summed,
        "tok",
        split_axis=0,
        concat_axis=0,
        tiled=True,
        axis_index_groups=[[2 * i + c for i in range(chips)] for c in range(2)],
    )
    total = jnp.sum(terms.astype(F32).reshape(chips // 2, 2, 2, latents, STEP), axis=0)
    return total[:, 0].reshape(2 * latents, STEP), total[:, 1].reshape(2 * latents, STEP)


def solution(mesh):
    in_specs = (
        P(("tok", "lat"), None),
        P(),
        P("lat", None),
        P("lat"),
        P("lat", None),
        P(("tok", "lat"), None),
        P(),
    )
    out_specs = (P("lat", "tok"), P("lat", "tok"))
    return jax.shard_map(
        on_device, mesh=mesh, in_specs=in_specs, out_specs=out_specs, check_vma=False
    )
```

```python
import functools

import jax
import jax.numpy as jnp
from jax import lax
from jax.experimental import pallas as pl
from jax.experimental.pallas import tpu as pltpu
from jax.sharding import PartitionSpec as P

BF = jnp.bfloat16
F32 = jnp.float32
I32 = jnp.int32

CUTS = 4
SLOTS = 2
DIRECT = 2 * SLOTS
GROUP = CUTS * SLOTS
STRIDE = 8
EMPTY = 2.0**100
EXTRA = 128
STEP = 1024
PIECES = 8
LENT = (6, 7)


def room(mib):
    return pltpu.CompilerParams(vmem_limit_bytes=mib * 2**20)


def mm(a, b):
    return jnp.dot(a, b, preferred_element_type=F32)


def mm_t(a, b):
    return lax.dot_general(a, b, (((1,), (1,)), ((), ())), preferred_element_type=F32)


def iota(shape, axis):
    return lax.broadcasted_iota(I32, shape, axis)


def flat(mask):
    return jnp.where(mask, 1.0, 0.0)


def slot_codes(targets, first):
    row = iota((targets * GROUP, 1), 0)
    inner = row % GROUP
    return (row // GROUP) * STRIDE + first + inner % SLOTS, inner // SLOTS


def before(n):
    return (iota((n, n), 0) < iota((n, n), 1)).astype(F32).astype(BF)


def ranks_of(target, targets):
    g, n = target.shape
    members = flat(target[:, None, :] == iota((g, targets, n), 1))
    counts = mm(members.reshape(g * targets, n).astype(BF), before(n)).reshape(g, targets, n)
    return members, jnp.sum(members * counts, axis=1)


def target_of(places, targets):
    return (places & 1) * (targets // 2) + (places >> 1)


def cut_columns(ref, i):
    part = ref.shape[1] // CUTS
    return [ref[:, h * part + i * STEP : h * part + (i + 1) * STEP] for h in range(CUTS)]


def places_of(ids, home):
    total = home.shape[1]
    named = flat(iota((total, ids.shape[1]), 0) == ids[...]).astype(BF)
    table = jnp.broadcast_to(home[...], (8, total)).astype(F32).astype(BF)
    return mm(table, named)[:1].astype(I32)


def first_kernel(targets, ids, home, tokens_in, chunk_out, tokens, chunk, sems_in, sems_out):
    rows, width = tokens.shape
    part = width // CUTS
    steps = part // STEP
    loads = []
    for i in range(steps):
        for h in range(CUTS):
            columns = pl.ds(h * part + i * STEP, STEP)
            sem = sems_in.at[len(loads)]
            loads.append(pltpu.make_async_copy(tokens_in.at[:, columns], tokens.at[:, columns], sem))
            loads[-1].start()
    target = target_of(places_of(ids, home), targets)
    unused, rank = ranks_of(target, targets)
    codes, cut = slot_codes(targets, 0)
    hit = flat(codes == target * STRIDE + rank.astype(I32))
    wide = jnp.concatenate([jnp.where(cut == h, hit, 0.0) for h in range(CUTS)], axis=1)
    wide = wide.astype(BF)
    filled = jnp.sum(hit, axis=1, keepdims=True) > 0.5
    stores = []
    for i in range(steps):
        for h in range(CUTS):
            loads[i * CUTS + h].wait()
        got = mm(wide, jnp.concatenate(cut_columns(tokens, i), axis=0))
        chunk[:, i * STEP : (i + 1) * STEP] = jnp.where(filled, got, EMPTY).astype(BF)
        columns = pl.ds(i * STEP, STEP)
        stores.append(
            pltpu.make_async_copy(chunk.at[:, columns], chunk_out.at[:, columns], sems_out.at[i])
        )
        stores[-1].start()
    for store in stores:
        store.wait()


def lend_kernel(targets, ids, home, tokens, lent_a, lent_b):
    rows = tokens.shape[0]
    places = places_of(ids, home)
    unused, rank = ranks_of(target_of(places, targets), targets)
    over = flat(rank.astype(I32) >= DIRECT)
    order = mm(jnp.broadcast_to(over, (8, rows)).astype(BF), before(rows))[:1].astype(I32)
    first = 0
    for count, lent in zip(LENT, (lent_a, lent_b)):
        lines = lent.shape[0]
        line = iota((lines, rows), 0)
        take = jnp.logical_and(order == first + line // PIECES, over > 0.5)
        take = flat(jnp.logical_and(take, line < count * PIECES))
        piece = iota((lines, 1), 0) % PIECES
        got = jnp.zeros((lines, STEP), F32)
        for i in range(PIECES):
            chosen = jnp.where(piece == i, take, 0.0).astype(BF)
            got = got + mm(chosen, tokens[:, i * STEP : (i + 1) * STEP])
        if first == 0:
            head = jnp.where(line == count * PIECES, places.astype(F32), got[:, :rows])
            got = jnp.concatenate([head, got[:, rows:]], axis=1)
        lent[...] = got.astype(BF)
        first += count


def second_kernel(targets, group, tokens, loans_a, loans_b, chunk, left):
    rows, width = tokens.shape
    part = width // CUTS
    lines = (LENT[0] + 1) * PIECES
    groups = loans_a.shape[0] // lines
    me = group[0]
    heads = loans_a[:, :rows].astype(F32).reshape(groups, lines, rows)
    places = heads[:, LENT[0] * PIECES, :].astype(I32)
    target = target_of(places, targets)
    members, rank_f = ranks_of(target, targets)
    rank = rank_f.astype(I32)
    over = rank >= DIRECT
    order = mm(flat(over).astype(BF), before(rows)).astype(I32)
    listed = jnp.logical_and(over, order < sum(LENT))
    count = jnp.sum(members, axis=2, keepdims=True)
    asked = jnp.sum(members * flat(listed)[:, None, :], axis=2, keepdims=True)
    used = jnp.maximum(count, float(SLOTS))
    free = jnp.maximum(DIRECT - used, 0.0)
    asked_before = []
    running = jnp.zeros((1, targets, 1), F32)
    free_total = jnp.zeros((1, targets, 1), F32)
    free_before = jnp.zeros((1, targets, 1), F32)
    for t in range(groups):
        asked_before.append(running)
        running = running + asked[t : t + 1]
        free_before = free_before + jnp.where(me > t, free[t : t + 1], 0.0)
        free_total = free_total + free[t : t + 1]
    mine = flat(iota((groups, 1, 1), 0) == me)
    my_free = jnp.sum(free * mine, axis=0, keepdims=True)
    my_used = jnp.sum(used * mine, axis=0, keepdims=True)

    def look(values):
        return jnp.sum(members * values, axis=1).astype(I32)

    in_pool = look(jnp.concatenate(asked_before, axis=0)) + rank - DIRECT
    placed = jnp.logical_and(listed, in_pool < look(free_total))
    at = in_pool - look(free_before)
    here = jnp.logical_and(placed, jnp.logical_and(at >= 0, at < look(my_free)))
    lent_code = jnp.where(here, target * STRIDE + look(my_used) + at, -1)
    size = groups * lines
    square = iota((size, size), 0) == iota((size, size), 1)
    line_of = iota((lines, rows), 0) // PIECES

    def codes_of_lines(first, count):
        columns = []
        for t in range(groups):
            chosen = jnp.logical_and(order[t : t + 1] == first + line_of, listed[t : t + 1])
            chosen = jnp.logical_and(chosen, line_of < count)
            value = jnp.where(chosen, lent_code[t : t + 1] + 1, 0)
            columns.append(jnp.sum(value, axis=1, keepdims=True) - 1)
        column = jnp.concatenate(columns, axis=0)
        return jnp.sum(jnp.where(square, column, 0), axis=0, keepdims=True)

    mine2 = (iota((groups, 1), 0) == me).astype(I32)
    own_code = jnp.sum((target * STRIDE + rank) * mine2, axis=0, keepdims=True)
    missing = jnp.logical_and(over, jnp.logical_not(placed)).astype(I32)
    own_missing = jnp.sum(missing * mine2, axis=0, keepdims=True)
    left[...] = jnp.broadcast_to(jnp.where(own_missing > 0, own_code, -1), left.shape)
    flag = jnp.max(jnp.max(missing.astype(F32), axis=1, keepdims=True), axis=0, keepdims=True)
    codes, cut = slot_codes(targets, SLOTS)
    hit = flat(codes == own_code)
    wide = jnp.concatenate([jnp.where(cut == h, hit, 0.0) for h in range(CUTS)], axis=1)
    wide = wide.astype(BF)
    hit_a = flat(codes == codes_of_lines(0, LENT[0]))
    hit_b = flat(codes == codes_of_lines(LENT[0], LENT[1]))
    filled = jnp.sum(hit, axis=1, keepdims=True) + jnp.sum(hit_a, axis=1, keepdims=True)
    filled = filled + jnp.sum(hit_b, axis=1, keepdims=True) > 0.5
    chunk[:, part:] = jnp.broadcast_to(flag, (hit.shape[0], EXTRA)).astype(BF)
    per_cut = part // STEP
    piece = iota((1, size), 1) % PIECES
    for i in range(per_cut):
        at_cut = cut * per_cut + i == piece
        got = mm(wide, jnp.concatenate(cut_columns(tokens, i), axis=0))
        got = got + mm(jnp.where(at_cut, hit_a, 0.0).astype(BF), loans_a[...])
        got = got + mm(jnp.where(at_cut, hit_b, 0.0).astype(BF), loans_b[...])
        chunk[:, i * STEP : (i + 1) * STEP] = jnp.where(filled, got, EMPTY).astype(BF)


def gradient_body(chunk, enc, dec, bias, dec_bias, cent, err, acc, store, ready):
    rows, part = chunk.shape
    latents = enc.shape[0]
    steps = part // STEP
    inner = iota((1, rows), 1) % GROUP
    cut = inner // SLOTS
    cut8 = iota((GROUP, 1), 0) // SLOTS

    def here(i):
        return slice(i * STEP, (i + 1) * STEP)

    def offset(i):
        value = jnp.zeros((GROUP, STEP), F32)
        for h, columns in enumerate(cut_columns(dec_bias, i)):
            value = jnp.where(cut8 == h, columns, value)
        return value[None]

    def joined(total):
        own = total[:latents]
        for h in range(1, CUTS):
            own = jnp.where(cut == h, total[h * latents : (h + 1) * latents], own)
        shift = GROUP // 2
        while shift >= SLOTS:
            down = pltpu.roll(own, rows - shift, 1)
            wrapped = pltpu.roll(own, GROUP - shift, 1)
            own = own + jnp.where(inner < GROUP - shift, down, wrapped)
            shift //= 2
        return own

    def spread(values):
        return jnp.concatenate([jnp.where(cut == h, values, 0.0) for h in range(CUTS)], axis=0)

    for i in range(steps):
        ready("first", i)
        x = chunk[:, here(i)].astype(F32).reshape(rows // GROUP, GROUP, STEP)
        c = (x - offset(i)).reshape(rows, STEP).astype(BF)
        cent[:, here(i)] = c
        w = jnp.concatenate(cut_columns(enc, i), axis=0)
        if i == 0:
            acc[...] = mm_t(w, c)
        else:
            acc[...] += mm_t(w, c)
    filled = flat(chunk[:, :128].astype(F32) < EMPTY / 2).astype(BF)
    valid = mm_t(flat(iota((8, 128), 1) == 0).astype(BF), filled)[:1] > 0.5
    pre = joined(acc[...]) + bias[...]
    gate = 1.0 / (1.0 + jnp.exp(-pre))
    latent = spread(jnp.where(valid, pre * gate, 0.0))
    latent_t = latent.astype(BF)
    latent_b = latent.T.astype(BF)
    ready("second", 0)
    for i in range(steps):
        w = jnp.concatenate(cut_columns(dec, i), axis=0)
        d = mm(latent_b, w).astype(BF).astype(F32).reshape(rows // GROUP, GROUP, STEP)
        x = chunk[:, here(i)].astype(F32).reshape(rows // GROUP, GROUP, STEP)
        e = ((offset(i) + d - x) * (1.0 / 32.0)).reshape(rows, STEP).astype(BF)
        err[:, here(i)] = e
        if i == 0:
            acc[...] = mm_t(w, e)
        else:
            acc[...] += mm_t(w, e)
    dlatent = joined(acc[...])
    dpre = spread(jnp.where(valid, dlatent * gate * (1.0 + pre * (1.0 - gate)), 0.0))
    dpre_t = dpre.astype(BF)
    ready("third", 0)
    for i in range(steps):
        store(i, 0, mm(dpre_t, cent[:, here(i)]))
        store(i, 1, mm(latent_t, err[:, here(i)]))


class Loader:
    def __init__(self, sems, first_row, chunk_in, enc_in, dec_in, chunk, enc, dec):
        self.sems = sems
        self.moves = {}
        part = chunk.shape[1]
        latents = enc.shape[0]
        rows = pl.ds(pl.multiple_of(first_row, latents), latents)
        for i in range(part // STEP):
            here = pl.ds(i * STEP, STEP)
            self.move(("chunk", i), chunk_in.at[:, here], chunk.at[:, here])
            for h in range(CUTS):
                columns = pl.ds(h * part + i * STEP, STEP)
                self.move(("enc", i, h), enc_in.at[rows, columns], enc.at[:, columns])
        self.move("second", dec_in.at[rows], dec)

    def move(self, key, source, target):
        self.moves[key] = pltpu.make_async_copy(source, target, self.sems.at[len(self.moves)])
        self.moves[key].start()

    def __call__(self, stage, i):
        if stage == "first":
            self.moves[("chunk", i)].wait()
            for h in range(CUTS):
                self.moves[("enc", i, h)].wait()
        elif stage in self.moves:
            self.moves[stage].wait()


def chunk_kernel(with_prior, at, chunk_in, enc_in, dec_in, bias, dec_bias, *refs):
    refs = list(refs)
    prior_in = refs.pop(0) if with_prior else None
    mine_out, other_out = refs.pop(0), refs.pop(0)
    flags = refs.pop(0) if with_prior else None
    chunk, enc, dec, cent, err, acc, sems, mine, other, sems_out = refs[:10]
    latents = enc.shape[0]
    core = at[0]
    ready = Loader(sems, at[1], chunk_in, enc_in, dec_in, chunk, enc, dec)
    if with_prior:
        prior, marks = refs[10:]
        ready.move("third", prior_in, prior)
        ready.move("marks", chunk_in.at[:, pl.ds(chunk.shape[1], EXTRA)], marks)

    def out_copy(which, grad):
        source, result = ((mine, mine_out), (other, other_out))[which]
        rows = pl.ds(grad * latents, latents)
        sem = sems_out.at[2 * which + grad]
        return pltpu.make_async_copy(source.at[:, rows], result.at[:, rows], sem)

    def store(i, grad, value):
        rows = slice(grad * latents, (grad + 1) * latents)
        cuts = [value[h * latents : (h + 1) * latents] for h in range(CUTS)]

        @pl.when(core == i)
        def _():
            for h in range(CUTS):
                mine[h, rows] = cuts[h] + prior[h, rows] if with_prior else cuts[h]
            out_copy(0, grad).start()

        @pl.when(core != i)
        def _():
            for h in range(CUTS):
                other[h, rows] = cuts[h].astype(other.dtype)
            out_copy(1, grad).start()

    gradient_body(chunk, enc, dec, bias, dec_bias, cent, err, acc, store, ready)
    if with_prior:
        ready("marks", 0)
        flags[0] = jnp.max(marks[...].astype(F32))
    for which in range(2):
        for grad in range(2):
            out_copy(which, grad).wait()


def vmem():
    return pl.BlockSpec(memory_space=pltpu.VMEM)


def anywhere():
    return pl.BlockSpec(memory_space=pl.ANY)


def hbm():
    return pl.BlockSpec(memory_space=pltpu.HBM)


def smem():
    return pl.BlockSpec(memory_space=pltpu.SMEM)


def on_device(tokens, dec_bias, enc_weight, enc_bias, dec_weight, block_ids, block_home):
    rows, width = tokens.shape
    lat_count = lax.axis_size("lat")
    groups = lax.axis_size("tok")
    chips = groups // 2
    targets = 2 * lat_count
    part = width // CUTS
    slot_rows = targets * GROUP
    latents = enc_weight.shape[0] // 2
    per_cut = part // STEP
    me = lax.axis_index("tok").astype(I32)
    core = me % 2
    first_row = (me // 2 % 2) * latents
    scalars = jnp.stack([core, first_row])
    exchange_groups = [
        [(4 * p + 2 * b + c) * lat_count + at for b in range(2) for at in range(lat_count)]
        for p in range(groups // 4)
        for c in range(2)
    ]
    chunk_shape = jax.ShapeDtypeStruct((slot_rows, part), BF)
    lent_shape = jax.ShapeDtypeStruct((max(LENT) * PIECES, STEP), BF)
    matmul_cost = pl.CostEstimate(
        flops=5 * 2 * slot_rows * CUTS * latents * part,
        bytes_accessed=12 * 2**20,
        transcendentals=0,
    )
    move_cost = pl.CostEstimate(
        flops=2 * slot_rows * CUTS * rows * part, bytes_accessed=5 * 2**20, transcendentals=0
    )

    ids_row = block_ids.reshape(1, rows)
    home_row = block_home.reshape(1, -1)
    chunk1 = pl.pallas_call(
        functools.partial(first_kernel, targets),
        out_shape=chunk_shape,
        in_specs=[vmem()] * 2 + [anywhere()],
        out_specs=anywhere(),
        scratch_shapes=[
            pltpu.VMEM((rows, width), BF),
            pltpu.VMEM((slot_rows, part), BF),
            pltpu.SemaphoreType.DMA((CUTS * per_cut,)),
            pltpu.SemaphoreType.DMA((per_cut,)),
        ],
        compiler_params=room(56),
        cost_estimate=move_cost,
        name="first_slots",
    )(ids_row, home_row, tokens)
    lent_a, lent_b = pl.pallas_call(
        functools.partial(lend_kernel, targets),
        out_shape=[lent_shape, lent_shape],
        in_specs=[vmem()] * 3,
        out_specs=[vmem()] * 2,
        compiler_params=room(20),
        cost_estimate=move_cost,
        name="lent_rows",
    )(ids_row, home_row, tokens)

    def exchange(chunk):
        shaped = chunk.reshape(targets, GROUP, chunk.shape[1])
        got = lax.all_to_all(
            shaped,
            ("tok", "lat"),
            split_axis=0,
            concat_axis=0,
            tiled=True,
            axis_index_groups=exchange_groups,
        )
        return got.reshape(chunk.shape)

    loans_a = lax.all_gather(lent_a, "tok", tiled=True)
    loans_a, lent_b = lax.optimization_barrier((loans_a, lent_b))
    loans_b = lax.all_gather(lent_b, "tok", tiled=True)
    got1 = exchange(chunk1)
    chunk2, left = pl.pallas_call(
        functools.partial(second_kernel, targets),
        out_shape=[
            jax.ShapeDtypeStruct((slot_rows, part + EXTRA), BF),
            jax.ShapeDtypeStruct((8, rows), I32),
        ],
        in_specs=[smem()] + [vmem()] * 3,
        out_specs=[vmem()] * 2,
        compiler_params=room(24),
        cost_estimate=move_cost,
        name="second_slots",
    )(me.reshape(1), tokens, loans_a, loans_b)
    got2 = exchange(chunk2)
    bias_row = lax.dynamic_slice_in_dim(enc_bias, first_row, latents).reshape(latents, 1)
    offset_row = dec_bias.reshape(1, width)
    half_shape = (CUTS, 2 * latents, STEP)

    def work(kind):
        return [
            pltpu.VMEM((slot_rows, part), BF),
            pltpu.VMEM((latents, width), BF),
            pltpu.VMEM((latents, width), BF),
            pltpu.VMEM((slot_rows, part), BF),
            pltpu.VMEM((slot_rows, part), BF),
            pltpu.VMEM((CUTS * latents, slot_rows), F32),
            pltpu.SemaphoreType.DMA((per_cut * (CUTS + 1) + 3,)),
            pltpu.VMEM(half_shape, F32),
            pltpu.VMEM(half_shape, kind),
            pltpu.SemaphoreType.DMA((4,)),
        ]

    def swap(values):
        return lax.ppermute(values, "tok", [(i, i ^ 1) for i in range(groups)])

    operands = (enc_weight, dec_weight, bias_row, offset_row)
    part_call = pl.pallas_call(
        functools.partial(chunk_kernel, False),
        out_shape=[jax.ShapeDtypeStruct(half_shape, F32)] * 2,
        in_specs=[smem()] + [hbm()] * 3 + [vmem()] * 2,
        out_specs=[hbm()] * 2,
        scratch_shapes=work(F32),
        compiler_params=room(56),
        cost_estimate=matmul_cost,
        name="chunk_gradients",
    )
    mine1, other1 = part_call(scalars, got1, *operands)
    prior = mine1 + swap(other1)
    mine, other, flags = pl.pallas_call(
        functools.partial(chunk_kernel, True),
        out_shape=[
            jax.ShapeDtypeStruct(half_shape, F32),
            jax.ShapeDtypeStruct(half_shape, BF),
            jax.ShapeDtypeStruct((1,), F32),
        ],
        in_specs=[smem(), anywhere()] + [hbm()] * 2 + [vmem()] * 2 + [hbm()],
        out_specs=[anywhere()] * 2 + [smem()],
        scratch_shapes=[
            *work(BF),
            pltpu.VMEM(half_shape, F32),
            pltpu.VMEM((slot_rows, EXTRA), BF),
        ],
        compiler_params=room(56),
        cost_estimate=matmul_cost,
        name="last_gradients",
    )(scalars, got2, *operands, prior)

    def rest(carry):
        mine, other, unused = carry
        codes, cut = slot_codes(targets, DIRECT)
        hit = flat(codes == left[:1])
        data = jnp.zeros((slot_rows, part), F32)
        for h in range(CUTS):
            chosen = jnp.where(cut == h, hit, 0.0).astype(BF)
            data = data + mm(chosen, tokens[:, h * part : (h + 1) * part])
        filled = jnp.sum(hit, axis=1, keepdims=True) > 0.5
        chunk3 = jnp.where(filled, data, EMPTY).astype(BF)
        more, more_other = part_call(scalars, exchange(chunk3), *operands)
        return mine + more, (other.astype(F32) + more_other).astype(BF), jnp.zeros((), F32)

    mine, other, unused = lax.while_loop(
        lambda carry: carry[2] > 0.5, rest, (mine, other, flags.reshape(()))
    )
    summed = (mine + swap(other).astype(F32)).astype(BF)
    terms = lax.all_to_all(
        summed,
        "tok",
        split_axis=0,
        concat_axis=0,
        tiled=True,
        axis_index_groups=[[2 * i + c for i in range(chips)] for c in range(2)],
    )
    total = jnp.sum(terms.astype(F32).reshape(chips // 2, 2, 2, latents, STEP), axis=0)
    return total[:, 0].reshape(2 * latents, STEP), total[:, 1].reshape(2 * latents, STEP)


def solution(mesh):
    in_specs = (
        P(("tok", "lat"), None),
        P(),
        P("lat", None),
        P("lat"),
        P("lat", None),
        P(("tok", "lat"), None),
        P(),
    )
    out_specs = (P("lat", "tok"), P("lat", "tok"))
    return jax.shard_map(
        on_device, mesh=mesh, in_specs=in_specs, out_specs=out_specs, check_vma=False
    )
```

```python
import functools

import jax
import jax.numpy as jnp
from jax import lax
from jax.experimental import pallas as pl
from jax.experimental.pallas import tpu as pltpu
from jax.sharding import PartitionSpec as P

BF = jnp.bfloat16
F32 = jnp.float32
I32 = jnp.int32

CUTS = 4
SLOTS = 2
DIRECT = 2 * SLOTS
GROUP = CUTS * SLOTS
STRIDE = 8
EMPTY = 2.0**100
STEP = 1024
PIECES = 8
LENT = (6, 7)


def room(mib):
    return pltpu.CompilerParams(vmem_limit_bytes=mib * 2**20)


def mm(a, b):
    return jnp.dot(a, b, preferred_element_type=F32)


def mm_t(a, b):
    return lax.dot_general(a, b, (((1,), (1,)), ((), ())), preferred_element_type=F32)


def iota(shape, axis):
    return lax.broadcasted_iota(I32, shape, axis)


def flat(mask):
    return jnp.where(mask, 1.0, 0.0)


def slot_codes(targets, first):
    row = iota((targets * GROUP, 1), 0)
    inner = row % GROUP
    return (row // GROUP) * STRIDE + first + inner % SLOTS, inner // SLOTS


def before(n):
    return (iota((n, n), 0) < iota((n, n), 1)).astype(F32).astype(BF)


def ranks_of(target, targets):
    g, n = target.shape
    members = flat(target[:, None, :] == iota((g, targets, n), 1))
    counts = mm(members.reshape(g * targets, n).astype(BF), before(n)).reshape(g, targets, n)
    return members, jnp.sum(members * counts, axis=1)


def target_of(places, targets):
    return (places & 1) * (targets // 2) + (places >> 1)


def cut_columns(ref, i):
    part = ref.shape[1] // CUTS
    return [ref[:, h * part + i * STEP : h * part + (i + 1) * STEP] for h in range(CUTS)]


def places_of(ids, home):
    total = home.shape[1]
    named = flat(iota((total, ids.shape[1]), 0) == ids[...]).astype(BF)
    table = jnp.broadcast_to(home[...], (8, total)).astype(F32).astype(BF)
    return mm(table, named)[:1].astype(I32)


def first_kernel(targets, ids, home, tokens_in, chunk_out, tokens, chunk, sems_in, sems_out):
    rows, width = tokens.shape
    part = width // CUTS
    steps = part // STEP
    loads = []
    for i in range(steps):
        for h in range(CUTS):
            columns = pl.ds(h * part + i * STEP, STEP)
            sem = sems_in.at[len(loads)]
            loads.append(pltpu.make_async_copy(tokens_in.at[:, columns], tokens.at[:, columns], sem))
            loads[-1].start()
    target = target_of(places_of(ids, home), targets)
    unused, rank = ranks_of(target, targets)
    codes, cut = slot_codes(targets, 0)
    hit = flat(codes == target * STRIDE + rank.astype(I32))
    wide = jnp.concatenate([jnp.where(cut == h, hit, 0.0) for h in range(CUTS)], axis=1)
    wide = wide.astype(BF)
    filled = jnp.sum(hit, axis=1, keepdims=True) > 0.5
    stores = []
    for i in range(steps):
        for h in range(CUTS):
            loads[i * CUTS + h].wait()
        got = mm(wide, jnp.concatenate(cut_columns(tokens, i), axis=0))
        chunk[:, i * STEP : (i + 1) * STEP] = jnp.where(filled, got, EMPTY).astype(BF)
        columns = pl.ds(i * STEP, STEP)
        stores.append(
            pltpu.make_async_copy(chunk.at[:, columns], chunk_out.at[:, columns], sems_out.at[i])
        )
        stores[-1].start()
    for store in stores:
        store.wait()


def lend_kernel(targets, ids, home, tokens, lent_a, lent_b):
    rows = tokens.shape[0]
    places = places_of(ids, home)
    unused, rank = ranks_of(target_of(places, targets), targets)
    over = flat(rank.astype(I32) >= DIRECT)
    order = mm(jnp.broadcast_to(over, (8, rows)).astype(BF), before(rows))[:1].astype(I32)
    first = 0
    for count, lent in zip(LENT, (lent_a, lent_b)):
        lines = lent.shape[0]
        line = iota((lines, rows), 0)
        take = jnp.logical_and(order == first + line // PIECES, over > 0.5)
        take = flat(jnp.logical_and(take, line < count * PIECES))
        piece = iota((lines, 1), 0) % PIECES
        got = jnp.zeros((lines, STEP), F32)
        for i in range(PIECES):
            chosen = jnp.where(piece == i, take, 0.0).astype(BF)
            got = got + mm(chosen, tokens[:, i * STEP : (i + 1) * STEP])
        if first == 0:
            head = jnp.where(line == count * PIECES, places.astype(F32), got[:, :rows])
            got = jnp.concatenate([head, got[:, rows:]], axis=1)
        lent[...] = got.astype(BF)
        first += count


def second_kernel(targets, group, tokens, loans_a, loans_b, chunk, left, flags):
    rows, width = tokens.shape
    part = width // CUTS
    lines = (LENT[0] + 1) * PIECES
    groups = loans_a.shape[0] // lines
    me = group[0]
    heads = loans_a[:, :rows].astype(F32).reshape(groups, lines, rows)
    places = heads[:, LENT[0] * PIECES, :].astype(I32)
    target = target_of(places, targets)
    members, rank_f = ranks_of(target, targets)
    rank = rank_f.astype(I32)
    over = rank >= DIRECT
    order = mm(flat(over).astype(BF), before(rows)).astype(I32)
    listed = jnp.logical_and(over, order < sum(LENT))
    count = jnp.sum(members, axis=2, keepdims=True)
    asked = jnp.sum(members * flat(listed)[:, None, :], axis=2, keepdims=True)
    used = jnp.maximum(count, float(SLOTS))
    free = jnp.maximum(DIRECT - used, 0.0)
    asked_before = []
    running = jnp.zeros((1, targets, 1), F32)
    free_total = jnp.zeros((1, targets, 1), F32)
    free_before = jnp.zeros((1, targets, 1), F32)
    for t in range(groups):
        asked_before.append(running)
        running = running + asked[t : t + 1]
        free_before = free_before + jnp.where(me > t, free[t : t + 1], 0.0)
        free_total = free_total + free[t : t + 1]
    mine = flat(iota((groups, 1, 1), 0) == me)
    my_free = jnp.sum(free * mine, axis=0, keepdims=True)
    my_used = jnp.sum(used * mine, axis=0, keepdims=True)

    def look(values):
        return jnp.sum(members * values, axis=1).astype(I32)

    in_pool = look(jnp.concatenate(asked_before, axis=0)) + rank - DIRECT
    placed = jnp.logical_and(listed, in_pool < look(free_total))
    at = in_pool - look(free_before)
    here = jnp.logical_and(placed, jnp.logical_and(at >= 0, at < look(my_free)))
    lent_code = jnp.where(here, target * STRIDE + look(my_used) + at, -1)
    size = groups * lines
    square = iota((size, size), 0) == iota((size, size), 1)
    line_of = iota((lines, rows), 0) // PIECES

    def codes_of_lines(first, count):
        columns = []
        for t in range(groups):
            chosen = jnp.logical_and(order[t : t + 1] == first + line_of, listed[t : t + 1])
            chosen = jnp.logical_and(chosen, line_of < count)
            value = jnp.where(chosen, lent_code[t : t + 1] + 1, 0)
            columns.append(jnp.sum(value, axis=1, keepdims=True) - 1)
        column = jnp.concatenate(columns, axis=0)
        return jnp.sum(jnp.where(square, column, 0), axis=0, keepdims=True)

    mine2 = (iota((groups, 1), 0) == me).astype(I32)
    own_code = jnp.sum((target * STRIDE + rank) * mine2, axis=0, keepdims=True)
    missing = jnp.logical_and(over, jnp.logical_not(placed)).astype(I32)
    own_missing = jnp.sum(missing * mine2, axis=0, keepdims=True)
    left[...] = jnp.broadcast_to(jnp.where(own_missing > 0, own_code, -1), left.shape)
    flag = jnp.max(jnp.max(missing.astype(F32), axis=1, keepdims=True), axis=0, keepdims=True)
    codes, cut = slot_codes(targets, SLOTS)
    hit = flat(codes == own_code)
    wide = jnp.concatenate([jnp.where(cut == h, hit, 0.0) for h in range(CUTS)], axis=1)
    wide = wide.astype(BF)
    hit_a = flat(codes == codes_of_lines(0, LENT[0]))
    hit_b = flat(codes == codes_of_lines(LENT[0], LENT[1]))
    filled = jnp.sum(hit, axis=1, keepdims=True) + jnp.sum(hit_a, axis=1, keepdims=True)
    filled = filled + jnp.sum(hit_b, axis=1, keepdims=True) > 0.5
    flags[...] = jnp.broadcast_to(flag, flags.shape)
    per_cut = part // STEP
    piece = iota((1, size), 1) % PIECES
    for i in range(per_cut):
        at_cut = cut * per_cut + i == piece
        got = mm(wide, jnp.concatenate(cut_columns(tokens, i), axis=0))
        got = got + mm(jnp.where(at_cut, hit_a, 0.0).astype(BF), loans_a[...])
        got = got + mm(jnp.where(at_cut, hit_b, 0.0).astype(BF), loans_b[...])
        chunk[:, i * STEP : (i + 1) * STEP] = jnp.where(filled, got, EMPTY).astype(BF)


def gradient_body(chunk, enc, dec, bias, dec_bias, cent, err, acc, store, ready):
    rows, part = chunk.shape
    latents = enc.shape[0]
    steps = part // STEP
    inner = iota((1, rows), 1) % GROUP
    cut = inner // SLOTS
    cut8 = iota((GROUP, 1), 0) // SLOTS

    def here(i):
        return slice(i * STEP, (i + 1) * STEP)

    def offset(i):
        value = jnp.zeros((GROUP, STEP), F32)
        for h, columns in enumerate(cut_columns(dec_bias, i)):
            value = jnp.where(cut8 == h, columns, value)
        return value[None]

    def joined(total):
        own = total[:latents]
        for h in range(1, CUTS):
            own = jnp.where(cut == h, total[h * latents : (h + 1) * latents], own)
        shift = GROUP // 2
        while shift >= SLOTS:
            down = pltpu.roll(own, rows - shift, 1)
            wrapped = pltpu.roll(own, GROUP - shift, 1)
            own = own + jnp.where(inner < GROUP - shift, down, wrapped)
            shift //= 2
        return own

    def spread(values):
        return jnp.concatenate([jnp.where(cut == h, values, 0.0) for h in range(CUTS)], axis=0)

    for i in range(steps):
        ready("first", i)
        x = chunk[:, here(i)].astype(F32).reshape(rows // GROUP, GROUP, STEP)
        c = (x - offset(i)).reshape(rows, STEP).astype(BF)
        cent[:, here(i)] = c
        w = jnp.concatenate(cut_columns(enc, i), axis=0)
        if i == 0:
            acc[...] = mm_t(w, c)
        else:
            acc[...] += mm_t(w, c)
    filled = flat(chunk[:, :128].astype(F32) < EMPTY / 2).astype(BF)
    valid = mm_t(flat(iota((8, 128), 1) == 0).astype(BF), filled)[:1] > 0.5
    pre = joined(acc[...]) + bias[...]
    gate = 1.0 / (1.0 + jnp.exp(-pre))
    latent = spread(jnp.where(valid, pre * gate, 0.0))
    latent_t = latent.astype(BF)
    latent_b = latent.T.astype(BF)
    ready("second", 0)
    for i in range(steps):
        w = jnp.concatenate(cut_columns(dec, i), axis=0)
        d = mm(latent_b, w).astype(BF).astype(F32).reshape(rows // GROUP, GROUP, STEP)
        x = chunk[:, here(i)].astype(F32).reshape(rows // GROUP, GROUP, STEP)
        e = ((offset(i) + d - x) * (1.0 / 32.0)).reshape(rows, STEP).astype(BF)
        err[:, here(i)] = e
        if i == 0:
            acc[...] = mm_t(w, e)
        else:
            acc[...] += mm_t(w, e)
    dlatent = joined(acc[...])
    dpre = spread(jnp.where(valid, dlatent * gate * (1.0 + pre * (1.0 - gate)), 0.0))
    dpre_t = dpre.astype(BF)
    ready("third", 0)
    for i in range(steps):
        store(i, 0, mm(dpre_t, cent[:, here(i)]))
        store(i, 1, mm(latent_t, err[:, here(i)]))


class Loader:
    def __init__(self, sems, first_row, chunk_in, enc_in, dec_in, chunk, enc, dec):
        self.sems = sems
        self.moves = {}
        part = chunk.shape[1]
        latents = enc.shape[0]
        rows = pl.ds(pl.multiple_of(first_row, latents), latents)
        for i in range(part // STEP):
            here = pl.ds(i * STEP, STEP)
            self.move(("chunk", i), chunk_in.at[:, here], chunk.at[:, here])
            for h in range(CUTS):
                columns = pl.ds(h * part + i * STEP, STEP)
                self.move(("enc", i, h), enc_in.at[rows, columns], enc.at[:, columns])
        self.move("second", dec_in.at[rows], dec)

    def move(self, key, source, target):
        self.moves[key] = pltpu.make_async_copy(source, target, self.sems.at[len(self.moves)])
        self.moves[key].start()

    def __call__(self, stage, i):
        if stage == "first":
            self.moves[("chunk", i)].wait()
            for h in range(CUTS):
                self.moves[("enc", i, h)].wait()
        elif stage in self.moves:
            self.moves[stage].wait()


def chunk_kernel(with_prior, at, chunk_in, enc_in, dec_in, bias, dec_bias, *refs):
    refs = list(refs)
    prior_in = refs.pop(0) if with_prior else None
    mine_out, other_out = refs.pop(0), refs.pop(0)
    chunk, enc, dec, cent, err, acc, sems, mine, other, sems_out = refs[:10]
    latents = enc.shape[0]
    core = at[0]
    ready = Loader(sems, at[1], chunk_in, enc_in, dec_in, chunk, enc, dec)
    if with_prior:
        prior = refs[10]
        ready.move("third", prior_in, prior)

    def out_copy(which, grad):
        source, result = ((mine, mine_out), (other, other_out))[which]
        rows = pl.ds(grad * latents, latents)
        sem = sems_out.at[2 * which + grad]
        return pltpu.make_async_copy(source.at[:, rows], result.at[:, rows], sem)

    def store(i, grad, value):
        rows = slice(grad * latents, (grad + 1) * latents)
        cuts = [value[h * latents : (h + 1) * latents] for h in range(CUTS)]

        @pl.when(core == i)
        def _():
            for h in range(CUTS):
                mine[h, rows] = cuts[h] + prior[h, rows] if with_prior else cuts[h]
            out_copy(0, grad).start()

        @pl.when(core != i)
        def _():
            for h in range(CUTS):
                other[h, rows] = cuts[h].astype(other.dtype)
            out_copy(1, grad).start()

    gradient_body(chunk, enc, dec, bias, dec_bias, cent, err, acc, store, ready)
    for which in range(2):
        for grad in range(2):
            out_copy(which, grad).wait()


def vmem():
    return pl.BlockSpec(memory_space=pltpu.VMEM)


def anywhere():
    return pl.BlockSpec(memory_space=pl.ANY)


def hbm():
    return pl.BlockSpec(memory_space=pltpu.HBM)


def smem():
    return pl.BlockSpec(memory_space=pltpu.SMEM)


def on_device(tokens, dec_bias, enc_weight, enc_bias, dec_weight, block_ids, block_home):
    rows, width = tokens.shape
    lat_count = lax.axis_size("lat")
    groups = lax.axis_size("tok")
    chips = groups // 2
    targets = 2 * lat_count
    part = width // CUTS
    slot_rows = targets * GROUP
    latents = enc_weight.shape[0] // 2
    per_cut = part // STEP
    me = lax.axis_index("tok").astype(I32)
    core = me % 2
    first_row = (me // 2 % 2) * latents
    scalars = jnp.stack([core, first_row])
    exchange_groups = [
        [(4 * p + 2 * b + c) * lat_count + at for b in range(2) for at in range(lat_count)]
        for p in range(groups // 4)
        for c in range(2)
    ]
    chunk_shape = jax.ShapeDtypeStruct((slot_rows, part), BF)
    lent_shape = jax.ShapeDtypeStruct((max(LENT) * PIECES, STEP), BF)
    matmul_cost = pl.CostEstimate(
        flops=5 * 2 * slot_rows * CUTS * latents * part,
        bytes_accessed=12 * 2**20,
        transcendentals=0,
    )
    move_cost = pl.CostEstimate(
        flops=2 * slot_rows * CUTS * rows * part, bytes_accessed=5 * 2**20, transcendentals=0
    )

    ids_row = block_ids.reshape(1, rows)
    home_row = block_home.reshape(1, -1)
    chunk1 = pl.pallas_call(
        functools.partial(first_kernel, targets),
        out_shape=chunk_shape,
        in_specs=[vmem()] * 2 + [anywhere()],
        out_specs=anywhere(),
        scratch_shapes=[
            pltpu.VMEM((rows, width), BF),
            pltpu.VMEM((slot_rows, part), BF),
            pltpu.SemaphoreType.DMA((CUTS * per_cut,)),
            pltpu.SemaphoreType.DMA((per_cut,)),
        ],
        compiler_params=room(56),
        cost_estimate=move_cost,
        name="first_slots",
    )(ids_row, home_row, tokens)
    lent_a, lent_b = pl.pallas_call(
        functools.partial(lend_kernel, targets),
        out_shape=[lent_shape, lent_shape],
        in_specs=[vmem()] * 3,
        out_specs=[vmem()] * 2,
        compiler_params=room(20),
        cost_estimate=move_cost,
        name="lent_rows",
    )(ids_row, home_row, tokens)

    def exchange(chunk):
        shaped = chunk.reshape(targets, GROUP, chunk.shape[1])
        got = lax.all_to_all(
            shaped,
            ("tok", "lat"),
            split_axis=0,
            concat_axis=0,
            tiled=True,
            axis_index_groups=exchange_groups,
        )
        return got.reshape(chunk.shape)

    loans_a = lax.all_gather(lent_a, "tok", tiled=True)
    loans_a, lent_b = lax.optimization_barrier((loans_a, lent_b))
    loans_b = lax.all_gather(lent_b, "tok", tiled=True)
    got1 = exchange(chunk1)
    chunk2, left, flags = pl.pallas_call(
        functools.partial(second_kernel, targets),
        out_shape=[
            chunk_shape,
            jax.ShapeDtypeStruct((8, rows), I32),
            jax.ShapeDtypeStruct((8, rows), F32),
        ],
        in_specs=[smem()] + [vmem()] * 3,
        out_specs=[vmem()] * 3,
        compiler_params=room(24),
        cost_estimate=move_cost,
        name="second_slots",
    )(me.reshape(1), tokens, loans_a, loans_b)
    got2 = exchange(chunk2)
    line = 4
    along_x = [[i * line + j for j in range(line)] for i in range(lat_count // line)]
    along_z = [[i * line + j for i in range(lat_count // line)] for j in range(line)]

    def highest(values, lines):
        return jnp.max(lax.all_gather(values, "lat", axis_index_groups=lines), axis=0)

    flags = highest(flags, along_x)
    bias_row = lax.dynamic_slice_in_dim(enc_bias, first_row, latents).reshape(latents, 1)
    offset_row = dec_bias.reshape(1, width)
    half_shape = (CUTS, 2 * latents, STEP)

    def work(kind):
        return [
            pltpu.VMEM((slot_rows, part), BF),
            pltpu.VMEM((latents, width), BF),
            pltpu.VMEM((latents, width), BF),
            pltpu.VMEM((slot_rows, part), BF),
            pltpu.VMEM((slot_rows, part), BF),
            pltpu.VMEM((CUTS * latents, slot_rows), F32),
            pltpu.SemaphoreType.DMA((per_cut * (CUTS + 1) + 3,)),
            pltpu.VMEM(half_shape, F32),
            pltpu.VMEM(half_shape, kind),
            pltpu.SemaphoreType.DMA((4,)),
        ]

    def swap(values):
        return lax.ppermute(values, "tok", [(i, i ^ 1) for i in range(groups)])

    operands = (enc_weight, dec_weight, bias_row, offset_row)
    part_call = pl.pallas_call(
        functools.partial(chunk_kernel, False),
        out_shape=[jax.ShapeDtypeStruct(half_shape, F32)] * 2,
        in_specs=[smem()] + [hbm()] * 3 + [vmem()] * 2,
        out_specs=[hbm()] * 2,
        scratch_shapes=work(F32),
        compiler_params=room(56),
        cost_estimate=matmul_cost,
        name="chunk_gradients",
    )
    mine1, other1 = part_call(scalars, got1, *operands)
    other1, flags = lax.optimization_barrier((other1, flags))
    prior = mine1 + swap(other1)
    mine, other = pl.pallas_call(
        functools.partial(chunk_kernel, True),
        out_shape=[
            jax.ShapeDtypeStruct(half_shape, F32),
            jax.ShapeDtypeStruct(half_shape, BF),
        ],
        in_specs=[smem(), anywhere()] + [hbm()] * 2 + [vmem()] * 2 + [hbm()],
        out_specs=[anywhere()] * 2,
        scratch_shapes=[
            *work(BF),
            pltpu.VMEM(half_shape, F32),
        ],
        compiler_params=room(56),
        cost_estimate=matmul_cost,
        name="last_gradients",
    )(scalars, got2, *operands, prior)

    def gradients(summed):
        terms = lax.all_to_all(
            summed,
            "tok",
            split_axis=0,
            concat_axis=0,
            tiled=True,
            axis_index_groups=[[2 * i + c for i in range(chips)] for c in range(2)],
        )
        total = jnp.sum(terms.astype(F32).reshape(chips // 2, 2, 2, latents, STEP), axis=0)
        return total[:, 0].reshape(2 * latents, STEP), total[:, 1].reshape(2 * latents, STEP)

    def rest(carry):
        enc_grad, dec_grad, unused = carry
        codes, cut = slot_codes(targets, DIRECT)
        hit = flat(codes == left[:1])
        data = jnp.zeros((slot_rows, part), F32)
        for h in range(CUTS):
            chosen = jnp.where(cut == h, hit, 0.0).astype(BF)
            data = data + mm(chosen, tokens[:, h * part : (h + 1) * part])
        filled = jnp.sum(hit, axis=1, keepdims=True) > 0.5
        chunk3 = jnp.where(filled, data, EMPTY).astype(BF)
        more, more_other = part_call(scalars, exchange(chunk3), *operands)
        enc_more, dec_more = gradients((more + swap(more_other)).astype(BF))
        return enc_grad + enc_more, dec_grad + dec_more, jnp.zeros((), F32)

    summed = (mine + swap(other).astype(F32)).astype(BF)
    summed, flags = lax.optimization_barrier((summed, flags))
    enc_grad, dec_grad = gradients(summed)
    flags = highest(flags, along_z)
    enc_grad, dec_grad, unused = lax.while_loop(
        lambda carry: carry[2] > 0.5, rest, (enc_grad, dec_grad, flags[0, 0])
    )
    return enc_grad, dec_grad


def solution(mesh):
    in_specs = (
        P(("tok", "lat"), None),
        P(),
        P("lat", None),
        P("lat"),
        P("lat", None),
        P(("tok", "lat"), None),
        P(),
    )
    out_specs = (P("lat", "tok"), P("lat", "tok"))
    return jax.shard_map(
        on_device, mesh=mesh, in_specs=in_specs, out_specs=out_specs, check_vma=False
    )
```

```python
import functools

import jax
import jax.numpy as jnp
from jax import lax
from jax.experimental import pallas as pl
from jax.experimental.pallas import tpu as pltpu
from jax.sharding import PartitionSpec as P

BF = jnp.bfloat16
F32 = jnp.float32
I32 = jnp.int32

CUTS = 4
SLOTS = 2
DIRECT = 2 * SLOTS
GROUP = CUTS * SLOTS
STRIDE = 8
EMPTY = 2.0**100
EXTRA = 128
STEP = 1024
FINE = 512
PIECES = 8
LENT = (6, 7)


def room(mib):
    return pltpu.CompilerParams(vmem_limit_bytes=mib * 2**20)


def mm(a, b):
    return jnp.dot(a, b, preferred_element_type=F32)


def mm_t(a, b):
    return lax.dot_general(a, b, (((1,), (1,)), ((), ())), preferred_element_type=F32)


def iota(shape, axis):
    return lax.broadcasted_iota(I32, shape, axis)


def flat(mask):
    return jnp.where(mask, 1.0, 0.0)


def slot_codes(targets, first):
    row = iota((targets * GROUP, 1), 0)
    inner = row % GROUP
    return (row // GROUP) * STRIDE + first + inner % SLOTS, inner // SLOTS


def before(n):
    return (iota((n, n), 0) < iota((n, n), 1)).astype(F32).astype(BF)


def ranks_of(target, targets):
    g, n = target.shape
    members = flat(target[:, None, :] == iota((g, targets, n), 1))
    counts = mm(members.reshape(g * targets, n).astype(BF), before(n)).reshape(g, targets, n)
    return members, jnp.sum(members * counts, axis=1)


def target_of(places, targets):
    return (places & 1) * (targets // 2) + (places >> 1)


def cut_columns(ref, i, step=STEP):
    part = ref.shape[1] // CUTS
    return [ref[:, h * part + i * step : h * part + (i + 1) * step] for h in range(CUTS)]


def places_of(ids, home):
    total = home.shape[1]
    named = flat(iota((total, ids.shape[1]), 0) == ids[...]).astype(BF)
    table = jnp.broadcast_to(home[...], (8, total)).astype(F32).astype(BF)
    return mm(table, named)[:1].astype(I32)


def first_kernel(
    targets, ids_in, home_in, tokens_in, chunk_out, ids, home, tokens, chunk, sems_in, sems_out
):
    rows, width = tokens.shape
    part = width // CUTS
    steps = part // FINE
    loads = []

    def load(source, target):
        loads.append(pltpu.make_async_copy(source, target, sems_in.at[len(loads)]))
        loads[-1].start()

    load(ids_in, ids)
    load(home_in, home)
    for i in range(steps):
        for h in range(CUTS):
            columns = pl.ds(h * part + i * FINE, FINE)
            load(tokens_in.at[:, columns], tokens.at[:, columns])
    loads[0].wait()
    loads[1].wait()
    target = target_of(places_of(ids, home), targets)
    unused, rank = ranks_of(target, targets)
    codes, cut = slot_codes(targets, 0)
    hit = flat(codes == target * STRIDE + rank.astype(I32))
    wide = jnp.concatenate([jnp.where(cut == h, hit, 0.0) for h in range(CUTS)], axis=1)
    wide = wide.astype(BF)
    filled = jnp.sum(hit, axis=1, keepdims=True) > 0.5
    stores = []
    for i in range(steps):
        for h in range(CUTS):
            loads[2 + i * CUTS + h].wait()
        got = mm(wide, jnp.concatenate(cut_columns(tokens, i, FINE), axis=0))
        chunk[:, i * FINE : (i + 1) * FINE] = jnp.where(filled, got, EMPTY).astype(BF)
        columns = pl.ds(i * FINE, FINE)
        stores.append(
            pltpu.make_async_copy(chunk.at[:, columns], chunk_out.at[:, columns], sems_out.at[i])
        )
        stores[-1].start()
    for store in stores:
        store.wait()


def lend_kernel(targets, ids, home, tokens, lent_a, lent_b):
    rows = tokens.shape[0]
    places = places_of(ids, home)
    unused, rank = ranks_of(target_of(places, targets), targets)
    over = flat(rank.astype(I32) >= DIRECT)
    order = mm(jnp.broadcast_to(over, (8, rows)).astype(BF), before(rows))[:1].astype(I32)
    first = 0
    for count, lent in zip(LENT, (lent_a, lent_b)):
        lines = lent.shape[0]
        line = iota((lines, rows), 0)
        take = jnp.logical_and(order == first + line // PIECES, over > 0.5)
        take = flat(jnp.logical_and(take, line < count * PIECES))
        piece = iota((lines, 1), 0) % PIECES
        got = jnp.zeros((lines, STEP), F32)
        for i in range(PIECES):
            chosen = jnp.where(piece == i, take, 0.0).astype(BF)
            got = got + mm(chosen, tokens[:, i * STEP : (i + 1) * STEP])
        if first == 0:
            head = jnp.where(line == count * PIECES, places.astype(F32), got[:, :rows])
            got = jnp.concatenate([head, got[:, rows:]], axis=1)
        lent[...] = got.astype(BF)
        first += count


def second_kernel(targets, group, tokens, loans_a, loans_b, chunk, left):
    rows, width = tokens.shape
    part = width // CUTS
    lines = (LENT[0] + 1) * PIECES
    groups = loans_a.shape[0] // lines
    me = group[0]
    heads = loans_a[:, :rows].astype(F32).reshape(groups, lines, rows)
    places = heads[:, LENT[0] * PIECES, :].astype(I32)
    target = target_of(places, targets)
    members, rank_f = ranks_of(target, targets)
    rank = rank_f.astype(I32)
    over = rank >= DIRECT
    order = mm(flat(over).astype(BF), before(rows)).astype(I32)
    listed = jnp.logical_and(over, order < sum(LENT))
    count = jnp.sum(members, axis=2, keepdims=True)
    asked = jnp.sum(members * flat(listed)[:, None, :], axis=2, keepdims=True)
    used = jnp.maximum(count, float(SLOTS))
    free = jnp.maximum(DIRECT - used, 0.0)
    asked_before = []
    running = jnp.zeros((1, targets, 1), F32)
    free_total = jnp.zeros((1, targets, 1), F32)
    free_before = jnp.zeros((1, targets, 1), F32)
    for t in range(groups):
        asked_before.append(running)
        running = running + asked[t : t + 1]
        free_before = free_before + jnp.where(me > t, free[t : t + 1], 0.0)
        free_total = free_total + free[t : t + 1]
    mine = flat(iota((groups, 1, 1), 0) == me)
    my_free = jnp.sum(free * mine, axis=0, keepdims=True)
    my_used = jnp.sum(used * mine, axis=0, keepdims=True)

    def look(values):
        return jnp.sum(members * values, axis=1).astype(I32)

    in_pool = look(jnp.concatenate(asked_before, axis=0)) + rank - DIRECT
    placed = jnp.logical_and(listed, in_pool < look(free_total))
    at = in_pool - look(free_before)
    here = jnp.logical_and(placed, jnp.logical_and(at >= 0, at < look(my_free)))
    lent_code = jnp.where(here, target * STRIDE + look(my_used) + at, -1)
    size = groups * lines
    square = iota((size, size), 0) == iota((size, size), 1)
    line_of = iota((lines, rows), 0) // PIECES

    def codes_of_lines(first, count):
        columns = []
        for t in range(groups):
            chosen = jnp.logical_and(order[t : t + 1] == first + line_of, listed[t : t + 1])
            chosen = jnp.logical_and(chosen, line_of < count)
            value = jnp.where(chosen, lent_code[t : t + 1] + 1, 0)
            columns.append(jnp.sum(value, axis=1, keepdims=True) - 1)
        column = jnp.concatenate(columns, axis=0)
        return jnp.sum(jnp.where(square, column, 0), axis=0, keepdims=True)

    mine2 = (iota((groups, 1), 0) == me).astype(I32)
    own_code = jnp.sum((target * STRIDE + rank) * mine2, axis=0, keepdims=True)
    missing = jnp.logical_and(over, jnp.logical_not(placed)).astype(I32)
    own_missing = jnp.sum(missing * mine2, axis=0, keepdims=True)
    left[...] = jnp.broadcast_to(jnp.where(own_missing > 0, own_code, -1), left.shape)
    flag = jnp.max(jnp.max(missing.astype(F32), axis=1, keepdims=True), axis=0, keepdims=True)
    codes, cut = slot_codes(targets, SLOTS)
    hit = flat(codes == own_code)
    wide = jnp.concatenate([jnp.where(cut == h, hit, 0.0) for h in range(CUTS)], axis=1)
    wide = wide.astype(BF)
    hit_a = flat(codes == codes_of_lines(0, LENT[0]))
    hit_b = flat(codes == codes_of_lines(LENT[0], LENT[1]))
    filled = jnp.sum(hit, axis=1, keepdims=True) + jnp.sum(hit_a, axis=1, keepdims=True)
    filled = filled + jnp.sum(hit_b, axis=1, keepdims=True) > 0.5
    chunk[:, part:] = jnp.broadcast_to(flag, (hit.shape[0], EXTRA)).astype(BF)
    per_cut = part // STEP
    piece = iota((1, size), 1) % PIECES
    for i in range(per_cut):
        at_cut = cut * per_cut + i == piece
        got = mm(wide, jnp.concatenate(cut_columns(tokens, i), axis=0))
        got = got + mm(jnp.where(at_cut, hit_a, 0.0).astype(BF), loans_a[...])
        got = got + mm(jnp.where(at_cut, hit_b, 0.0).astype(BF), loans_b[...])
        chunk[:, i * STEP : (i + 1) * STEP] = jnp.where(filled, got, EMPTY).astype(BF)


def gradient_body(chunk, enc, dec, bias, dec_bias, cent, err, acc, store, ready):
    rows, part = chunk.shape
    latents = enc.shape[0]
    steps = part // STEP
    inner = iota((1, rows), 1) % GROUP
    cut = inner // SLOTS
    cut8 = iota((GROUP, 1), 0) // SLOTS

    def here(i):
        return slice(i * STEP, (i + 1) * STEP)

    def offset(i):
        value = jnp.zeros((GROUP, STEP), F32)
        for h, columns in enumerate(cut_columns(dec_bias, i)):
            value = jnp.where(cut8 == h, columns, value)
        return value[None]

    def joined(total):
        own = total[:latents]
        for h in range(1, CUTS):
            own = jnp.where(cut == h, total[h * latents : (h + 1) * latents], own)
        shift = GROUP // 2
        while shift >= SLOTS:
            down = pltpu.roll(own, rows - shift, 1)
            wrapped = pltpu.roll(own, GROUP - shift, 1)
            own = own + jnp.where(inner < GROUP - shift, down, wrapped)
            shift //= 2
        return own

    def spread(values):
        return jnp.concatenate([jnp.where(cut == h, values, 0.0) for h in range(CUTS)], axis=0)

    for i in range(steps):
        ready("first", i)
        x = chunk[:, here(i)].astype(F32).reshape(rows // GROUP, GROUP, STEP)
        c = (x - offset(i)).reshape(rows, STEP).astype(BF)
        cent[:, here(i)] = c
        w = jnp.concatenate(cut_columns(enc, i), axis=0)
        if i == 0:
            acc[...] = mm_t(w, c)
        else:
            acc[...] += mm_t(w, c)
    filled = flat(chunk[:, :128].astype(F32) < EMPTY / 2).astype(BF)
    valid = mm_t(flat(iota((8, 128), 1) == 0).astype(BF), filled)[:1] > 0.5
    pre = joined(acc[...]) + bias[...]
    gate = 1.0 / (1.0 + jnp.exp(-pre))
    latent = spread(jnp.where(valid, pre * gate, 0.0))
    latent_t = latent.astype(BF)
    latent_b = latent.T.astype(BF)
    ready("second", 0)
    for i in range(steps):
        w = jnp.concatenate(cut_columns(dec, i), axis=0)
        d = mm(latent_b, w).astype(BF).astype(F32).reshape(rows // GROUP, GROUP, STEP)
        x = chunk[:, here(i)].astype(F32).reshape(rows // GROUP, GROUP, STEP)
        e = ((offset(i) + d - x) * (1.0 / 32.0)).reshape(rows, STEP).astype(BF)
        err[:, here(i)] = e
        if i == 0:
            acc[...] = mm_t(w, e)
        else:
            acc[...] += mm_t(w, e)
    dlatent = joined(acc[...])
    dpre = spread(jnp.where(valid, dlatent * gate * (1.0 + pre * (1.0 - gate)), 0.0))
    dpre_t = dpre.astype(BF)
    ready("third", 0)
    for i in range(steps):
        store(i, 0, mm(dpre_t, cent[:, here(i)]))
        store(i, 1, mm(latent_t, err[:, here(i)]))


class Loader:
    def __init__(self, sems, first_row, chunk_in, enc_in, dec_in, chunk, enc, dec):
        self.sems = sems
        self.moves = {}
        part = chunk.shape[1]
        latents = enc.shape[0]
        rows = pl.ds(pl.multiple_of(first_row, latents), latents)
        for i in range(part // STEP):
            here = pl.ds(i * STEP, STEP)
            self.move(("chunk", i), chunk_in.at[:, here], chunk.at[:, here])
            for h in range(CUTS):
                columns = pl.ds(h * part + i * STEP, STEP)
                self.move(("enc", i, h), enc_in.at[rows, columns], enc.at[:, columns])
        self.move("second", dec_in.at[rows], dec)

    def move(self, key, source, target):
        self.moves[key] = pltpu.make_async_copy(source, target, self.sems.at[len(self.moves)])
        self.moves[key].start()

    def __call__(self, stage, i):
        if stage == "first":
            self.moves[("chunk", i)].wait()
            for h in range(CUTS):
                self.moves[("enc", i, h)].wait()
        elif stage in self.moves:
            self.moves[stage].wait()


def chunk_kernel(with_prior, at, chunk_in, enc_in, dec_in, bias, dec_bias, *refs):
    refs = list(refs)
    prior_in = refs.pop(0) if with_prior else None
    mine_out, other_out = refs.pop(0), refs.pop(0)
    flags = refs.pop(0) if with_prior else None
    chunk, enc, dec, cent, err, acc, sems, mine, other, sems_out = refs[:10]
    latents = enc.shape[0]
    core = at[0]
    ready = Loader(sems, at[1], chunk_in, enc_in, dec_in, chunk, enc, dec)
    if with_prior:
        prior, marks = refs[10:]
        ready.move("third", prior_in, prior)
        ready.move("marks", chunk_in.at[:, pl.ds(chunk.shape[1], EXTRA)], marks)

    def out_copy(which, grad):
        source, result = ((mine, mine_out), (other, other_out))[which]
        rows = pl.ds(grad * latents, latents)
        sem = sems_out.at[2 * which + grad]
        return pltpu.make_async_copy(source.at[:, rows], result.at[:, rows], sem)

    def store(i, grad, value):
        rows = slice(grad * latents, (grad + 1) * latents)
        cuts = [value[h * latents : (h + 1) * latents] for h in range(CUTS)]

        @pl.when(core == i)
        def _():
            for h in range(CUTS):
                mine[h, rows] = cuts[h] + prior[h, rows] if with_prior else cuts[h]
            out_copy(0, grad).start()

        @pl.when(core != i)
        def _():
            for h in range(CUTS):
                other[h, rows] = cuts[h].astype(other.dtype)
            out_copy(1, grad).start()

    gradient_body(chunk, enc, dec, bias, dec_bias, cent, err, acc, store, ready)
    if with_prior:
        ready("marks", 0)
        flags[0] = jnp.max(marks[...].astype(F32))
    for which in range(2):
        for grad in range(2):
            out_copy(which, grad).wait()


def vmem():
    return pl.BlockSpec(memory_space=pltpu.VMEM)


def anywhere():
    return pl.BlockSpec(memory_space=pl.ANY)


def hbm():
    return pl.BlockSpec(memory_space=pltpu.HBM)


def smem():
    return pl.BlockSpec(memory_space=pltpu.SMEM)


def on_device(tokens, dec_bias, enc_weight, enc_bias, dec_weight, block_ids, block_home):
    rows, width = tokens.shape
    lat_count = lax.axis_size("lat")
    groups = lax.axis_size("tok")
    chips = groups // 2
    targets = 2 * lat_count
    part = width // CUTS
    slot_rows = targets * GROUP
    latents = enc_weight.shape[0] // 2
    per_cut = part // STEP
    me = lax.axis_index("tok").astype(I32)
    core = me % 2
    first_row = (me // 2 % 2) * latents
    scalars = jnp.stack([core, first_row])
    exchange_groups = [
        [(4 * p + 2 * b + c) * lat_count + at for b in range(2) for at in range(lat_count)]
        for p in range(groups // 4)
        for c in range(2)
    ]
    chunk_shape = jax.ShapeDtypeStruct((slot_rows, part), BF)
    lent_shape = jax.ShapeDtypeStruct((max(LENT) * PIECES, STEP), BF)
    matmul_cost = pl.CostEstimate(
        flops=5 * 2 * slot_rows * CUTS * latents * part,
        bytes_accessed=12 * 2**20,
        transcendentals=0,
    )
    move_cost = pl.CostEstimate(
        flops=2 * slot_rows * CUTS * rows * part, bytes_accessed=5 * 2**20, transcendentals=0
    )

    ids_row = block_ids.reshape(1, rows)
    home_row = block_home.reshape(1, -1)
    chunk1 = pl.pallas_call(
        functools.partial(first_kernel, targets),
        out_shape=chunk_shape,
        in_specs=[anywhere()] * 3,
        out_specs=anywhere(),
        scratch_shapes=[
            pltpu.VMEM(ids_row.shape, I32),
            pltpu.VMEM(home_row.shape, I32),
            pltpu.VMEM((rows, width), BF),
            pltpu.VMEM((slot_rows, part), BF),
            pltpu.SemaphoreType.DMA((2 + CUTS * (part // FINE),)),
            pltpu.SemaphoreType.DMA((part // FINE,)),
        ],
        compiler_params=room(56),
        cost_estimate=move_cost,
        name="first_slots",
    )(ids_row, home_row, tokens)
    lent_a, lent_b = pl.pallas_call(
        functools.partial(lend_kernel, targets),
        out_shape=[lent_shape, lent_shape],
        in_specs=[vmem()] * 3,
        out_specs=[vmem()] * 2,
        compiler_params=room(20),
        cost_estimate=move_cost,
        name="lent_rows",
    )(ids_row, home_row, tokens)

    def exchange(chunk):
        shaped = chunk.reshape(targets, GROUP, chunk.shape[1])
        got = lax.all_to_all(
            shaped,
            ("tok", "lat"),
            split_axis=0,
            concat_axis=0,
            tiled=True,
            axis_index_groups=exchange_groups,
        )
        return got.reshape(chunk.shape)

    loans_a = lax.all_gather(lent_a, "tok", tiled=True)
    loans_a, lent_b = lax.optimization_barrier((loans_a, lent_b))
    loans_b = lax.all_gather(lent_b, "tok", tiled=True)
    got1 = exchange(chunk1)
    chunk2, left = pl.pallas_call(
        functools.partial(second_kernel, targets),
        out_shape=[
            jax.ShapeDtypeStruct((slot_rows, part + EXTRA), BF),
            jax.ShapeDtypeStruct((8, rows), I32),
        ],
        in_specs=[smem()] + [vmem()] * 3,
        out_specs=[vmem()] * 2,
        compiler_params=room(24),
        cost_estimate=move_cost,
        name="second_slots",
    )(me.reshape(1), tokens, loans_a, loans_b)
    got2 = exchange(chunk2)
    bias_row = lax.dynamic_slice_in_dim(enc_bias, first_row, latents).reshape(latents, 1)
    offset_row = dec_bias.reshape(1, width)
    half_shape = (CUTS, 2 * latents, STEP)

    def work(kind):
        return [
            pltpu.VMEM((slot_rows, part), BF),
            pltpu.VMEM((latents, width), BF),
            pltpu.VMEM((latents, width), BF),
            pltpu.VMEM((slot_rows, part), BF),
            pltpu.VMEM((slot_rows, part), BF),
            pltpu.VMEM((CUTS * latents, slot_rows), F32),
            pltpu.SemaphoreType.DMA((per_cut * (CUTS + 1) + 3,)),
            pltpu.VMEM(half_shape, F32),
            pltpu.VMEM(half_shape, kind),
            pltpu.SemaphoreType.DMA((4,)),
        ]

    def swap(values):
        return lax.ppermute(values, "tok", [(i, i ^ 1) for i in range(groups)])

    operands = (enc_weight, dec_weight, bias_row, offset_row)
    part_call = pl.pallas_call(
        functools.partial(chunk_kernel, False),
        out_shape=[jax.ShapeDtypeStruct(half_shape, F32)] * 2,
        in_specs=[smem()] + [hbm()] * 3 + [vmem()] * 2,
        out_specs=[hbm()] * 2,
        scratch_shapes=work(F32),
        compiler_params=room(56),
        cost_estimate=matmul_cost,
        name="chunk_gradients",
    )
    mine1, other1 = part_call(scalars, got1, *operands)
    prior = mine1 + swap(other1)
    mine, other, flags = pl.pallas_call(
        functools.partial(chunk_kernel, True),
        out_shape=[
            jax.ShapeDtypeStruct(half_shape, F32),
            jax.ShapeDtypeStruct(half_shape, BF),
            jax.ShapeDtypeStruct((1,), F32),
        ],
        in_specs=[smem(), anywhere()] + [hbm()] * 2 + [vmem()] * 2 + [hbm()],
        out_specs=[anywhere()] * 2 + [smem()],
        scratch_shapes=[
            *work(BF),
            pltpu.VMEM(half_shape, F32),
            pltpu.VMEM((slot_rows, EXTRA), BF),
        ],
        compiler_params=room(56),
        cost_estimate=matmul_cost,
        name="last_gradients",
    )(scalars, got2, *operands, prior)

    def rest(carry):
        mine, other, unused = carry
        codes, cut = slot_codes(targets, DIRECT)
        hit = flat(codes == left[:1])
        data = jnp.zeros((slot_rows, part), F32)
        for h in range(CUTS):
            chosen = jnp.where(cut == h, hit, 0.0).astype(BF)
            data = data + mm(chosen, tokens[:, h * part : (h + 1) * part])
        filled = jnp.sum(hit, axis=1, keepdims=True) > 0.5
        chunk3 = jnp.where(filled, data, EMPTY).astype(BF)
        more, more_other = part_call(scalars, exchange(chunk3), *operands)
        return mine + more, (other.astype(F32) + more_other).astype(BF), jnp.zeros((), F32)

    mine, other, unused = lax.while_loop(
        lambda carry: carry[2] > 0.5, rest, (mine, other, flags.reshape(()))
    )
    summed = (mine + swap(other).astype(F32)).astype(BF)
    terms = lax.all_to_all(
        summed,
        "tok",
        split_axis=0,
        concat_axis=0,
        tiled=True,
        axis_index_groups=[[2 * i + c for i in range(chips)] for c in range(2)],
    )
    terms = terms.reshape(chips // 2, 2, 2, latents, STEP)

    def summed_over_pairs(grad):
        total = terms[0, :, grad].astype(F32)
        for p in range(1, chips // 2):
            total = total + terms[p, :, grad].astype(F32)
        return total.reshape(2 * latents, STEP)

    return summed_over_pairs(0), summed_over_pairs(1)


def solution(mesh):
    in_specs = (
        P(("tok", "lat"), None),
        P(),
        P("lat", None),
        P("lat"),
        P("lat", None),
        P(("tok", "lat"), None),
        P(),
    )
    out_specs = (P("lat", "tok"), P("lat", "tok"))
    return jax.shard_map(
        on_device, mesh=mesh, in_specs=in_specs, out_specs=out_specs, check_vma=False
    )
```

```python
import functools

import jax
import jax.numpy as jnp
from jax import lax
from jax.experimental import pallas as pl
from jax.experimental.pallas import tpu as pltpu
from jax.sharding import PartitionSpec as P

BF = jnp.bfloat16
F32 = jnp.float32
I32 = jnp.int32

CUTS = 4
SLOTS = 2
DIRECT = 2 * SLOTS
GROUP = CUTS * SLOTS
STRIDE = 8
EMPTY = 2.0**100
EXTRA = 128
STEP = 1024
FINE = 512
PIECES = 8
LENT = (6, 7)


def room(mib):
    return pltpu.CompilerParams(vmem_limit_bytes=mib * 2**20)


def mm(a, b):
    return jnp.dot(a, b, preferred_element_type=F32)


def mm_t(a, b):
    return lax.dot_general(a, b, (((1,), (1,)), ((), ())), preferred_element_type=F32)


def iota(shape, axis):
    return lax.broadcasted_iota(I32, shape, axis)


def flat(mask):
    return jnp.where(mask, 1.0, 0.0)


def slot_codes(targets, first):
    row = iota((targets * GROUP, 1), 0)
    inner = row % GROUP
    return (row // GROUP) * STRIDE + first + inner % SLOTS, inner // SLOTS


def before(n):
    return (iota((n, n), 0) < iota((n, n), 1)).astype(F32).astype(BF)


def ranks_of(target, targets):
    g, n = target.shape
    members = flat(target[:, None, :] == iota((g, targets, n), 1))
    counts = mm(members.reshape(g * targets, n).astype(BF), before(n)).reshape(g, targets, n)
    return members, jnp.sum(members * counts, axis=1)


def target_of(places, targets):
    return (places & 1) * (targets // 2) + (places >> 1)


def cut_columns(ref, i, step=STEP):
    part = ref.shape[1] // CUTS
    return [ref[:, h * part + i * step : h * part + (i + 1) * step] for h in range(CUTS)]


def places_of(ids, home):
    total = home.shape[1]
    named = flat(iota((total, ids.shape[1]), 0) == ids[...]).astype(BF)
    table = jnp.broadcast_to(home[...], (8, total)).astype(F32).astype(BF)
    return mm(table, named)[:1].astype(I32)


def first_kernel(
    targets, ids_in, home_in, tokens_in, chunk_out, ids, home, tokens, chunk, sems_in, sems_out
):
    rows, width = tokens.shape
    part = width // CUTS
    steps = part // FINE
    loads = []

    def load(source, target):
        loads.append(pltpu.make_async_copy(source, target, sems_in.at[len(loads)]))
        loads[-1].start()

    load(ids_in, ids)
    load(home_in, home)
    for i in range(steps):
        for h in range(CUTS):
            columns = pl.ds(h * part + i * FINE, FINE)
            load(tokens_in.at[:, columns], tokens.at[:, columns])
    loads[0].wait()
    loads[1].wait()
    target = target_of(places_of(ids, home), targets)
    unused, rank = ranks_of(target, targets)
    codes, cut = slot_codes(targets, 0)
    hit = flat(codes == target * STRIDE + rank.astype(I32))
    wide = jnp.concatenate([jnp.where(cut == h, hit, 0.0) for h in range(CUTS)], axis=1)
    wide = wide.astype(BF)
    filled = jnp.sum(hit, axis=1, keepdims=True) > 0.5
    stores = []
    for i in range(steps):
        for h in range(CUTS):
            loads[2 + i * CUTS + h].wait()
        got = mm(wide, jnp.concatenate(cut_columns(tokens, i, FINE), axis=0))
        chunk[:, i * FINE : (i + 1) * FINE] = jnp.where(filled, got, EMPTY).astype(BF)
        columns = pl.ds(i * FINE, FINE)
        stores.append(
            pltpu.make_async_copy(chunk.at[:, columns], chunk_out.at[:, columns], sems_out.at[i])
        )
        stores[-1].start()
    for store in stores:
        store.wait()


def lend_kernel(targets, ids, home, tokens, lent_a, lent_b):
    rows = tokens.shape[0]
    places = places_of(ids, home)
    unused, rank = ranks_of(target_of(places, targets), targets)
    over = flat(rank.astype(I32) >= DIRECT)
    order = mm(jnp.broadcast_to(over, (8, rows)).astype(BF), before(rows))[:1].astype(I32)
    first = 0
    for count, lent in zip(LENT, (lent_a, lent_b)):
        lines = lent.shape[0]
        line = iota((lines, rows), 0)
        take = jnp.logical_and(order == first + line // PIECES, over > 0.5)
        take = flat(jnp.logical_and(take, line < count * PIECES))
        piece = iota((lines, 1), 0) % PIECES
        got = jnp.zeros((lines, STEP), F32)
        for i in range(PIECES):
            chosen = jnp.where(piece == i, take, 0.0).astype(BF)
            got = got + mm(chosen, tokens[:, i * STEP : (i + 1) * STEP])
        if first == 0:
            head = jnp.where(line == count * PIECES, places.astype(F32), got[:, :rows])
            got = jnp.concatenate([head, got[:, rows:]], axis=1)
        lent[...] = got.astype(BF)
        first += count


def second_kernel(targets, group, tokens, loans_a, loans_b, chunk, left):
    rows, width = tokens.shape
    part = width // CUTS
    lines = (LENT[0] + 1) * PIECES
    groups = loans_a.shape[0] // lines
    me = group[0]
    heads = loans_a[:, :rows].astype(F32).reshape(groups, lines, rows)
    places = heads[:, LENT[0] * PIECES, :].astype(I32)
    target = target_of(places, targets)
    members, rank_f = ranks_of(target, targets)
    rank = rank_f.astype(I32)
    over = rank >= DIRECT
    order = mm(flat(over).astype(BF), before(rows)).astype(I32)
    listed = jnp.logical_and(over, order < sum(LENT))
    count = jnp.sum(members, axis=2, keepdims=True)
    asked = jnp.sum(members * flat(listed)[:, None, :], axis=2, keepdims=True)
    used = jnp.maximum(count, float(SLOTS))
    free = jnp.maximum(DIRECT - used, 0.0)
    asked_before = []
    running = jnp.zeros((1, targets, 1), F32)
    free_total = jnp.zeros((1, targets, 1), F32)
    free_before = jnp.zeros((1, targets, 1), F32)
    for t in range(groups):
        asked_before.append(running)
        running = running + asked[t : t + 1]
        free_before = free_before + jnp.where(me > t, free[t : t + 1], 0.0)
        free_total = free_total + free[t : t + 1]
    mine = flat(iota((groups, 1, 1), 0) == me)
    my_free = jnp.sum(free * mine, axis=0, keepdims=True)
    my_used = jnp.sum(used * mine, axis=0, keepdims=True)

    def look(values):
        return jnp.sum(members * values, axis=1).astype(I32)

    in_pool = look(jnp.concatenate(asked_before, axis=0)) + rank - DIRECT
    placed = jnp.logical_and(listed, in_pool < look(free_total))
    at = in_pool - look(free_before)
    here = jnp.logical_and(placed, jnp.logical_and(at >= 0, at < look(my_free)))
    lent_code = jnp.where(here, target * STRIDE + look(my_used) + at, -1)
    size = groups * lines
    square = iota((size, size), 0) == iota((size, size), 1)
    line_of = iota((lines, rows), 0) // PIECES

    def codes_of_lines(first, count):
        columns = []
        for t in range(groups):
            chosen = jnp.logical_and(order[t : t + 1] == first + line_of, listed[t : t + 1])
            chosen = jnp.logical_and(chosen, line_of < count)
            value = jnp.where(chosen, lent_code[t : t + 1] + 1, 0)
            columns.append(jnp.sum(value, axis=1, keepdims=True) - 1)
        column = jnp.concatenate(columns, axis=0)
        return jnp.sum(jnp.where(square, column, 0), axis=0, keepdims=True)

    mine2 = (iota((groups, 1), 0) == me).astype(I32)
    own_code = jnp.sum((target * STRIDE + rank) * mine2, axis=0, keepdims=True)
    missing = jnp.logical_and(over, jnp.logical_not(placed)).astype(I32)
    own_missing = jnp.sum(missing * mine2, axis=0, keepdims=True)
    left[...] = jnp.broadcast_to(jnp.where(own_missing > 0, own_code, -1), left.shape)
    flag = jnp.max(jnp.max(missing.astype(F32), axis=1, keepdims=True), axis=0, keepdims=True)
    codes, cut = slot_codes(targets, SLOTS)
    hit = flat(codes == own_code)
    wide = jnp.concatenate([jnp.where(cut == h, hit, 0.0) for h in range(CUTS)], axis=1)
    wide = wide.astype(BF)
    hit_a = flat(codes == codes_of_lines(0, LENT[0]))
    hit_b = flat(codes == codes_of_lines(LENT[0], LENT[1]))
    filled = jnp.sum(hit, axis=1, keepdims=True) + jnp.sum(hit_a, axis=1, keepdims=True)
    filled = filled + jnp.sum(hit_b, axis=1, keepdims=True) > 0.5
    chunk[:, part:] = jnp.broadcast_to(flag, (hit.shape[0], EXTRA)).astype(BF)
    per_cut = part // STEP
    piece = iota((1, size), 1) % PIECES
    for i in range(per_cut):
        at_cut = cut * per_cut + i == piece
        got = mm(wide, jnp.concatenate(cut_columns(tokens, i), axis=0))
        got = got + mm(jnp.where(at_cut, hit_a, 0.0).astype(BF), loans_a[...])
        got = got + mm(jnp.where(at_cut, hit_b, 0.0).astype(BF), loans_b[...])
        chunk[:, i * STEP : (i + 1) * STEP] = jnp.where(filled, got, EMPTY).astype(BF)


def gradient_body(chunk, enc, dec, bias, dec_bias, cent, err, acc, store, ready):
    rows, part = chunk.shape
    latents = enc.shape[0]
    steps = part // STEP
    inner = iota((1, rows), 1) % GROUP
    cut = inner // SLOTS
    cut8 = iota((GROUP, 1), 0) // SLOTS

    def here(i):
        return slice(i * STEP, (i + 1) * STEP)

    def offset(i):
        value = jnp.zeros((GROUP, STEP), F32)
        for h, columns in enumerate(cut_columns(dec_bias, i)):
            value = jnp.where(cut8 == h, columns, value)
        return value[None]

    def joined(total):
        own = total[:latents]
        for h in range(1, CUTS):
            own = jnp.where(cut == h, total[h * latents : (h + 1) * latents], own)
        shift = GROUP // 2
        while shift >= SLOTS:
            down = pltpu.roll(own, rows - shift, 1)
            wrapped = pltpu.roll(own, GROUP - shift, 1)
            own = own + jnp.where(inner < GROUP - shift, down, wrapped)
            shift //= 2
        return own

    def spread(values):
        return jnp.concatenate([jnp.where(cut == h, values, 0.0) for h in range(CUTS)], axis=0)

    for i in range(steps):
        ready("first", i)
        x = chunk[:, here(i)].astype(F32).reshape(rows // GROUP, GROUP, STEP)
        c = (x - offset(i)).reshape(rows, STEP).astype(BF)
        cent[:, here(i)] = c
        w = jnp.concatenate(cut_columns(enc, i), axis=0)
        if i == 0:
            acc[...] = mm_t(w, c)
        else:
            acc[...] += mm_t(w, c)
    filled = flat(chunk[:, :128].astype(F32) < EMPTY / 2).astype(BF)
    valid = mm_t(flat(iota((8, 128), 1) == 0).astype(BF), filled)[:1] > 0.5
    pre = joined(acc[...]) + bias[...]
    gate = 1.0 / (1.0 + jnp.exp(-pre))
    latent = spread(jnp.where(valid, pre * gate, 0.0))
    latent_t = latent.astype(BF)
    latent_b = latent.T.astype(BF)
    ready("second", 0)
    for i in range(steps):
        w = jnp.concatenate(cut_columns(dec, i), axis=0)
        d = mm(latent_b, w).astype(BF).astype(F32).reshape(rows // GROUP, GROUP, STEP)
        x = chunk[:, here(i)].astype(F32).reshape(rows // GROUP, GROUP, STEP)
        e = ((offset(i) + d - x) * (1.0 / 32.0)).reshape(rows, STEP).astype(BF)
        err[:, here(i)] = e
        if i == 0:
            acc[...] = mm_t(w, e)
        else:
            acc[...] += mm_t(w, e)
    dlatent = joined(acc[...])
    dpre = spread(jnp.where(valid, dlatent * gate * (1.0 + pre * (1.0 - gate)), 0.0))
    dpre_t = dpre.astype(BF)
    ready("third", 0)
    for i in range(steps):
        store(i, 0, mm(dpre_t, cent[:, here(i)]))
        store(i, 1, mm(latent_t, err[:, here(i)]))


class Loader:
    def __init__(self, sems, first_row, chunk_in, enc_in, dec_in, chunk, enc, dec):
        self.sems = sems
        self.moves = {}
        part = chunk.shape[1]
        latents = enc.shape[0]
        rows = pl.ds(pl.multiple_of(first_row, latents), latents)
        for i in range(part // STEP):
            here = pl.ds(i * STEP, STEP)
            self.move(("chunk", i), chunk_in.at[:, here], chunk.at[:, here])
            for h in range(CUTS):
                columns = pl.ds(h * part + i * STEP, STEP)
                self.move(("enc", i, h), enc_in.at[rows, columns], enc.at[:, columns])
        self.move("second", dec_in.at[rows], dec)

    def move(self, key, source, target):
        self.moves[key] = pltpu.make_async_copy(source, target, self.sems.at[len(self.moves)])
        self.moves[key].start()

    def __call__(self, stage, i):
        if stage == "first":
            self.moves[("chunk", i)].wait()
            for h in range(CUTS):
                self.moves[("enc", i, h)].wait()
        elif stage in self.moves:
            self.moves[stage].wait()


def chunk_kernel(with_prior, at, chunk_in, enc_in, dec_in, bias, dec_bias, *refs):
    refs = list(refs)
    prior_in = refs.pop(0) if with_prior else None
    mine_out, other_out = refs.pop(0), refs.pop(0)
    flags = refs.pop(0) if with_prior else None
    chunk, enc, dec, cent, err, acc, sems, mine, other, sems_out = refs[:10]
    latents = enc.shape[0]
    core = at[0]
    ready = Loader(sems, at[1], chunk_in, enc_in, dec_in, chunk, enc, dec)
    if with_prior:
        prior, marks = refs[10:]
        ready.move("third", prior_in, prior)
        ready.move("marks", chunk_in.at[:, pl.ds(chunk.shape[1], EXTRA)], marks)

    def out_copy(which, grad):
        source, result = ((mine, mine_out), (other, other_out))[which]
        rows = pl.ds(grad * latents, latents)
        sem = sems_out.at[2 * which + grad]
        return pltpu.make_async_copy(source.at[:, rows], result.at[:, rows], sem)

    def store(i, grad, value):
        rows = slice(grad * latents, (grad + 1) * latents)
        cuts = [value[h * latents : (h + 1) * latents] for h in range(CUTS)]

        @pl.when(core == i)
        def _():
            for h in range(CUTS):
                mine[h, rows] = cuts[h] + prior[h, rows] if with_prior else cuts[h]
            out_copy(0, grad).start()

        @pl.when(core != i)
        def _():
            for h in range(CUTS):
                other[h, rows] = cuts[h].astype(other.dtype)
            out_copy(1, grad).start()

    gradient_body(chunk, enc, dec, bias, dec_bias, cent, err, acc, store, ready)
    if with_prior:
        ready("marks", 0)
        flags[0] = jnp.max(marks[...].astype(F32))
    for which in range(2):
        for grad in range(2):
            out_copy(which, grad).wait()


def vmem():
    return pl.BlockSpec(memory_space=pltpu.VMEM)


def anywhere():
    return pl.BlockSpec(memory_space=pl.ANY)


def hbm():
    return pl.BlockSpec(memory_space=pltpu.HBM)


def smem():
    return pl.BlockSpec(memory_space=pltpu.SMEM)


def on_device(tokens, dec_bias, enc_weight, enc_bias, dec_weight, block_ids, block_home):
    rows, width = tokens.shape
    lat_count = lax.axis_size("lat")
    groups = lax.axis_size("tok")
    chips = groups // 2
    targets = 2 * lat_count
    part = width // CUTS
    slot_rows = targets * GROUP
    latents = enc_weight.shape[0] // 2
    per_cut = part // STEP
    me = lax.axis_index("tok").astype(I32)
    core = me % 2
    first_row = (me // 2 % 2) * latents
    scalars = jnp.stack([core, first_row])
    exchange_groups = [
        [(4 * p + 2 * b + c) * lat_count + at for b in range(2) for at in range(lat_count)]
        for p in range(groups // 4)
        for c in range(2)
    ]
    chunk_shape = jax.ShapeDtypeStruct((slot_rows, part), BF)
    lent_shape = jax.ShapeDtypeStruct((max(LENT) * PIECES, STEP), BF)
    matmul_cost = pl.CostEstimate(
        flops=5 * 2 * slot_rows * CUTS * latents * part,
        bytes_accessed=12 * 2**20,
        transcendentals=0,
    )
    move_cost = pl.CostEstimate(
        flops=2 * slot_rows * CUTS * rows * part, bytes_accessed=5 * 2**20, transcendentals=0
    )

    ids_row = block_ids.reshape(1, rows)
    home_row = block_home.reshape(1, -1)
    chunk1 = pl.pallas_call(
        functools.partial(first_kernel, targets),
        out_shape=chunk_shape,
        in_specs=[anywhere()] * 3,
        out_specs=anywhere(),
        scratch_shapes=[
            pltpu.VMEM(ids_row.shape, I32),
            pltpu.VMEM(home_row.shape, I32),
            pltpu.VMEM((rows, width), BF),
            pltpu.VMEM((slot_rows, part), BF),
            pltpu.SemaphoreType.DMA((2 + CUTS * (part // FINE),)),
            pltpu.SemaphoreType.DMA((part // FINE,)),
        ],
        compiler_params=room(56),
        cost_estimate=move_cost,
        name="first_slots",
    )(ids_row, home_row, tokens)
    lent_a, lent_b = pl.pallas_call(
        functools.partial(lend_kernel, targets),
        out_shape=[lent_shape, lent_shape],
        in_specs=[vmem()] * 3,
        out_specs=[vmem()] * 2,
        compiler_params=room(20),
        cost_estimate=move_cost,
        name="lent_rows",
    )(ids_row, home_row, tokens)

    def exchange(chunk):
        shaped = chunk.reshape(targets, GROUP, chunk.shape[1])
        got = lax.all_to_all(
            shaped,
            ("tok", "lat"),
            split_axis=0,
            concat_axis=0,
            tiled=True,
            axis_index_groups=exchange_groups,
        )
        return got.reshape(chunk.shape)

    loans_a = lax.all_gather(lent_a, "tok", tiled=True)
    loans_a, lent_b = lax.optimization_barrier((loans_a, lent_b))
    loans_b = lax.all_gather(lent_b, "tok", tiled=True)
    got1 = exchange(chunk1)
    chunk2, left = pl.pallas_call(
        functools.partial(second_kernel, targets),
        out_shape=[
            jax.ShapeDtypeStruct((slot_rows, part + EXTRA), BF),
            jax.ShapeDtypeStruct((8, rows), I32),
        ],
        in_specs=[smem()] + [vmem()] * 3,
        out_specs=[vmem()] * 2,
        compiler_params=room(24),
        cost_estimate=move_cost,
        name="second_slots",
    )(me.reshape(1), tokens, loans_a, loans_b)
    got2 = exchange(chunk2)
    bias_row = lax.dynamic_slice_in_dim(enc_bias, first_row, latents).reshape(latents, 1)
    offset_row = dec_bias.reshape(1, width)
    half_shape = (CUTS, 2 * latents, STEP)

    def work(kind):
        return [
            pltpu.VMEM((slot_rows, part), BF),
            pltpu.VMEM((latents, width), BF),
            pltpu.VMEM((latents, width), BF),
            pltpu.VMEM((slot_rows, part), BF),
            pltpu.VMEM((slot_rows, part), BF),
            pltpu.VMEM((CUTS * latents, slot_rows), F32),
            pltpu.SemaphoreType.DMA((per_cut * (CUTS + 1) + 3,)),
            pltpu.VMEM(half_shape, F32),
            pltpu.VMEM(half_shape, kind),
            pltpu.SemaphoreType.DMA((4,)),
        ]

    def swap(values):
        return lax.ppermute(values, "tok", [(i, i ^ 1) for i in range(groups)])

    operands = (enc_weight, dec_weight, bias_row, offset_row)
    part_call = pl.pallas_call(
        functools.partial(chunk_kernel, False),
        out_shape=[jax.ShapeDtypeStruct(half_shape, F32)] * 2,
        in_specs=[smem()] + [hbm()] * 3 + [vmem()] * 2,
        out_specs=[hbm()] * 2,
        scratch_shapes=work(F32),
        compiler_params=room(56),
        cost_estimate=matmul_cost,
        name="chunk_gradients",
    )
    mine1, other1 = part_call(scalars, got1, *operands)
    prior = mine1 + swap(other1)
    mine, other, flags = pl.pallas_call(
        functools.partial(chunk_kernel, True),
        out_shape=[
            jax.ShapeDtypeStruct(half_shape, F32),
            jax.ShapeDtypeStruct(half_shape, BF),
            jax.ShapeDtypeStruct((1,), F32),
        ],
        in_specs=[smem(), anywhere()] + [hbm()] * 2 + [vmem()] * 2 + [hbm()],
        out_specs=[anywhere()] * 2 + [smem()],
        scratch_shapes=[
            *work(BF),
            pltpu.VMEM(half_shape, F32),
            pltpu.VMEM((slot_rows, EXTRA), BF),
        ],
        input_output_aliases={6: 0},
        compiler_params=room(46),
        cost_estimate=matmul_cost,
        name="last_gradients",
    )(scalars, got2, *operands, prior)

    def rest(carry):
        mine, other, unused = carry
        codes, cut = slot_codes(targets, DIRECT)
        hit = flat(codes == left[:1])
        data = jnp.zeros((slot_rows, part), F32)
        for h in range(CUTS):
            chosen = jnp.where(cut == h, hit, 0.0).astype(BF)
            data = data + mm(chosen, tokens[:, h * part : (h + 1) * part])
        filled = jnp.sum(hit, axis=1, keepdims=True) > 0.5
        chunk3 = jnp.where(filled, data, EMPTY).astype(BF)
        more, more_other = part_call(scalars, exchange(chunk3), *operands)
        return mine + more, (other.astype(F32) + more_other).astype(BF), jnp.zeros((), F32)

    mine, other, unused = lax.while_loop(
        lambda carry: carry[2] > 0.5, rest, (mine, other, flags.reshape(()))
    )
    summed = (mine + swap(other).astype(F32)).astype(BF)
    terms = lax.all_to_all(
        summed,
        "tok",
        split_axis=0,
        concat_axis=0,
        tiled=True,
        axis_index_groups=[[2 * i + c for i in range(chips)] for c in range(2)],
    )
    terms = terms.reshape(chips // 2, 2, 2, latents, STEP)

    def summed_over_pairs(grad):
        total = terms[0, :, grad].astype(F32)
        for p in range(1, chips // 2):
            total = total + terms[p, :, grad].astype(F32)
        return total.reshape(2 * latents, STEP)

    return summed_over_pairs(0), summed_over_pairs(1)


def solution(mesh):
    in_specs = (
        P(("tok", "lat"), None),
        P(),
        P("lat", None),
        P("lat"),
        P("lat", None),
        P(("tok", "lat"), None),
        P(),
    )
    out_specs = (P("lat", "tok"), P("lat", "tok"))
    return jax.shard_map(
        on_device, mesh=mesh, in_specs=in_specs, out_specs=out_specs, check_vma=False
    )
```

```python
import functools

import jax
import jax.numpy as jnp
from jax import lax
from jax.experimental import pallas as pl
from jax.experimental.pallas import tpu as pltpu
from jax.sharding import PartitionSpec as P

BF = jnp.bfloat16
F32 = jnp.float32
I32 = jnp.int32

CUTS = 4
SLOTS = 2
DIRECT = 2 * SLOTS
GROUP = CUTS * SLOTS
STRIDE = 8
EMPTY = 2.0**100
EXTRA = 128
STEP = 1024
FINE = 512
PIECES = 8
LENT = (6, 7)


def room(mib):
    return pltpu.CompilerParams(vmem_limit_bytes=mib * 2**20)


def mm(a, b):
    return jnp.dot(a, b, preferred_element_type=F32)


def mm_t(a, b):
    return lax.dot_general(a, b, (((1,), (1,)), ((), ())), preferred_element_type=F32)


def iota(shape, axis):
    return lax.broadcasted_iota(I32, shape, axis)


def flat(mask):
    return jnp.where(mask, 1.0, 0.0)


def slot_codes(targets, first):
    row = iota((targets * GROUP, 1), 0)
    inner = row % GROUP
    return (row // GROUP) * STRIDE + first + inner % SLOTS, inner // SLOTS


def before(n):
    return (iota((n, n), 0) < iota((n, n), 1)).astype(F32).astype(BF)


def ranks_of(target, targets):
    g, n = target.shape
    members = flat(target[:, None, :] == iota((g, targets, n), 1))
    counts = mm(members.reshape(g * targets, n).astype(BF), before(n)).reshape(g, targets, n)
    return members, jnp.sum(members * counts, axis=1)


def target_of(places, targets):
    return (places & 1) * (targets // 2) + (places >> 1)


def cut_columns(ref, i, step=STEP):
    part = ref.shape[1] // CUTS
    return [ref[:, h * part + i * step : h * part + (i + 1) * step] for h in range(CUTS)]


def places_of(ids, home):
    total = home.shape[1]
    named = flat(iota((total, ids.shape[1]), 0) == ids[...]).astype(BF)
    table = jnp.broadcast_to(home[...], (8, total)).astype(F32).astype(BF)
    return mm(table, named)[:1].astype(I32)


def first_kernel(
    targets, ids_in, home_in, tokens_in, chunk_out, ids, home, tokens, chunk, sems_in, sems_out
):
    rows, width = tokens.shape
    part = width // CUTS
    steps = part // FINE
    loads = []

    def load(source, target):
        loads.append(pltpu.make_async_copy(source, target, sems_in.at[len(loads)]))
        loads[-1].start()

    load(ids_in, ids)
    load(home_in, home)
    for i in range(steps):
        for h in range(CUTS):
            columns = pl.ds(h * part + i * FINE, FINE)
            load(tokens_in.at[:, columns], tokens.at[:, columns])
    loads[0].wait()
    loads[1].wait()
    target = target_of(places_of(ids, home), targets)
    unused, rank = ranks_of(target, targets)
    codes, cut = slot_codes(targets, 0)
    hit = flat(codes == target * STRIDE + rank.astype(I32))
    wide = jnp.concatenate([jnp.where(cut == h, hit, 0.0) for h in range(CUTS)], axis=1)
    wide = wide.astype(BF)
    filled = jnp.sum(hit, axis=1, keepdims=True) > 0.5
    stores = []
    for i in range(steps):
        for h in range(CUTS):
            loads[2 + i * CUTS + h].wait()
        got = mm(wide, jnp.concatenate(cut_columns(tokens, i, FINE), axis=0))
        chunk[:, i * FINE : (i + 1) * FINE] = jnp.where(filled, got, EMPTY).astype(BF)
        columns = pl.ds(i * FINE, FINE)
        stores.append(
            pltpu.make_async_copy(chunk.at[:, columns], chunk_out.at[:, columns], sems_out.at[i])
        )
        stores[-1].start()
    for store in stores:
        store.wait()


def lend_kernel(targets, ids, home, tokens, lent_a, lent_b):
    rows = tokens.shape[0]
    places = places_of(ids, home)
    unused, rank = ranks_of(target_of(places, targets), targets)
    over = flat(rank.astype(I32) >= DIRECT)
    order = mm(jnp.broadcast_to(over, (8, rows)).astype(BF), before(rows))[:1].astype(I32)
    first = 0
    for count, lent in zip(LENT, (lent_a, lent_b)):
        lines = lent.shape[0]
        line = iota((lines, rows), 0)
        take = jnp.logical_and(order == first + line // PIECES, over > 0.5)
        take = flat(jnp.logical_and(take, line < count * PIECES))
        piece = iota((lines, 1), 0) % PIECES
        got = jnp.zeros((lines, STEP), F32)
        for i in range(PIECES):
            chosen = jnp.where(piece == i, take, 0.0).astype(BF)
            got = got + mm(chosen, tokens[:, i * STEP : (i + 1) * STEP])
        if first == 0:
            head = jnp.where(line == count * PIECES, places.astype(F32), got[:, :rows])
            got = jnp.concatenate([head, got[:, rows:]], axis=1)
        lent[...] = got.astype(BF)
        first += count


def second_kernel(targets, group, tokens, loans_a, loans_b, chunk, left):
    rows, width = tokens.shape
    part = width // CUTS
    lines = (LENT[0] + 1) * PIECES
    groups = loans_a.shape[0] // lines
    me = group[0]
    heads = loans_a[:, :rows].astype(F32).reshape(groups, lines, rows)
    places = heads[:, LENT[0] * PIECES, :].astype(I32)
    target = target_of(places, targets)
    members, rank_f = ranks_of(target, targets)
    rank = rank_f.astype(I32)
    over = rank >= DIRECT
    order = mm(flat(over).astype(BF), before(rows)).astype(I32)
    listed = jnp.logical_and(over, order < sum(LENT))
    count = jnp.sum(members, axis=2, keepdims=True)
    asked = jnp.sum(members * flat(listed)[:, None, :], axis=2, keepdims=True)
    used = jnp.maximum(count, float(SLOTS))
    free = jnp.maximum(DIRECT - used, 0.0)
    asked_before = []
    running = jnp.zeros((1, targets, 1), F32)
    free_total = jnp.zeros((1, targets, 1), F32)
    free_before = jnp.zeros((1, targets, 1), F32)
    for t in range(groups):
        asked_before.append(running)
        running = running + asked[t : t + 1]
        free_before = free_before + jnp.where(me > t, free[t : t + 1], 0.0)
        free_total = free_total + free[t : t + 1]
    mine = flat(iota((groups, 1, 1), 0) == me)
    my_free = jnp.sum(free * mine, axis=0, keepdims=True)
    my_used = jnp.sum(used * mine, axis=0, keepdims=True)

    def look(values):
        return jnp.sum(members * values, axis=1).astype(I32)

    in_pool = look(jnp.concatenate(asked_before, axis=0)) + rank - DIRECT
    placed = jnp.logical_and(listed, in_pool < look(free_total))
    at = in_pool - look(free_before)
    here = jnp.logical_and(placed, jnp.logical_and(at >= 0, at < look(my_free)))
    lent_code = jnp.where(here, target * STRIDE + look(my_used) + at, -1)
    size = groups * lines
    square = iota((size, size), 0) == iota((size, size), 1)
    line_of = iota((lines, rows), 0) // PIECES

    def codes_of_lines(first, count):
        columns = []
        for t in range(groups):
            chosen = jnp.logical_and(order[t : t + 1] == first + line_of, listed[t : t + 1])
            chosen = jnp.logical_and(chosen, line_of < count)
            value = jnp.where(chosen, lent_code[t : t + 1] + 1, 0)
            columns.append(jnp.sum(value, axis=1, keepdims=True) - 1)
        column = jnp.concatenate(columns, axis=0)
        return jnp.sum(jnp.where(square, column, 0), axis=0, keepdims=True)

    mine2 = (iota((groups, 1), 0) == me).astype(I32)
    own_code = jnp.sum((target * STRIDE + rank) * mine2, axis=0, keepdims=True)
    missing = jnp.logical_and(over, jnp.logical_not(placed)).astype(I32)
    own_missing = jnp.sum(missing * mine2, axis=0, keepdims=True)
    left[...] = jnp.broadcast_to(jnp.where(own_missing > 0, own_code, -1), left.shape)
    flag = jnp.max(jnp.max(missing.astype(F32), axis=1, keepdims=True), axis=0, keepdims=True)
    codes, cut = slot_codes(targets, SLOTS)
    hit = flat(codes == own_code)
    wide = jnp.concatenate([jnp.where(cut == h, hit, 0.0) for h in range(CUTS)], axis=1)
    wide = wide.astype(BF)
    hit_a = flat(codes == codes_of_lines(0, LENT[0]))
    hit_b = flat(codes == codes_of_lines(LENT[0], LENT[1]))
    filled = jnp.sum(hit, axis=1, keepdims=True) + jnp.sum(hit_a, axis=1, keepdims=True)
    filled = filled + jnp.sum(hit_b, axis=1, keepdims=True) > 0.5
    chunk[:, part:] = jnp.broadcast_to(flag, (hit.shape[0], EXTRA)).astype(BF)
    per_cut = part // STEP
    piece = iota((1, size), 1) % PIECES
    for i in range(per_cut):
        at_cut = cut * per_cut + i == piece
        got = mm(wide, jnp.concatenate(cut_columns(tokens, i), axis=0))
        got = got + mm(jnp.where(at_cut, hit_a, 0.0).astype(BF), loans_a[...])
        got = got + mm(jnp.where(at_cut, hit_b, 0.0).astype(BF), loans_b[...])
        chunk[:, i * STEP : (i + 1) * STEP] = jnp.where(filled, got, EMPTY).astype(BF)


def gradient_body(chunk, enc, dec, bias, dec_bias, cent, err, acc, store, ready):
    rows, part = chunk.shape
    latents = enc.shape[0]
    steps = part // STEP
    inner = iota((1, rows), 1) % GROUP
    cut = inner // SLOTS
    cut8 = iota((GROUP, 1), 0) // SLOTS

    def here(i):
        return slice(i * STEP, (i + 1) * STEP)

    def offset(i):
        value = jnp.zeros((GROUP, STEP), F32)
        for h, columns in enumerate(cut_columns(dec_bias, i)):
            value = jnp.where(cut8 == h, columns, value)
        return value[None]

    def joined(total):
        own = total[:latents]
        for h in range(1, CUTS):
            own = jnp.where(cut == h, total[h * latents : (h + 1) * latents], own)
        shift = GROUP // 2
        while shift >= SLOTS:
            down = pltpu.roll(own, rows - shift, 1)
            wrapped = pltpu.roll(own, GROUP - shift, 1)
            own = own + jnp.where(inner < GROUP - shift, down, wrapped)
            shift //= 2
        return own

    def spread(values):
        return jnp.concatenate([jnp.where(cut == h, values, 0.0) for h in range(CUTS)], axis=0)

    for i in range(steps):
        ready("first", i)
        x = chunk[:, here(i)].astype(F32).reshape(rows // GROUP, GROUP, STEP)
        c = (x - offset(i)).reshape(rows, STEP).astype(BF)
        cent[:, here(i)] = c
        w = jnp.concatenate(cut_columns(enc, i), axis=0)
        if i == 0:
            acc[...] = mm_t(w, c)
        else:
            acc[...] += mm_t(w, c)
    filled = flat(chunk[:, :128].astype(F32) < EMPTY / 2).astype(BF)
    valid = mm_t(flat(iota((8, 128), 1) == 0).astype(BF), filled)[:1] > 0.5
    pre = joined(acc[...]) + bias[...]
    gate = 1.0 / (1.0 + jnp.exp(-pre))
    latent = spread(jnp.where(valid, pre * gate, 0.0))
    latent_t = latent.astype(BF)
    latent_b = latent.T.astype(BF)
    ready("second", 0)
    for i in range(steps):
        w = jnp.concatenate(cut_columns(dec, i), axis=0)
        d = mm(latent_b, w).astype(BF).astype(F32).reshape(rows // GROUP, GROUP, STEP)
        x = chunk[:, here(i)].astype(F32).reshape(rows // GROUP, GROUP, STEP)
        e = ((offset(i) + d - x) * (1.0 / 32.0)).reshape(rows, STEP).astype(BF)
        err[:, here(i)] = e
        if i == 0:
            acc[...] = mm_t(w, e)
        else:
            acc[...] += mm_t(w, e)
    dlatent = joined(acc[...])
    dpre = spread(jnp.where(valid, dlatent * gate * (1.0 + pre * (1.0 - gate)), 0.0))
    dpre_t = dpre.astype(BF)
    ready("third", 0)
    for i in range(steps):
        store(i, 0, mm(dpre_t, cent[:, here(i)]))
        store(i, 1, mm(latent_t, err[:, here(i)]))


class Loader:
    def __init__(self, sems, first_row, chunk_in, enc_in, dec_in, chunk, enc, dec):
        self.sems = sems
        self.moves = {}
        part = chunk.shape[1]
        latents = enc.shape[0]
        rows = pl.ds(pl.multiple_of(first_row, latents), latents)
        for i in range(part // STEP):
            here = pl.ds(i * STEP, STEP)
            if chunk_in is not None:
                self.move(("chunk", i), chunk_in.at[:, here], chunk.at[:, here])
            for h in range(CUTS):
                columns = pl.ds(h * part + i * STEP, STEP)
                self.move(("enc", i, h), enc_in.at[rows, columns], enc.at[:, columns])
        self.move("second", dec_in.at[rows], dec)

    def move(self, key, source, target):
        self.moves[key] = pltpu.make_async_copy(source, target, self.sems.at[len(self.moves)])
        self.moves[key].start()

    def __call__(self, stage, i):
        if stage == "first":
            if ("chunk", i) in self.moves:
                self.moves[("chunk", i)].wait()
            for h in range(CUTS):
                self.moves[("enc", i, h)].wait()
        elif stage in self.moves:
            self.moves[stage].wait()


def chunk_kernel(with_prior, at, chunk_in, enc_in, dec_in, bias, dec_bias, *refs):
    refs = list(refs)
    prior_in = refs.pop(0) if with_prior else None
    mine_out, other_out = refs.pop(0), refs.pop(0)
    flags = refs.pop(0) if with_prior else None
    chunk, enc, dec, cent, err, acc, sems, mine, other, sems_out = refs[:10]
    latents = enc.shape[0]
    core = at[0]
    received = chunk_in
    if with_prior:
        chunk, chunk_in = received.at[:, pl.ds(0, chunk.shape[1])], None
    ready = Loader(sems, at[1], chunk_in, enc_in, dec_in, chunk, enc, dec)
    if with_prior:
        prior = refs[10]
        ready.move("third", prior_in, prior)

    def out_copy(which, grad):
        source, result = ((mine, mine_out), (other, other_out))[which]
        rows = pl.ds(grad * latents, latents)
        sem = sems_out.at[2 * which + grad]
        return pltpu.make_async_copy(source.at[:, rows], result.at[:, rows], sem)

    def store(i, grad, value):
        rows = slice(grad * latents, (grad + 1) * latents)
        cuts = [value[h * latents : (h + 1) * latents] for h in range(CUTS)]

        @pl.when(core == i)
        def _():
            for h in range(CUTS):
                mine[h, rows] = cuts[h] + prior[h, rows] if with_prior else cuts[h]
            out_copy(0, grad).start()

        @pl.when(core != i)
        def _():
            for h in range(CUTS):
                other[h, rows] = cuts[h].astype(other.dtype)
            out_copy(1, grad).start()

    gradient_body(chunk, enc, dec, bias, dec_bias, cent, err, acc, store, ready)
    if with_prior:
        flags[0] = jnp.max(received[:, chunk.shape[1] :].astype(F32))
    for which in range(2):
        for grad in range(2):
            out_copy(which, grad).wait()


def vmem():
    return pl.BlockSpec(memory_space=pltpu.VMEM)


def anywhere():
    return pl.BlockSpec(memory_space=pl.ANY)


def hbm():
    return pl.BlockSpec(memory_space=pltpu.HBM)


def smem():
    return pl.BlockSpec(memory_space=pltpu.SMEM)


def on_device(tokens, dec_bias, enc_weight, enc_bias, dec_weight, block_ids, block_home):
    rows, width = tokens.shape
    lat_count = lax.axis_size("lat")
    groups = lax.axis_size("tok")
    chips = groups // 2
    targets = 2 * lat_count
    part = width // CUTS
    slot_rows = targets * GROUP
    latents = enc_weight.shape[0] // 2
    per_cut = part // STEP
    me = lax.axis_index("tok").astype(I32)
    core = me % 2
    first_row = (me // 2 % 2) * latents
    scalars = jnp.stack([core, first_row])
    exchange_groups = [
        [(4 * p + 2 * b + c) * lat_count + at for b in range(2) for at in range(lat_count)]
        for p in range(groups // 4)
        for c in range(2)
    ]
    chunk_shape = jax.ShapeDtypeStruct((slot_rows, part), BF)
    lent_shape = jax.ShapeDtypeStruct((max(LENT) * PIECES, STEP), BF)
    matmul_cost = pl.CostEstimate(
        flops=5 * 2 * slot_rows * CUTS * latents * part,
        bytes_accessed=12 * 2**20,
        transcendentals=0,
    )
    move_cost = pl.CostEstimate(
        flops=2 * slot_rows * CUTS * rows * part, bytes_accessed=5 * 2**20, transcendentals=0
    )

    ids_row = block_ids.reshape(1, rows)
    home_row = block_home.reshape(1, -1)
    chunk1 = pl.pallas_call(
        functools.partial(first_kernel, targets),
        out_shape=chunk_shape,
        in_specs=[anywhere()] * 3,
        out_specs=anywhere(),
        scratch_shapes=[
            pltpu.VMEM(ids_row.shape, I32),
            pltpu.VMEM(home_row.shape, I32),
            pltpu.VMEM((rows, width), BF),
            pltpu.VMEM((slot_rows, part), BF),
            pltpu.SemaphoreType.DMA((2 + CUTS * (part // FINE),)),
            pltpu.SemaphoreType.DMA((part // FINE,)),
        ],
        compiler_params=room(56),
        cost_estimate=move_cost,
        name="first_slots",
    )(ids_row, home_row, tokens)
    lent_a, lent_b = pl.pallas_call(
        functools.partial(lend_kernel, targets),
        out_shape=[lent_shape, lent_shape],
        in_specs=[vmem()] * 3,
        out_specs=[vmem()] * 2,
        compiler_params=room(20),
        cost_estimate=move_cost,
        name="lent_rows",
    )(ids_row, home_row, tokens)

    def exchange(chunk):
        shaped = chunk.reshape(targets, GROUP, chunk.shape[1])
        got = lax.all_to_all(
            shaped,
            ("tok", "lat"),
            split_axis=0,
            concat_axis=0,
            tiled=True,
            axis_index_groups=exchange_groups,
        )
        return got.reshape(chunk.shape)

    loans_a = lax.all_gather(lent_a, "tok", tiled=True)
    loans_a, lent_b = lax.optimization_barrier((loans_a, lent_b))
    loans_b = lax.all_gather(lent_b, "tok", tiled=True)
    got1 = exchange(chunk1)
    chunk2, left = pl.pallas_call(
        functools.partial(second_kernel, targets),
        out_shape=[
            jax.ShapeDtypeStruct((slot_rows, part + EXTRA), BF),
            jax.ShapeDtypeStruct((8, rows), I32),
        ],
        in_specs=[smem()] + [vmem()] * 3,
        out_specs=[vmem()] * 2,
        compiler_params=room(24),
        cost_estimate=move_cost,
        name="second_slots",
    )(me.reshape(1), tokens, loans_a, loans_b)
    got2 = exchange(chunk2)
    bias_row = lax.dynamic_slice_in_dim(enc_bias, first_row, latents).reshape(latents, 1)
    offset_row = dec_bias.reshape(1, width)
    half_shape = (CUTS, 2 * latents, STEP)

    def work(kind):
        return [
            pltpu.VMEM((slot_rows, part), BF),
            pltpu.VMEM((latents, width), BF),
            pltpu.VMEM((latents, width), BF),
            pltpu.VMEM((slot_rows, part), BF),
            pltpu.VMEM((slot_rows, part), BF),
            pltpu.VMEM((CUTS * latents, slot_rows), F32),
            pltpu.SemaphoreType.DMA((per_cut * (CUTS + 1) + 3,)),
            pltpu.VMEM(half_shape, F32),
            pltpu.VMEM(half_shape, kind),
            pltpu.SemaphoreType.DMA((4,)),
        ]

    def swap(values):
        return lax.ppermute(values, "tok", [(i, i ^ 1) for i in range(groups)])

    operands = (enc_weight, dec_weight, bias_row, offset_row)
    part_call = pl.pallas_call(
        functools.partial(chunk_kernel, False),
        out_shape=[jax.ShapeDtypeStruct(half_shape, F32)] * 2,
        in_specs=[smem()] + [hbm()] * 3 + [vmem()] * 2,
        out_specs=[hbm()] * 2,
        scratch_shapes=work(F32),
        compiler_params=room(56),
        cost_estimate=matmul_cost,
        name="chunk_gradients",
    )
    mine1, other1 = part_call(scalars, got1, *operands)
    prior = mine1 + swap(other1)
    mine, other, flags = pl.pallas_call(
        functools.partial(chunk_kernel, True),
        out_shape=[
            jax.ShapeDtypeStruct(half_shape, F32),
            jax.ShapeDtypeStruct(half_shape, BF),
            jax.ShapeDtypeStruct((1,), F32),
        ],
        in_specs=[smem(), vmem()] + [hbm()] * 2 + [vmem()] * 2 + [hbm()],
        out_specs=[anywhere()] * 2 + [smem()],
        scratch_shapes=[
            *work(BF),
            pltpu.VMEM(half_shape, F32),
        ],
        input_output_aliases={6: 0},
        compiler_params=room(46),
        cost_estimate=matmul_cost,
        name="last_gradients",
    )(scalars, got2, *operands, prior)

    def rest(carry):
        mine, other, unused = carry
        codes, cut = slot_codes(targets, DIRECT)
        hit = flat(codes == left[:1])
        data = jnp.zeros((slot_rows, part), F32)
        for h in range(CUTS):
            chosen = jnp.where(cut == h, hit, 0.0).astype(BF)
            data = data + mm(chosen, tokens[:, h * part : (h + 1) * part])
        filled = jnp.sum(hit, axis=1, keepdims=True) > 0.5
        chunk3 = jnp.where(filled, data, EMPTY).astype(BF)
        more, more_other = part_call(scalars, exchange(chunk3), *operands)
        return mine + more, (other.astype(F32) + more_other).astype(BF), jnp.zeros((), F32)

    mine, other, unused = lax.while_loop(
        lambda carry: carry[2] > 0.5, rest, (mine, other, flags.reshape(()))
    )
    summed = (mine + swap(other).astype(F32)).astype(BF)
    terms = lax.all_to_all(
        summed,
        "tok",
        split_axis=0,
        concat_axis=0,
        tiled=True,
        axis_index_groups=[[2 * i + c for i in range(chips)] for c in range(2)],
    )
    terms = terms.reshape(chips // 2, 2, 2, latents, STEP)

    def summed_over_pairs(grad):
        total = terms[0, :, grad].astype(F32)
        for p in range(1, chips // 2):
            total = total + terms[p, :, grad].astype(F32)
        return total.reshape(2 * latents, STEP)

    return summed_over_pairs(0), summed_over_pairs(1)


def solution(mesh):
    in_specs = (
        P(("tok", "lat"), None),
        P(),
        P("lat", None),
        P("lat"),
        P("lat", None),
        P(("tok", "lat"), None),
        P(),
    )
    out_specs = (P("lat", "tok"), P("lat", "tok"))
    return jax.shard_map(
        on_device, mesh=mesh, in_specs=in_specs, out_specs=out_specs, check_vma=False
    )
```
